32 devices in a mesh: parts: 2 (over y), section: 4 (over x, core), tensor: 4 (over z).
Axes of the slice: x: 2, y: 2, z: 4, core: 2. Of those that a mesh axis runs over, the one named last changes fastest.
Arguments:
- prompt: bfloat16 [8, 256, 5120], P(('parts', 'section'), None, 'tensor'), parts along dimension 0, may hold values from -6 to 6
- key_value_weight: bfloat16 [5120, 2048], P('tensor'), may hold values from -0.078125 to 0.078125
- key_gain: float32 [128], replicated, may hold values from 0.1 to 1.9
- prompt_blocks: int32 [12], P('parts'), parts along dimension 0, may hold values from 1 to 8, 16 in all
- block_owner: int32 [32], P('parts'), parts along dimension 0, may hold values from 0 to 3, as said below
- block_slot: int32 [32], P('parts'), parts along dimension 0, may hold values from 0 to 3
- queries: bfloat16 [32, 8192], P(('parts', 'section')), parts along dimension 0, may hold values from -15 to 15
- cache_keys: bfloat16 [32, 512, 1024], P(('parts', 'section'), 'tensor'), parts along dimension 0, may hold values from -6 to 6
- cache_values: bfloat16 [32, 512, 1024], P(('parts', 'section'), 'tensor'), parts along dimension 0, may hold values from -6 to 6
- new_keys: bfloat16 [32, 1024], P(('parts', 'section')), parts along dimension 0, may hold values from -12 to 12
- new_values: bfloat16 [32, 1024], P(('parts', 'section')), parts along dimension 0, may hold values from -6 to 6
- decode_lengths: int32 [32], P(('parts', 'section')), parts along dimension 0, may hold values from 64 to 512, as said below
Outputs:
- attended: bfloat16 [32, 8192], P(('parts', 'section'), 'tensor'), parts along dimension 0
- block_pool: bfloat16 [8, 4, 16, 2048], P(('parts', 'section')), parts along dimension 0
The draws below stay inside these ranges and needn't reach their ends.
There are 2 independent parts, one for each index of `parts`. The reference program is written for one: setup_inputs(seed, part) draws one part's arguments, and reference() takes and returns one part's arrays. A program takes and returns all parts, laid end to end along the dimension named above; an argument that names none is the same for every part. Nothing has to cross between parts.
Inputs may be any that keep to these rules, and one draw needn't show every extreme that they name: Prompt j takes prompt_blocks[j] whole blocks of 16 tokens; together they fill all 16 blocks; the longest takes exactly 8. `block_owner`: no two blocks share an owner and a slot; in every draw some group receives exactly 4 blocks. `decode_lengths`: in every group some row has all 512 positions live.
All inputs are finite; a program needn't handle non-finite values.
Results may differ from the reference program's by a relative error of at most 0.0015.
Values may be sent and summed in bfloat16 or wider, within the bound.
No kernel may reach another device: no remote copies, remote signals or barrier semaphores. Data moves between devices by JAX's collectives and lax.ppermute only.
A program may use at most 64 MiB of HBM per device.

```python
import math
import jax
import jax.numpy as jnp
import numpy as np
from jax import lax

D = 5120
H = 64
KVH = 8
HD = 128
P_SIZE = 256
BLK = 16
ROWS = 4
GROUPS = 4
NR = 16
L = 512
SPAN = 128
KVW = 1024
G = 8
NB = 16
CAP = 4
NPROMPT = 6
MOSTB = 8


def block_table(key):
    key = jax.random.fold_in(key, 202)
    heavy_key, order_key, rest_key, slot_key = jax.random.split(key, 4)
    heavy_group = jax.random.randint(heavy_key, (), 0, GROUPS)
    block_order = jax.random.permutation(order_key, NB)
    block_rank = jnp.argsort(block_order, stable=True).astype(jnp.int32)
    others = jax.random.permutation(rest_key, (GROUPS - 1) * CAP)
    heavy_slots = jax.random.permutation(slot_key, CAP)
    later_slot = others[jnp.clip(block_rank - CAP, 0, (GROUPS - 1) * CAP - 1)]
    other_group = later_slot // CAP
    owner_ids = jnp.where(block_rank < CAP, heavy_group, other_group + (other_group >= heavy_group).astype(jnp.int32))
    slot_ids = jnp.where(block_rank < CAP, heavy_slots[jnp.clip(block_rank, 0, CAP - 1)], later_slot % CAP)
    return (owner_ids.astype(jnp.int32), slot_ids.astype(jnp.int32))


def draw_block_owner(key, part):
    owner_ids, slot_ids = block_table(key)
    return owner_ids


def draw_block_slot(key, part):
    owner_ids, slot_ids = block_table(key)
    return slot_ids


def draw_decode_lengths(key, part):
    key = jax.random.fold_in(key, 3)
    length_key, full_key = jax.random.split(key)
    lengths = jax.random.randint(length_key, (NR,), L // 8, L + 1)
    full_pick = jax.random.randint(full_key, (GROUPS,), 0, ROWS)
    row_ids = jnp.arange(NR, dtype=jnp.int32)
    chosen = full_pick[row_ids // ROWS]
    return jnp.where(row_ids % ROWS == chosen, L, lengths).astype(jnp.int32)


def draw_queries(key, part):
    key = jax.random.fold_in(key, 1)
    result = 2.5 * jnp.clip(jax.random.normal(key, (NR, KVH, G, HD), jnp.float32), -6.0, 6.0)
    return result.reshape(NR, H * HD).astype(jnp.bfloat16)


def draw_cache_keys(key, part):
    key = jax.random.fold_in(key, 2)
    result = jnp.clip(jax.random.normal(key, (NR, L, KVH, HD), jnp.float32), -6.0, 6.0)
    return result.reshape(NR, L, KVW).astype(jnp.bfloat16)


def block_levels(key, extent, shards, smallest, top_value):
    level, own = 1.0, jax.random.fold_in(key, 6)
    for dim, blocks in shards:
        draws = jnp.exp(jax.random.uniform(jax.random.fold_in(own, dim), (blocks,), jnp.float32, smallest / len(shards), top_value / len(shards)))
        level = level * jnp.repeat(draws, extent[dim] // blocks).reshape([-1 if axis == dim else 1 for axis in range(len(extent))])
    return level


def length_profile(amount, total, bound, lean):
    loads = [(1 << 20) // math.isqrt(rank ** lean) + 1 for rank in range(2, amount + 1)]
    spare, given = total - bound - (amount - 1), [1] * (amount - 1)
    while spare > 0:
        movable = [i for i in range(amount - 1) if given[i] < bound]
        mass, left = sum([loads[i] for i in movable]), spare
        for i in movable:
            extra = min(bound - given[i], max(1, left * loads[i] // mass), spare)
            given[i] = given[i] + extra
            spare = spare - extra
    return np.array([bound] + given)


def uneven_parts(key, number_of, total, most, slope):
    if number_of == 2:
        one = jax.random.randint(key, (), max(1, total - most), min(most, total - 1) + 1)
        return jnp.stack([one, total - one])
    tallies = jnp.asarray(length_profile(number_of, total, most, slope), jnp.int32)
    couples = (number_of - 1) // 2
    giver, taker = tallies[1:1 + 2 * couples:2], tallies[2:2 + 2 * couples:2]
    slack = jnp.minimum(giver - 1, most - taker)
    shifted = jax.random.randint(jax.random.fold_in(key, 1), (couples,), 0, 1 << 20) % (slack + 1)
    tallies = tallies.at[1:1 + 2 * couples:2].set(giver - shifted).at[2:2 + 2 * couples:2].set(taker + shifted)
    return tallies[jax.random.permutation(jax.random.fold_in(key, 2), number_of)]


def noise(stream_key, extent, deviation, reach, pieces=(), kind=jnp.bfloat16):
    drawn = jax.random.normal(stream_key, extent, jnp.float32) * deviation
    if len(pieces) > 0:
        drawn = block_levels(stream_key, extent, pieces, -0.22, 0.18) * drawn
    return jnp.clip(drawn, min=-reach, max=reach).astype(kind)


def setup_inputs(seed: int = 0, part: int = 0) -> dict:
    splits = jax.random.split(jax.random.key(seed), 13)
    part_splits = jax.random.split(jax.random.fold_in(splits[12], part), 13)
    prompt = noise(part_splits[0], (GROUPS, P_SIZE, D), 1.0, 6.0, ((0, 4), (2, 4)))
    key_value_weight = noise(splits[1], (D, 2 * KVW), D ** -0.5, 0.078125, ((0, 4),))
    key_gain = jnp.clip(1.0 + 0.18 * jax.random.normal(splits[2], (HD,), jnp.float32), 0.1, 1.9)
    prompt_blocks = uneven_parts(part_splits[3], NPROMPT, NB, MOSTB, 1).astype(jnp.int32)
    block_owner = draw_block_owner(jax.random.fold_in(jax.random.fold_in(splits[12], part), 71), part)
    block_slot = draw_block_slot(jax.random.fold_in(jax.random.fold_in(splits[12], part), 71), part)
    queries = draw_queries(jax.random.fold_in(jax.random.fold_in(splits[12], part), 71), part)
    cache_keys = draw_cache_keys(jax.random.fold_in(jax.random.fold_in(splits[12], part), 71), part)
    cache_values = noise(part_splits[8], (NR, L, KVW), 1.0, 6.0, ((0, 4), (1, 4)))
    new_keys = noise(part_splits[9], (NR, KVW), 3.0, 12.0, ((0, 4),))
    new_values = noise(part_splits[10], (NR, KVW), 1.0, 6.0, ((0, 4),))
    decode_lengths = draw_decode_lengths(jax.random.fold_in(jax.random.fold_in(splits[12], part), 71), part)
    return dict(prompt=prompt, key_value_weight=key_value_weight, key_gain=key_gain, prompt_blocks=prompt_blocks, block_owner=block_owner, block_slot=block_slot, queries=queries, cache_keys=cache_keys, cache_values=cache_values, new_keys=new_keys, new_values=new_values, decode_lengths=decode_lengths)


NORM_EPSILON = 1e-06
ROPE_BASE = 1000000.0
MASKED_SCORE = -1e+30

def positions_of(prompt_blocks, token_count):
    prompt_ends = jnp.cumsum(prompt_blocks).astype(jnp.int32)
    prompt_starts = (prompt_ends - prompt_blocks).astype(jnp.int32)
    token_ids = jnp.arange(token_count, dtype=jnp.int32)
    block_index = token_ids // BLK
    prompt_index = lax.optimization_barrier(jnp.sum((block_index[:, None] >= prompt_ends[None, :]).astype(jnp.int32), axis=1)).astype(jnp.int32)
    chosen = prompt_index[:, None] == jnp.arange(prompt_ends.shape[0], dtype=jnp.int32)[None, :]
    first_block = lax.optimization_barrier(jnp.sum(jnp.where(chosen, prompt_starts[None, :], 0), axis=1)).astype(jnp.int32)
    return (token_ids - first_block * BLK).astype(jnp.int32)

def finish_keys(projected, positions, key_gain):
    token_count = projected.shape[0]
    key_heads = projected[:, :KVW].reshape(token_count, KVH, HD)
    inv_root = lax.rsqrt(lax.optimization_barrier(jnp.mean(key_heads * key_heads, axis=-1, keepdims=True)) + NORM_EPSILON)
    key_heads = key_heads * inv_root * key_gain
    half_dim = HD // 2
    frequency = ROPE_BASE ** (jnp.arange(half_dim, dtype=jnp.float32) * (-2.0 / HD))
    angles = positions.astype(jnp.float32)[:, None, None] * frequency[None, None, :]
    cosine = jnp.cos(angles)
    sine_part = jnp.sin(angles)
    lower_half = key_heads[..., :half_dim]
    upper_half = key_heads[..., half_dim:]
    rotated = jnp.concatenate([lower_half * cosine - upper_half * sine_part, upper_half * cosine + lower_half * sine_part], axis=-1)
    return jnp.concatenate([rotated.reshape(token_count, KVW), projected[:, KVW:]], axis=1).astype(jnp.bfloat16)

def fill_pool(prompt_kv, block_owner, block_slot):
    blocks = prompt_kv.reshape(NB, BLK * 2 * KVW)
    group_ids = jnp.arange(GROUPS, dtype=jnp.int32)
    slot_ids = jnp.arange(CAP, dtype=jnp.int32)
    selector = (block_owner[None, None, :] == group_ids[:, None, None]) & (block_slot[None, None, :] == slot_ids[None, :, None])
    filled = jnp.dot(selector.reshape(GROUPS * CAP, NB).astype(jnp.bfloat16), blocks, preferred_element_type=jnp.float32)
    return filled.reshape(GROUPS, CAP, BLK, 2 * KVW).astype(jnp.bfloat16)

def attend_row(inputs):
    query_row, key_rows, value_rows, new_key, new_value, length = inputs
    query_heads = query_row.astype(jnp.float32).reshape(KVH, G, HD)
    key_heads = key_rows.astype(jnp.float32).reshape(L, KVH, HD)
    value_heads = value_rows.astype(jnp.float32).reshape(L // SPAN, SPAN, KVH, HD)
    scores = jnp.einsum('kgd,pkd->kgp', query_heads, key_heads, precision=lax.Precision.HIGHEST) * HD ** (-0.5)
    live_mask = jnp.arange(L, dtype=jnp.int32) < length
    scores = jnp.where(live_mask[None, None, :], scores, MASKED_SCORE)
    spans = scores.reshape(KVH, G, L // SPAN, SPAN)
    span_max = lax.optimization_barrier(jnp.max(spans, axis=-1))
    live_spans = live_mask.reshape(L // SPAN, SPAN)
    weights = jnp.where(live_spans[None, None], jnp.exp(spans - span_max[..., None]), 0.0)
    span_sum = lax.optimization_barrier(jnp.sum(weights, axis=-1))
    rounded = lax.optimization_barrier(weights.astype(jnp.bfloat16)).astype(jnp.float32)
    span_out = jnp.einsum('kgns,nskd->kgnd', rounded, value_heads, precision=lax.Precision.HIGHEST)
    self_score = jnp.einsum('kgd,kd->kg', query_heads, new_key.astype(jnp.float32).reshape(KVH, HD), precision=lax.Precision.HIGHEST) * HD ** (-0.5)
    row_peak = jnp.maximum(lax.optimization_barrier(jnp.max(span_max, axis=-1)), self_score)
    factor = jnp.exp(span_max - row_peak[..., None])
    self_weight = jnp.exp(self_score - row_peak)
    numerator = lax.optimization_barrier(jnp.sum(span_out * factor[..., None], axis=2)) + self_weight[..., None] * new_value.astype(jnp.float32).reshape(KVH, 1, HD)
    denominator = lax.optimization_barrier(jnp.sum(span_sum * factor, axis=2)) + self_weight
    return (numerator / denominator[..., None]).reshape(H * HD).astype(jnp.bfloat16)

def reference(prompt, key_value_weight, key_gain, prompt_blocks, block_owner, block_slot, queries, cache_keys, cache_values, new_keys, new_values, decode_lengths):
    kv_raw = jnp.dot(prompt[0], key_value_weight, preferred_element_type=jnp.float32)
    positions = positions_of(prompt_blocks, P_SIZE)
    prompt_kv = finish_keys(kv_raw, positions, key_gain)
    block_pool = fill_pool(prompt_kv, block_owner, block_slot)
    attended = lax.map(attend_row, (queries, cache_keys, cache_values, new_keys, new_values, decode_lengths))
    return (attended, block_pool)
```

```python
import jax
import jax.numpy as jnp
from jax import lax
from jax.sharding import PartitionSpec as P

H = 64
KVH = 8
HD = 128
BLK = 16
SPAN = 128
KVW = 1024
G = 8
NB = 16
CAP = 4


NORM_EPSILON = 1e-06
ROPE_BASE = 1000000.0
MASKED_SCORE = -1e30


def exchange(pieces, axis):
    count = lax.axis_size(axis)
    rank = lax.axis_index(axis)
    landed = [lax.dynamic_index_in_dim(pieces, rank, 0, keepdims=False)]
    for step in range(1, count):
        piece = lax.dynamic_index_in_dim(pieces, rank ^ step, 0, keepdims=False)
        landed.append(lax.ppermute(piece, axis, [(i, i ^ step) for i in range(count)]))
    return landed


def collected(own, axis):
    count = lax.axis_size(axis)
    rank = lax.axis_index(axis)
    landed = [own]
    for step in range(1, count):
        landed.append(lax.ppermute(own, axis, [(i, i ^ step) for i in range(count)]))
    stacked = jnp.zeros((count,) + own.shape, own.dtype)
    for step, piece in enumerate(landed):
        stacked = lax.dynamic_update_index_in_dim(stacked, piece, rank ^ step, 0)
    return stacked


def rows_for_groups(states, block_owner, block_slot, group_count):
    slot_ids = jnp.arange(group_count * CAP, dtype=jnp.int32)
    selector = (block_owner * CAP + block_slot)[None, :] == slot_ids[:, None]
    filled = jnp.any(selector, axis=1)
    source = jnp.argmax(selector, axis=1)
    blocks = states.reshape(NB, BLK, states.shape[1])
    chosen = jnp.where(filled[:, None, None], blocks[source], jnp.zeros((), states.dtype))
    return chosen.reshape(group_count, CAP * BLK, states.shape[1])


def spread(rows, axis):
    count = lax.axis_size(axis)
    landed = jnp.where(lax.axis_index(axis) == 0, rows[0], jnp.zeros_like(rows[0]))
    for k in range(1, count):
        landed = landed + lax.ppermute(rows[k], axis, [(0, k)])
    return landed


def slot_positions(prompt_blocks, block_owner, block_slot, group_index):
    prompt_ends = jnp.cumsum(prompt_blocks)
    prompt_starts = prompt_ends - prompt_blocks
    slot_ids = jnp.arange(CAP, dtype=jnp.int32)
    selector = (block_owner[None, :] == group_index) & (block_slot[None, :] == slot_ids[:, None])
    block = jnp.sum(jnp.where(selector, jnp.arange(NB, dtype=jnp.int32)[None, :], 0), axis=1)
    inside = (block[:, None] >= prompt_starts[None, :]) & (block[:, None] < prompt_ends[None, :])
    first = jnp.sum(jnp.where(inside, prompt_starts[None, :], 0), axis=1)
    return (((block - first) * BLK)[:, None] + jnp.arange(BLK, dtype=jnp.int32)[None, :]).reshape(-1)


def finish_keys(projected, positions, key_gain):
    token_count = projected.shape[0]
    key_heads = projected[:, :KVW].reshape(token_count, KVH, HD)
    inv_root = lax.rsqrt(jnp.mean(key_heads * key_heads, axis=-1, keepdims=True) + NORM_EPSILON)
    key_heads = key_heads * inv_root * key_gain
    half_dim = HD // 2
    frequency = ROPE_BASE ** (jnp.arange(half_dim, dtype=jnp.float32) * (-2.0 / HD))
    angles = positions.astype(jnp.float32)[:, None, None] * frequency[None, None, :]
    cosine = jnp.cos(angles)
    sine_part = jnp.sin(angles)
    lower_half = key_heads[..., :half_dim]
    upper_half = key_heads[..., half_dim:]
    rotated = jnp.concatenate(
        [
            lower_half * cosine - upper_half * sine_part,
            upper_half * cosine + lower_half * sine_part,
        ],
        axis=-1,
    )
    return jnp.concatenate([rotated.reshape(token_count, KVW), projected[:, KVW:]], axis=1).astype(
        jnp.bfloat16
    )


def partial_attention(queries, cache_keys, cache_values, decode_lengths, first_position):
    row_count = queries.shape[0]
    local_len = cache_keys.shape[1]
    span_count = local_len // SPAN
    query_heads = queries.reshape(row_count, KVH, G, HD)
    key_heads = cache_keys.reshape(row_count, local_len, KVH, HD)
    scores = jnp.einsum(
        "rkgd,rpkd->rkgp", query_heads, key_heads, preferred_element_type=jnp.float32
    ) * HD ** (-0.5)
    live_mask = (first_position + jnp.arange(local_len, dtype=jnp.int32))[None, :] < decode_lengths[
        :, None
    ]
    scores = jnp.where(live_mask[:, None, None, :], scores, MASKED_SCORE)
    spans = scores.reshape(row_count, KVH, G, span_count, SPAN)
    span_max = jnp.max(spans, axis=-1)
    live_spans = live_mask.reshape(row_count, 1, 1, span_count, SPAN)
    weights = jnp.where(live_spans, jnp.exp(spans - span_max[..., None]), 0.0)
    span_sum = jnp.sum(weights, axis=-1)
    value_spans = cache_values.reshape(row_count, span_count, SPAN, KVH, HD)
    span_out = jnp.einsum(
        "rkgns,rnskd->rkgnd",
        weights.astype(jnp.bfloat16),
        value_spans,
        preferred_element_type=jnp.float32,
    )
    row_peak = jnp.max(span_max, axis=-1)
    factor = jnp.exp(span_max - row_peak[..., None])
    partial_out = jnp.sum(span_out * factor[..., None], axis=3)
    partial_sum = jnp.sum(span_sum * factor, axis=-1)
    return (
        partial_out.reshape(row_count, H, HD),
        row_peak.reshape(row_count, H),
        partial_sum.reshape(row_count, H),
    )


def combine_partials(former, latter):
    former_out, former_peak, former_sum = former
    latter_out, latter_peak, latter_sum = latter
    highest = jnp.maximum(former_peak, latter_peak)
    former_factor = jnp.exp(former_peak - highest)
    latter_factor = jnp.exp(latter_peak - highest)
    merged_out = former_out * former_factor[..., None] + latter_out * latter_factor[..., None]
    return (merged_out, highest, former_sum * former_factor + latter_sum * latter_factor)


def finish_heads(
    own_out, own_peak, own_sum, queries, new_keys, new_values, tensor_rank, heads_here
):
    row_count = queries.shape[0]
    own_width = heads_here * HD
    own_queries = (
        lax.dynamic_slice_in_dim(queries, tensor_rank * own_width, own_width, 1)
        .reshape(row_count, heads_here, HD)
        .astype(jnp.float32)
    )
    head_ids = tensor_rank * heads_here + jnp.arange(heads_here, dtype=jnp.int32)
    selector = (head_ids[:, None] // G == jnp.arange(KVH, dtype=jnp.int32)[None, :]).astype(
        jnp.float32
    )
    own_keys = jnp.einsum(
        "jk,rkd->rjd",
        selector,
        new_keys.reshape(row_count, KVH, HD).astype(jnp.float32),
        precision=lax.Precision.HIGHEST,
    )
    own_values = jnp.einsum(
        "jk,rkd->rjd",
        selector,
        new_values.reshape(row_count, KVH, HD).astype(jnp.float32),
        precision=lax.Precision.HIGHEST,
    )
    self_score = jnp.sum(own_queries * own_keys, axis=-1) * HD ** (-0.5)
    row_peak = jnp.maximum(own_peak, self_score)
    factor = jnp.exp(own_peak - row_peak)
    self_weight = jnp.exp(self_score - row_peak)
    numerator = own_out * factor[..., None] + self_weight[..., None] * own_values
    denominator = own_sum * factor + self_weight
    return (numerator / denominator[..., None]).reshape(row_count, own_width).astype(jnp.bfloat16)


def local(
    prompt,
    key_value_weight,
    key_gain,
    prompt_blocks,
    block_owner,
    block_slot,
    queries,
    cache_keys,
    cache_values,
    new_keys,
    new_values,
    decode_lengths,
):
    tensor_count = lax.axis_size("tensor")
    tensor_rank = lax.axis_index("tensor")
    group_index = lax.axis_index("section")
    group_count = lax.axis_size("section")
    slot_rows = CAP * BLK
    rows_here = slot_rows // tensor_count
    rows = rows_for_groups(prompt[0], block_owner, block_slot, group_count)
    own_rows = spread(rows, "section")
    local_len = cache_keys.shape[1]
    row_count = queries.shape[0]
    heads_here = H // tensor_count
    partial_out, partial_peak, partial_sum = partial_attention(
        queries, cache_keys, cache_values, decode_lengths, tensor_rank * local_len
    )
    stats = jnp.stack([partial_peak, partial_sum], axis=-1).reshape(row_count, tensor_count, heads_here, 2)
    outs = partial_out.reshape(row_count, tensor_count, heads_here, HD)
    packed = jnp.concatenate([outs, jnp.pad(stats, ((0, 0), (0, 0), (0, 0), (0, HD - 2)))], axis=-1)
    shares = exchange(packed.transpose(1, 0, 2, 3), "tensor")
    merged = (shares[0][..., :HD], shares[0][..., HD], shares[0][..., HD + 1])
    for share in shares[1:]:
        merged = combine_partials(merged, (share[..., :HD], share[..., HD], share[..., HD + 1]))
    own_out, own_peak, own_sum = merged
    partial_terms = jnp.dot(own_rows, key_value_weight, preferred_element_type=jnp.float32)
    terms = exchange(partial_terms.reshape(tensor_count, rows_here, -1), "tensor")
    summed = sum(terms[1:], terms[0])
    positions = lax.dynamic_slice_in_dim(
        slot_positions(prompt_blocks, block_owner, block_slot, group_index), tensor_rank * rows_here, rows_here, 0
    )
    prompt_kv = finish_keys(summed, positions, key_gain)
    block_pool = collected(prompt_kv, "tensor").reshape(1, CAP, BLK, -1)
    attended = finish_heads(
        own_out, own_peak, own_sum, queries, new_keys, new_values, tensor_rank, heads_here
    )
    return (attended, block_pool)


def solution(mesh):
    in_specs = (
        P(("parts", "section"), None, "tensor"),
        P("tensor", None),
        P(),
        P("parts"),
        P("parts"),
        P("parts"),
        P(("parts", "section"), None),
        P(("parts", "section"), "tensor", None),
        P(("parts", "section"), "tensor", None),
        P(("parts", "section"), None),
        P(("parts", "section"), None),
        P(("parts", "section")),
    )
    out_specs = (P(("parts", "section"), "tensor"), P(("parts", "section"), None, None, None))
    return jax.shard_map(local, mesh=mesh, in_specs=in_specs, out_specs=out_specs, check_vma=False)
```

```python
import jax
import jax.numpy as jnp
from jax import lax
from jax.experimental import pallas as pl
from jax.experimental.pallas import tpu as pltpu
from jax.sharding import PartitionSpec as P

H = 64
KVH = 8
HD = 128
BLK = 16
SPAN = 128
KVW = 1024
G = 8
NB = 16
CAP = 4


NORM_EPSILON = 1e-06
ROPE_BASE = 1000000.0
MASKED_SCORE = -1e30


def exchange(pieces, axis):
    count = lax.axis_size(axis)
    rank = lax.axis_index(axis)
    landed = [lax.dynamic_index_in_dim(pieces, rank, 0, keepdims=False)]
    for step in range(1, count):
        piece = lax.dynamic_index_in_dim(pieces, rank ^ step, 0, keepdims=False)
        landed.append(lax.ppermute(piece, axis, [(i, i ^ step) for i in range(count)]))
    return landed


def collected(own, axis):
    count = lax.axis_size(axis)
    rank = lax.axis_index(axis)
    landed = [own]
    for step in range(1, count):
        landed.append(lax.ppermute(own, axis, [(i, i ^ step) for i in range(count)]))
    stacked = jnp.zeros((count,) + own.shape, own.dtype)
    for step, piece in enumerate(landed):
        stacked = lax.dynamic_update_index_in_dim(stacked, piece, rank ^ step, 0)
    return stacked


def rows_for_groups(states, block_owner, block_slot, group_count):
    slot_ids = jnp.arange(group_count * CAP, dtype=jnp.int32)
    selector = (block_owner * CAP + block_slot)[None, :] == slot_ids[:, None]
    filled = jnp.any(selector, axis=1)
    source = jnp.argmax(selector, axis=1)
    blocks = states.reshape(NB, BLK, states.shape[1])
    chosen = jnp.where(filled[:, None, None], blocks[source], jnp.zeros((), states.dtype))
    return chosen.reshape(group_count, CAP * BLK, states.shape[1])


def spread(rows, axis):
    count = lax.axis_size(axis)
    landed = jnp.where(lax.axis_index(axis) == 0, rows[0], jnp.zeros_like(rows[0]))
    for k in range(1, count):
        landed = landed + lax.ppermute(rows[k], axis, [(0, k)])
    return landed


def slot_positions(prompt_blocks, block_owner, block_slot, group_index):
    prompt_ends = jnp.cumsum(prompt_blocks)
    prompt_starts = prompt_ends - prompt_blocks
    slot_ids = jnp.arange(CAP, dtype=jnp.int32)
    selector = (block_owner[None, :] == group_index) & (block_slot[None, :] == slot_ids[:, None])
    block = jnp.sum(jnp.where(selector, jnp.arange(NB, dtype=jnp.int32)[None, :], 0), axis=1)
    inside = (block[:, None] >= prompt_starts[None, :]) & (block[:, None] < prompt_ends[None, :])
    first = jnp.sum(jnp.where(inside, prompt_starts[None, :], 0), axis=1)
    return (((block - first) * BLK)[:, None] + jnp.arange(BLK, dtype=jnp.int32)[None, :]).reshape(-1)


def finish_keys(projected, positions, key_gain):
    token_count = projected.shape[0]
    key_heads = projected[:, :KVW].reshape(token_count, KVH, HD)
    inv_root = lax.rsqrt(jnp.mean(key_heads * key_heads, axis=-1, keepdims=True) + NORM_EPSILON)
    key_heads = key_heads * inv_root * key_gain
    half_dim = HD // 2
    frequency = ROPE_BASE ** (jnp.arange(half_dim, dtype=jnp.float32) * (-2.0 / HD))
    angles = positions.astype(jnp.float32)[:, None, None] * frequency[None, None, :]
    cosine = jnp.cos(angles)
    sine_part = jnp.sin(angles)
    lower_half = key_heads[..., :half_dim]
    upper_half = key_heads[..., half_dim:]
    rotated = jnp.concatenate(
        [
            lower_half * cosine - upper_half * sine_part,
            upper_half * cosine + lower_half * sine_part,
        ],
        axis=-1,
    )
    return jnp.concatenate([rotated.reshape(token_count, KVW), projected[:, KVW:]], axis=1).astype(
        jnp.bfloat16
    )


def partial_attention(queries, cache_keys, cache_values, decode_lengths, first_position):
    row_count = queries.shape[0]
    local_len = cache_keys.shape[1]
    span_count = local_len // SPAN
    query_heads = queries.reshape(row_count, KVH, G, HD)
    key_heads = cache_keys.reshape(row_count, local_len, KVH, HD)
    scores = jnp.einsum(
        "rkgd,rpkd->rkgp", query_heads, key_heads, preferred_element_type=jnp.float32
    ) * HD ** (-0.5)
    live_mask = (first_position + jnp.arange(local_len, dtype=jnp.int32))[None, :] < decode_lengths[
        :, None
    ]
    scores = jnp.where(live_mask[:, None, None, :], scores, MASKED_SCORE)
    spans = scores.reshape(row_count, KVH, G, span_count, SPAN)
    span_max = jnp.max(spans, axis=-1)
    live_spans = live_mask.reshape(row_count, 1, 1, span_count, SPAN)
    weights = jnp.where(live_spans, jnp.exp(spans - span_max[..., None]), 0.0)
    span_sum = jnp.sum(weights, axis=-1)
    value_spans = cache_values.reshape(row_count, span_count, SPAN, KVH, HD)
    span_out = jnp.einsum(
        "rkgns,rnskd->rkgnd",
        weights.astype(jnp.bfloat16),
        value_spans,
        preferred_element_type=jnp.float32,
    )
    row_peak = jnp.max(span_max, axis=-1)
    factor = jnp.exp(span_max - row_peak[..., None])
    partial_out = jnp.sum(span_out * factor[..., None], axis=3)
    partial_sum = jnp.sum(span_sum * factor, axis=-1)
    return (
        partial_out.reshape(row_count, H, HD),
        row_peak.reshape(row_count, H),
        partial_sum.reshape(row_count, H),
    )


def combine_partials(former, latter):
    former_out, former_peak, former_sum = former
    latter_out, latter_peak, latter_sum = latter
    highest = jnp.maximum(former_peak, latter_peak)
    former_factor = jnp.exp(former_peak - highest)
    latter_factor = jnp.exp(latter_peak - highest)
    merged_out = former_out * former_factor[..., None] + latter_out * latter_factor[..., None]
    return (merged_out, highest, former_sum * former_factor + latter_sum * latter_factor)


def finish_heads(
    own_out, own_peak, own_sum, queries, new_keys, new_values, tensor_rank, heads_here
):
    row_count = queries.shape[0]
    own_width = heads_here * HD
    own_queries = (
        lax.dynamic_slice_in_dim(queries, tensor_rank * own_width, own_width, 1)
        .reshape(row_count, heads_here, HD)
        .astype(jnp.float32)
    )
    head_ids = tensor_rank * heads_here + jnp.arange(heads_here, dtype=jnp.int32)
    selector = (head_ids[:, None] // G == jnp.arange(KVH, dtype=jnp.int32)[None, :]).astype(
        jnp.float32
    )
    own_keys = jnp.einsum(
        "jk,rkd->rjd",
        selector,
        new_keys.reshape(row_count, KVH, HD).astype(jnp.float32),
        precision=lax.Precision.HIGHEST,
    )
    own_values = jnp.einsum(
        "jk,rkd->rjd",
        selector,
        new_values.reshape(row_count, KVH, HD).astype(jnp.float32),
        precision=lax.Precision.HIGHEST,
    )
    self_score = jnp.sum(own_queries * own_keys, axis=-1) * HD ** (-0.5)
    row_peak = jnp.maximum(own_peak, self_score)
    factor = jnp.exp(own_peak - row_peak)
    self_weight = jnp.exp(self_score - row_peak)
    numerator = own_out * factor[..., None] + self_weight[..., None] * own_values
    denominator = own_sum * factor + self_weight
    return (numerator / denominator[..., None]).reshape(row_count, own_width).astype(jnp.bfloat16)


def local_small_shares(
    prompt,
    key_value_weight,
    key_gain,
    prompt_blocks,
    block_owner,
    block_slot,
    queries,
    cache_keys,
    cache_values,
    new_keys,
    new_values,
    decode_lengths,
):
    tensor_count = lax.axis_size("tensor")
    tensor_rank = lax.axis_index("tensor")
    group_index = lax.axis_index("section")
    group_count = lax.axis_size("section")
    slot_rows = CAP * BLK
    rows_here = slot_rows // tensor_count
    rows = rows_for_groups(prompt[0], block_owner, block_slot, group_count)
    own_rows = spread(rows, "section")
    local_len = cache_keys.shape[1]
    row_count = queries.shape[0]
    heads_here = H // tensor_count
    partial_out, partial_peak, partial_sum = partial_attention(
        queries, cache_keys, cache_values, decode_lengths, tensor_rank * local_len
    )
    stats = jnp.stack([partial_peak, partial_sum], axis=-1).reshape(row_count, tensor_count, heads_here, 2)
    outs = partial_out.reshape(row_count, tensor_count, heads_here, HD)
    packed = jnp.concatenate([outs, jnp.pad(stats, ((0, 0), (0, 0), (0, 0), (0, HD - 2)))], axis=-1)
    shares = exchange(packed.transpose(1, 0, 2, 3), "tensor")
    merged = (shares[0][..., :HD], shares[0][..., HD], shares[0][..., HD + 1])
    for share in shares[1:]:
        merged = combine_partials(merged, (share[..., :HD], share[..., HD], share[..., HD + 1]))
    own_out, own_peak, own_sum = merged
    partial_terms = jnp.dot(own_rows, key_value_weight, preferred_element_type=jnp.float32)
    terms = exchange(partial_terms.reshape(tensor_count, rows_here, -1), "tensor")
    summed = sum(terms[1:], terms[0])
    positions = lax.dynamic_slice_in_dim(
        slot_positions(prompt_blocks, block_owner, block_slot, group_index), tensor_rank * rows_here, rows_here, 0
    )
    prompt_kv = finish_keys(summed, positions, key_gain)
    block_pool = collected(prompt_kv, "tensor").reshape(1, CAP, BLK, -1)
    attended = finish_heads(
        own_out, own_peak, own_sum, queries, new_keys, new_values, tensor_rank, heads_here
    )
    return (attended, block_pool)


VMEM = pl.BlockSpec(memory_space=pltpu.VMEM)
SMEM = pl.BlockSpec(memory_space=pltpu.SMEM)
ANY = pl.BlockSpec(memory_space=pl.ANY)
F32 = jnp.float32
BF16 = jnp.bfloat16


def on_chip(kernel, operands, in_specs, out_shapes, scratch=(), flops=0, moved=0):
    return pl.pallas_call(
        kernel,
        out_shape=out_shapes,
        in_specs=in_specs,
        out_specs=[VMEM] * len(out_shapes),
        scratch_shapes=list(scratch),
        compiler_params=pltpu.CompilerParams(vmem_limit_bytes=40 * 1024 * 1024),
        cost_estimate=pl.CostEstimate(flops=flops, bytes_accessed=moved, transcendentals=0),
    )(*operands)


def place_rows(states, block_owner, block_slot, group_count):
    width = states.shape[1]
    slot_count = group_count * CAP

    def kernel(owner_ref, slot_ref, states_ref, *refs):
        row_refs, source_ref, sems = refs[:group_count], refs[group_count], refs[group_count + 1]
        for j in range(slot_count):
            source_ref[j] = -1
        for b in range(NB):
            source_ref[owner_ref[b] * CAP + slot_ref[b]] = b

        def copy_of(j, b):
            start = pl.multiple_of(b * BLK, BLK)
            target = row_refs[j // CAP].at[pl.ds((j % CAP) * BLK, BLK)]
            return pltpu.make_async_copy(states_ref.at[pl.ds(start, BLK)], target, sems.at[j])

        for j in range(slot_count):
            b = source_ref[j]

            @pl.when(b >= 0)
            def _():
                copy_of(j, b).start()

            @pl.when(b < 0)
            def _():
                row_refs[j // CAP][pl.ds((j % CAP) * BLK, BLK), :] = jnp.zeros((BLK, width), BF16)

        for j in range(slot_count):
            b = source_ref[j]

            @pl.when(b >= 0)
            def _():
                copy_of(j, b).wait()

    return on_chip(
        kernel,
        (block_owner, block_slot, states),
        [SMEM, SMEM, ANY],
        [jax.ShapeDtypeStruct((CAP * BLK, width), BF16)] * group_count,
        [pltpu.SMEM((slot_count,), jnp.int32), pltpu.SemaphoreType.DMA((slot_count,))],
        moved=states.size * 4,
    )


def attend_span(queries, cache_keys, cache_values, decode_lengths, tensor_count):
    row_count, local_len = cache_keys.shape[0], cache_keys.shape[1]
    heads_here = H // tensor_count
    out_rows = row_count * heads_here

    def kernel(length_ref, query_ref, key_ref, value_ref, *refs):
        share_refs, held = refs[:tensor_count], refs[tensor_count]
        rank = lax.axis_index("tensor")
        first = rank * local_len
        place = lax.broadcasted_iota(jnp.int32, (1, local_len), 1) + first
        lane = lax.broadcasted_iota(jnp.int32, (G, HD), 1)
        stats = jnp.zeros((G, HD), F32)
        for r in range(row_count):
            live = place < length_ref[r]
            for pair in range(KVH // 2):
                pair_queries = query_ref[r, pl.ds(pair * 2 * G, 2 * G), :]
                weights = []
                for half in range(2):
                    n = pair * 2 + half
                    scores = lax.dot_general(
                        pair_queries,
                        key_ref[r, :, n * HD : (n + 1) * HD],
                        (((1,), (1,)), ((), ())),
                        preferred_element_type=F32,
                    )[half * G : (half + 1) * G] * HD ** (-0.5)
                    scores = jnp.where(live, scores, MASKED_SCORE)
                    peak = jnp.max(scores, axis=1, keepdims=True)
                    weight = jnp.where(live, jnp.exp(scores - peak), 0.0)
                    total = jnp.sum(weight, axis=1, keepdims=True)
                    stats = jnp.where(lane == 2 * KVH * r + n, peak, stats)
                    stats = jnp.where(lane == 2 * KVH * r + KVH + n, total, stats)
                    weights.append(weight)
                rounded = jnp.concatenate(weights, axis=0).astype(BF16)
                for half in range(2):
                    n = pair * 2 + half
                    out = jnp.dot(rounded, value_ref[r, :, n * HD : (n + 1) * HD], preferred_element_type=F32)
                    held[r, pl.ds(n * G, G), :] = out[half * G : (half + 1) * G]
        for step in range(tensor_count):
            start = pl.multiple_of((rank ^ step) * heads_here, heads_here)
            for r in range(row_count):
                share_refs[step][pl.ds(r * heads_here, heads_here), :] = held[r, pl.ds(start, heads_here), :]
            share_refs[step][pl.ds(out_rows, G), :] = stats

    return on_chip(
        kernel,
        (decode_lengths, queries.reshape(row_count, H, HD), cache_keys, cache_values),
        [SMEM, VMEM, VMEM, VMEM],
        [jax.ShapeDtypeStruct((out_rows + G, HD), F32)] * tensor_count,
        [pltpu.VMEM((row_count, H, HD), F32)],
        flops=4 * row_count * H * HD * local_len,
        moved=4 * cache_keys.size,
    )


def merge_spans(shares, queries, new_keys, new_values, heads_here):
    row_count = queries.shape[0]
    share_count = len(shares)
    keys_here = heads_here // G
    out_rows = row_count * heads_here

    def kernel(*refs):
        share_refs = refs[:share_count]
        query_ref, key_ref, value_ref, out_ref = refs[share_count:]
        rank = lax.axis_index("tensor")
        lane = lax.broadcasted_iota(jnp.int32, (G, HD), 1)
        stats = [ref[pl.ds(out_rows, G), :] for ref in share_refs]
        for r in range(row_count):
            for kk in range(keys_here):
                n = rank * keys_here + kk

                def column(tile, index):
                    return jnp.sum(jnp.where(lane == index, tile, 0.0), axis=1, keepdims=True)

                query = query_ref[r, pl.ds(pl.multiple_of(n * G, G), G), :]
                column_start = pl.multiple_of(n * HD, HD)
                new_key = key_ref[pl.ds(r, 1), pl.ds(column_start, HD)]
                new_value = value_ref[pl.ds(r, 1), pl.ds(column_start, HD)]
                self_score = jnp.sum(query * new_key, axis=1, keepdims=True) * HD ** (-0.5)
                peaks = [column(tile, 2 * KVH * r + n) for tile in stats]
                sums = [column(tile, 2 * KVH * r + KVH + n) for tile in stats]
                row_peak = self_score
                for peak in peaks:
                    row_peak = jnp.maximum(row_peak, peak)
                self_weight = jnp.exp(self_score - row_peak)
                numerator = self_weight * new_value
                denominator = self_weight
                for ref, peak, total in zip(share_refs, peaks, sums):
                    factor = jnp.exp(peak - row_peak)
                    numerator += factor * ref[pl.ds(r * heads_here + kk * G, G), :]
                    denominator += factor * total
                out_ref[r, pl.ds(kk * G, G), :] = numerator / denominator

    attended = on_chip(
        kernel,
        (*shares, queries.reshape(row_count, H, HD).astype(F32), new_keys.astype(F32), new_values.astype(F32)),
        [VMEM] * (share_count + 3),
        [jax.ShapeDtypeStruct((row_count, heads_here, HD), F32)],
    )[0]
    return attended.astype(BF16).reshape(row_count, heads_here * HD)


def project_rows(candidates, weight, tensor_count):
    slot_rows, depth = candidates[0].shape
    width = weight.shape[1]
    rows_here = slot_rows // tensor_count
    count = len(candidates)
    step_width = 512

    def kernel(*refs):
        candidate_refs, weight_ref = refs[:count], refs[count]
        share_refs, rows_ref, held = refs[count + 1 : count + 1 + tensor_count], refs[-2], refs[-1]
        group = lax.axis_index("section")
        rank = lax.axis_index("tensor")
        for k in range(count):

            @pl.when(group == k)
            def _():
                rows_ref[...] = candidate_refs[k][...]

        for c in range(width // step_width):
            columns = pl.ds(c * step_width, step_width)
            held[:, columns] = jnp.dot(rows_ref[...], weight_ref[:, columns], preferred_element_type=F32)
        for step in range(tensor_count):
            start = pl.multiple_of((rank ^ step) * rows_here, rows_here)
            share_refs[step][...] = held[pl.ds(start, rows_here), :]

    return on_chip(
        kernel,
        (*candidates, weight),
        [VMEM] * (count + 1),
        [jax.ShapeDtypeStruct((rows_here, width), F32)] * tensor_count,
        [pltpu.VMEM((slot_rows, depth), BF16), pltpu.VMEM((slot_rows, width), F32)],
        flops=2 * slot_rows * depth * width,
        moved=2 * weight.size,
    )


def finish_rows(shares, cosine, sine, gain):
    share_count = len(shares)
    rows, width = shares[0].shape

    def kernel(*refs):
        share_refs = refs[:share_count]
        cosine_ref, sine_ref, gain_ref, out_ref = refs[share_count:]
        for n in range(width // HD):
            columns = pl.ds(n * HD, HD)
            total = share_refs[0][:, columns]
            for ref in share_refs[1:]:
                total = total + ref[:, columns]
            if n < KVH:
                mean = jnp.sum(total * total, axis=1, keepdims=True) * (1.0 / HD)
                total = total * lax.rsqrt(mean + NORM_EPSILON) * gain_ref[...]
                total = total * cosine_ref[...] + pltpu.roll(total, HD // 2, 1) * sine_ref[...]
            out_ref[:, columns] = total.astype(BF16)

    return on_chip(
        kernel,
        (*shares, cosine, sine, gain),
        [VMEM] * (share_count + 3),
        [jax.ShapeDtypeStruct((rows, width), BF16)],
    )[0]


def join_rows(pieces):
    count = len(pieces)
    rows, width = pieces[0].shape

    def kernel(*refs):
        piece_refs, out_ref = refs[:count], refs[count]
        rank = lax.axis_index("tensor")
        for step in range(count):
            out_ref[pl.ds(pl.multiple_of((rank ^ step) * rows, rows), rows), :] = piece_refs[step][...]

    return on_chip(
        kernel, pieces, [VMEM] * count, [jax.ShapeDtypeStruct((count * rows, width), BF16)]
    )[0]


def rotation_tables(positions):
    frequency = ROPE_BASE ** (jnp.arange(HD // 2, dtype=F32) * (-2.0 / HD))
    angles = positions.astype(F32)[:, None] * frequency[None, :]
    cosine, sine = jnp.cos(angles), jnp.sin(angles)
    return jnp.concatenate([cosine, cosine], axis=1), jnp.concatenate([-sine, sine], axis=1)


def swapped(pieces, axis):
    count = lax.axis_size(axis)
    return [pieces[0]] + [
        lax.ppermute(pieces[k], axis, [(i, i ^ k) for i in range(count)]) for k in range(1, count)
    ]


def local(
    prompt,
    key_value_weight,
    key_gain,
    prompt_blocks,
    block_owner,
    block_slot,
    queries,
    cache_keys,
    cache_values,
    new_keys,
    new_values,
    decode_lengths,
):
    tensor_count = lax.axis_size("tensor")
    tensor_rank = lax.axis_index("tensor")
    group_count = lax.axis_size("section")
    group_index = lax.axis_index("section")
    rows_here = CAP * BLK // tensor_count
    heads_here = H // tensor_count
    rows = place_rows(prompt[0], block_owner, block_slot, group_count)
    candidates = [rows[0]] + [lax.ppermute(rows[k], "section", [(0, k)]) for k in range(1, group_count)]
    span_shares = attend_span(queries, cache_keys, cache_values, decode_lengths, tensor_count)
    span_shares = swapped(span_shares, "tensor")
    positions = lax.dynamic_slice_in_dim(
        slot_positions(prompt_blocks, block_owner, block_slot, group_index), tensor_rank * rows_here, rows_here, 0
    )
    cosine, sine = rotation_tables(positions)
    terms = swapped(project_rows(candidates, key_value_weight, tensor_count), "tensor")
    finished = finish_rows(terms, cosine, sine, key_gain[None, :])
    block_pool = join_rows(swapped([finished] * tensor_count, "tensor"))
    attended = merge_spans(span_shares, queries, new_keys, new_values, heads_here)
    return (attended, block_pool.reshape(1, CAP, BLK, -1))


def solution(mesh):
    in_specs = (
        P(("parts", "section"), None, "tensor"),
        P("tensor", None),
        P(),
        P("parts"),
        P("parts"),
        P("parts"),
        P(("parts", "section"), None),
        P(("parts", "section"), "tensor", None),
        P(("parts", "section"), "tensor", None),
        P(("parts", "section"), None),
        P(("parts", "section"), None),
        P(("parts", "section")),
    )
    out_specs = (P(("parts", "section"), "tensor"), P(("parts", "section"), None, None, None))
    tensor_count = mesh.shape["tensor"]
    whole_tiles = (CAP * BLK) % (16 * tensor_count) == 0 and H % (G * tensor_count) == 0
    program = local if whole_tiles else local_small_shares
    return jax.shard_map(program, mesh=mesh, in_specs=in_specs, out_specs=out_specs, check_vma=False)
```

```python
import math

import jax
import jax.numpy as jnp
from jax import lax
from jax.experimental import pallas as pl
from jax.experimental.pallas import tpu as pltpu
from jax.sharding import PartitionSpec as P

H = 64
KVH = 8
HD = 128
BLK = 16
SPAN = 128
KVW = 1024
G = 8
NB = 16
CAP = 4


NORM_EPSILON = 1e-06
ROPE_BASE = 1000000.0
MASKED_SCORE = -1e30


def exchange(pieces, axis):
    count = lax.axis_size(axis)
    rank = lax.axis_index(axis)
    landed = [lax.dynamic_index_in_dim(pieces, rank, 0, keepdims=False)]
    for step in range(1, count):
        piece = lax.dynamic_index_in_dim(pieces, rank ^ step, 0, keepdims=False)
        landed.append(lax.ppermute(piece, axis, [(i, i ^ step) for i in range(count)]))
    return landed


def collected(own, axis):
    count = lax.axis_size(axis)
    rank = lax.axis_index(axis)
    landed = [own]
    for step in range(1, count):
        landed.append(lax.ppermute(own, axis, [(i, i ^ step) for i in range(count)]))
    stacked = jnp.zeros((count,) + own.shape, own.dtype)
    for step, piece in enumerate(landed):
        stacked = lax.dynamic_update_index_in_dim(stacked, piece, rank ^ step, 0)
    return stacked


def rows_for_groups(states, block_owner, block_slot, group_count):
    slot_ids = jnp.arange(group_count * CAP, dtype=jnp.int32)
    selector = (block_owner * CAP + block_slot)[None, :] == slot_ids[:, None]
    filled = jnp.any(selector, axis=1)
    source = jnp.argmax(selector, axis=1)
    blocks = states.reshape(NB, BLK, states.shape[1])
    chosen = jnp.where(filled[:, None, None], blocks[source], jnp.zeros((), states.dtype))
    return chosen.reshape(group_count, CAP * BLK, states.shape[1])


def spread(rows, axis):
    count = lax.axis_size(axis)
    landed = jnp.where(lax.axis_index(axis) == 0, rows[0], jnp.zeros_like(rows[0]))
    for k in range(1, count):
        landed = landed + lax.ppermute(rows[k], axis, [(0, k)])
    return landed


def slot_positions(prompt_blocks, block_owner, block_slot, group_index):
    prompt_ends = jnp.cumsum(prompt_blocks)
    prompt_starts = prompt_ends - prompt_blocks
    slot_ids = jnp.arange(CAP, dtype=jnp.int32)
    selector = (block_owner[None, :] == group_index) & (block_slot[None, :] == slot_ids[:, None])
    block = jnp.sum(jnp.where(selector, jnp.arange(NB, dtype=jnp.int32)[None, :], 0), axis=1)
    inside = (block[:, None] >= prompt_starts[None, :]) & (block[:, None] < prompt_ends[None, :])
    first = jnp.sum(jnp.where(inside, prompt_starts[None, :], 0), axis=1)
    return (((block - first) * BLK)[:, None] + jnp.arange(BLK, dtype=jnp.int32)[None, :]).reshape(-1)


def finish_keys(projected, positions, key_gain):
    token_count = projected.shape[0]
    key_heads = projected[:, :KVW].reshape(token_count, KVH, HD)
    inv_root = lax.rsqrt(jnp.mean(key_heads * key_heads, axis=-1, keepdims=True) + NORM_EPSILON)
    key_heads = key_heads * inv_root * key_gain
    half_dim = HD // 2
    frequency = ROPE_BASE ** (jnp.arange(half_dim, dtype=jnp.float32) * (-2.0 / HD))
    angles = positions.astype(jnp.float32)[:, None, None] * frequency[None, None, :]
    cosine = jnp.cos(angles)
    sine_part = jnp.sin(angles)
    lower_half = key_heads[..., :half_dim]
    upper_half = key_heads[..., half_dim:]
    rotated = jnp.concatenate(
        [
            lower_half * cosine - upper_half * sine_part,
            upper_half * cosine + lower_half * sine_part,
        ],
        axis=-1,
    )
    return jnp.concatenate([rotated.reshape(token_count, KVW), projected[:, KVW:]], axis=1).astype(
        jnp.bfloat16
    )


def partial_attention(queries, cache_keys, cache_values, decode_lengths, first_position):
    row_count = queries.shape[0]
    local_len = cache_keys.shape[1]
    span_count = local_len // SPAN
    query_heads = queries.reshape(row_count, KVH, G, HD)
    key_heads = cache_keys.reshape(row_count, local_len, KVH, HD)
    scores = jnp.einsum(
        "rkgd,rpkd->rkgp", query_heads, key_heads, preferred_element_type=jnp.float32
    ) * HD ** (-0.5)
    live_mask = (first_position + jnp.arange(local_len, dtype=jnp.int32))[None, :] < decode_lengths[
        :, None
    ]
    scores = jnp.where(live_mask[:, None, None, :], scores, MASKED_SCORE)
    spans = scores.reshape(row_count, KVH, G, span_count, SPAN)
    span_max = jnp.max(spans, axis=-1)
    live_spans = live_mask.reshape(row_count, 1, 1, span_count, SPAN)
    weights = jnp.where(live_spans, jnp.exp(spans - span_max[..., None]), 0.0)
    span_sum = jnp.sum(weights, axis=-1)
    value_spans = cache_values.reshape(row_count, span_count, SPAN, KVH, HD)
    span_out = jnp.einsum(
        "rkgns,rnskd->rkgnd",
        weights.astype(jnp.bfloat16),
        value_spans,
        preferred_element_type=jnp.float32,
    )
    row_peak = jnp.max(span_max, axis=-1)
    factor = jnp.exp(span_max - row_peak[..., None])
    partial_out = jnp.sum(span_out * factor[..., None], axis=3)
    partial_sum = jnp.sum(span_sum * factor, axis=-1)
    return (
        partial_out.reshape(row_count, H, HD),
        row_peak.reshape(row_count, H),
        partial_sum.reshape(row_count, H),
    )


def combine_partials(former, latter):
    former_out, former_peak, former_sum = former
    latter_out, latter_peak, latter_sum = latter
    highest = jnp.maximum(former_peak, latter_peak)
    former_factor = jnp.exp(former_peak - highest)
    latter_factor = jnp.exp(latter_peak - highest)
    merged_out = former_out * former_factor[..., None] + latter_out * latter_factor[..., None]
    return (merged_out, highest, former_sum * former_factor + latter_sum * latter_factor)


def finish_heads(
    own_out, own_peak, own_sum, queries, new_keys, new_values, tensor_rank, heads_here
):
    row_count = queries.shape[0]
    own_width = heads_here * HD
    own_queries = (
        lax.dynamic_slice_in_dim(queries, tensor_rank * own_width, own_width, 1)
        .reshape(row_count, heads_here, HD)
        .astype(jnp.float32)
    )
    head_ids = tensor_rank * heads_here + jnp.arange(heads_here, dtype=jnp.int32)
    selector = (head_ids[:, None] // G == jnp.arange(KVH, dtype=jnp.int32)[None, :]).astype(
        jnp.float32
    )
    own_keys = jnp.einsum(
        "jk,rkd->rjd",
        selector,
        new_keys.reshape(row_count, KVH, HD).astype(jnp.float32),
        precision=lax.Precision.HIGHEST,
    )
    own_values = jnp.einsum(
        "jk,rkd->rjd",
        selector,
        new_values.reshape(row_count, KVH, HD).astype(jnp.float32),
        precision=lax.Precision.HIGHEST,
    )
    self_score = jnp.sum(own_queries * own_keys, axis=-1) * HD ** (-0.5)
    row_peak = jnp.maximum(own_peak, self_score)
    factor = jnp.exp(own_peak - row_peak)
    self_weight = jnp.exp(self_score - row_peak)
    numerator = own_out * factor[..., None] + self_weight[..., None] * own_values
    denominator = own_sum * factor + self_weight
    return (numerator / denominator[..., None]).reshape(row_count, own_width).astype(jnp.bfloat16)


def local_small_shares(
    prompt,
    key_value_weight,
    key_gain,
    prompt_blocks,
    block_owner,
    block_slot,
    queries,
    cache_keys,
    cache_values,
    new_keys,
    new_values,
    decode_lengths,
):
    tensor_count = lax.axis_size("tensor")
    tensor_rank = lax.axis_index("tensor")
    group_index = lax.axis_index("section")
    group_count = lax.axis_size("section")
    slot_rows = CAP * BLK
    rows_here = slot_rows // tensor_count
    rows = rows_for_groups(prompt[0], block_owner, block_slot, group_count)
    own_rows = spread(rows, "section")
    local_len = cache_keys.shape[1]
    row_count = queries.shape[0]
    heads_here = H // tensor_count
    partial_out, partial_peak, partial_sum = partial_attention(
        queries, cache_keys, cache_values, decode_lengths, tensor_rank * local_len
    )
    stats = jnp.stack([partial_peak, partial_sum], axis=-1).reshape(row_count, tensor_count, heads_here, 2)
    outs = partial_out.reshape(row_count, tensor_count, heads_here, HD)
    packed = jnp.concatenate([outs, jnp.pad(stats, ((0, 0), (0, 0), (0, 0), (0, HD - 2)))], axis=-1)
    shares = exchange(packed.transpose(1, 0, 2, 3), "tensor")
    merged = (shares[0][..., :HD], shares[0][..., HD], shares[0][..., HD + 1])
    for share in shares[1:]:
        merged = combine_partials(merged, (share[..., :HD], share[..., HD], share[..., HD + 1]))
    own_out, own_peak, own_sum = merged
    partial_terms = jnp.dot(own_rows, key_value_weight, preferred_element_type=jnp.float32)
    terms = exchange(partial_terms.reshape(tensor_count, rows_here, -1), "tensor")
    summed = sum(terms[1:], terms[0])
    positions = lax.dynamic_slice_in_dim(
        slot_positions(prompt_blocks, block_owner, block_slot, group_index), tensor_rank * rows_here, rows_here, 0
    )
    prompt_kv = finish_keys(summed, positions, key_gain)
    block_pool = collected(prompt_kv, "tensor").reshape(1, CAP, BLK, -1)
    attended = finish_heads(
        own_out, own_peak, own_sum, queries, new_keys, new_values, tensor_rank, heads_here
    )
    return (attended, block_pool)


VMEM = pl.BlockSpec(memory_space=pltpu.VMEM)
HBM = pl.BlockSpec(memory_space=pltpu.HBM)
F32 = jnp.float32
BF16 = jnp.bfloat16
I16 = jnp.int16
TOP = 32000.0
OCTAVE = 256.0
LN2 = math.log(2.0)
TINY = 1e-30


def on_chip(kernel, operands, in_specs, out_shapes, scratch=(), out_specs=None, flops=0, moved=0):
    return pl.pallas_call(
        kernel,
        out_shape=out_shapes,
        in_specs=in_specs,
        out_specs=out_specs or [VMEM] * len(out_shapes),
        scratch_shapes=list(scratch),
        compiler_params=pltpu.CompilerParams(vmem_limit_bytes=40 * 1024 * 1024),
        cost_estimate=pl.CostEstimate(flops=flops, bytes_accessed=moved, transcendentals=0),
    )(*operands)


def stays(array):
    return pltpu.with_memory_space_constraint(array, pltpu.HBM)


def level_of(peak):
    return jnp.ceil(jnp.log(jnp.maximum(peak, TINY)) * (OCTAVE / LN2))


def as_int16(value):
    return jnp.round(value).astype(jnp.int32).astype(I16)


def as_float(value):
    return value.astype(jnp.int32).astype(F32)


def table_of(block_owner, block_slot, prompt_blocks, decode_lengths):
    arrays = [block_owner, block_slot, prompt_blocks, decode_lengths]
    joined_up = jnp.concatenate(arrays)
    return jnp.pad(joined_up, (0, HD - joined_up.shape[0]))


def place_rows(own_states, near_states, table):
    width = own_states.shape[1]

    def kernel(table_ref, own_hbm, near_ref, keep_ref, send_ref, table, source, held, sems):
        core = lax.rem(lax.axis_index("section"), 2)
        large = pltpu.make_async_copy(own_hbm, held, sems.at[1])
        large.start()
        small = pltpu.make_async_copy(table_ref, table, sems.at[0])
        small.start()
        for j in range(2 * CAP):
            source[j] = -1
        small.wait()
        for b in range(NB):
            owner_b = table[b]

            @pl.when(lax.rem(owner_b, 2) == core)
            def _():
                source[(owner_b // 2) * CAP + table[NB + b]] = b

        large.wait()

        def place(states):
            for j in range(2 * CAP):
                b = source[j]
                start = pl.multiple_of(jnp.maximum(b, 0) * BLK, BLK)
                target = (keep_ref, send_ref)[j // CAP]
                target[pl.ds((j % CAP) * BLK, BLK), :] = states[pl.ds(start, BLK), :]

                @pl.when(b < 0)
                def _():
                    target[pl.ds((j % CAP) * BLK, BLK), :] = jnp.zeros((BLK, width), BF16)

        @pl.when(core == 0)
        def _():
            place(held)

        @pl.when(core == 1)
        def _():
            place(near_ref)

    return on_chip(
        kernel,
        (table, stays(own_states), near_states),
        [VMEM, HBM, VMEM],
        [jax.ShapeDtypeStruct((CAP * BLK, width), BF16)] * 2,
        [
            pltpu.SMEM((HD,), jnp.int32),
            pltpu.SMEM((2 * CAP,), jnp.int32),
            pltpu.VMEM(own_states.shape, BF16),
            pltpu.SemaphoreType.DMA((2,)),
        ],
        moved=own_states.size * 2,
    )


def attend_span(queries, cache_keys, cache_values, weight, table, prompt_count):
    row_count, local_len = cache_keys.shape[0], cache_keys.shape[1]
    tensor_count = lax.axis_size("tensor")
    rows_here = CAP * BLK // tensor_count
    slots_here = rows_here // BLK
    width = row_count * HD

    def kernel(
        table_ref, key_hbm, value_hbm, weight_hbm, query_ref,
        float_ref, code_ref, cosine_ref, sine_ref, weight_ref,
        table, keys, values, scores, weights, sems,
    ):
        pairs = [(table_ref, table), (key_hbm, keys), (value_hbm, values), (weight_hbm, weight_ref)]
        copies = [pltpu.make_async_copy(s, d, sems.at[i]) for i, (s, d) in enumerate(pairs)]
        for copy in copies:
            copy.start()
        group = lax.axis_index("section")
        rank = lax.axis_index("tensor")
        copies[0].wait()

        lane = lax.broadcasted_iota(jnp.int32, (BLK, HD), 1)
        row = lax.broadcasted_iota(jnp.int32, (BLK, HD), 0)
        half = lax.rem(lane, HD // 2).astype(F32)
        frequency = jnp.exp(half * (-2.0 / HD * math.log(ROPE_BASE)))
        for s in range(slots_here):
            block = 0
            for b in range(NB):
                block = jnp.where((table[b] == group) & (table[NB + b] == rank * slots_here + s), b, block)
            first, begin = 0, 0
            for j in range(prompt_count):
                first = jnp.where(block >= begin, begin, first)
                begin = begin + table[2 * NB + j]
            angles = ((block - first) * BLK + row).astype(F32) * frequency
            cosine_ref[pl.ds(s * BLK, BLK), :] = jnp.cos(angles)
            sine = jnp.sin(angles)
            sine_ref[pl.ds(s * BLK, BLK), :] = jnp.where(lane < HD // 2, -sine, sine)

        copies[1].wait()
        for r in range(row_count):
            for pair in range(KVH // 2):
                pair_queries = query_ref[r, pl.ds(pair * 2 * G, 2 * G), :]
                for n in (2 * pair, 2 * pair + 1):
                    both = lax.dot_general(
                        pair_queries,
                        keys[r, :, n * HD : (n + 1) * HD],
                        (((1,), (1,)), ((), ())),
                        preferred_element_type=F32,
                    )
                    scores[r, pl.ds(n * G, G), :] = both[(n % 2) * G : (n % 2 + 1) * G]
        place = lax.broadcasted_iota(jnp.int32, (H, local_len), 1) + rank * local_len
        column = lax.broadcasted_iota(jnp.int32, (H, HD), 1)
        stats = jnp.zeros((H, HD), F32)
        for r in range(row_count):
            live = place < table[2 * NB + prompt_count + r]
            row_scores = jnp.where(live, scores[r] * HD ** (-0.5), MASKED_SCORE)
            peak = jnp.max(row_scores, axis=1, keepdims=True)
            weight = jnp.where(live, jnp.exp(row_scores - peak), 0.0)
            total = jnp.sum(weight, axis=1, keepdims=True)
            weights[r] = weight.astype(BF16)
            stats = jnp.where(column == r, peak, stats)
            stats = jnp.where(column == row_count + r, total, stats)
        float_ref[:, pl.ds(width, HD)] = stats
        copies[2].wait()
        levels = jnp.zeros((H, HD), F32)
        for r in range(row_count):
            for pair in range(KVH // 2):
                pair_weights = weights[r, pl.ds(pair * 2 * G, 2 * G), :]
                for n in (2 * pair, 2 * pair + 1):
                    both = jnp.dot(
                        pair_weights, values[r, :, n * HD : (n + 1) * HD], preferred_element_type=F32
                    )
                    float_ref[pl.ds(n * G, G), pl.ds(r * HD, HD)] = both[(n % 2) * G : (n % 2 + 1) * G]
        for r in range(row_count):
            peak = jnp.max(jnp.abs(float_ref[:, pl.ds(r * HD, HD)]), axis=1, keepdims=True)
            levels = jnp.where(column == r, peak, levels)
        levels = level_of(levels)
        scale = TOP * jnp.exp(levels * (-LN2 / OCTAVE))
        for r in range(row_count):
            out = float_ref[:, pl.ds(r * HD, HD)]
            code_ref[:, pl.ds(r * HD, HD)] = as_int16(out * scale[:, r : r + 1])
        peaks = jnp.maximum(stats, -TOP)
        fine = jnp.where(column < row_count, peaks, stats * HD)
        whole = jnp.floor(fine)
        part = (fine - whole) * TOP
        packed = jnp.where(column < 2 * row_count, whole, 0.0)
        shifted = pltpu.roll(jnp.where(column < 2 * row_count, part, 0.0), 2 * row_count, 1)
        moved = pltpu.roll(jnp.where(column < row_count, levels, 0.0), 4 * row_count, 1)
        code_ref[:, pl.ds(width, HD)] = as_int16(packed + shifted + moved)
        copies[3].wait()

    return on_chip(
        kernel,
        (table, stays(cache_keys), stays(cache_values), stays(weight), queries.reshape(row_count, H, HD)),
        [VMEM, HBM, HBM, HBM, VMEM],
        [
            jax.ShapeDtypeStruct((H, width + HD), F32),
            jax.ShapeDtypeStruct((H, width + HD), I16),
            jax.ShapeDtypeStruct((rows_here, HD), F32),
            jax.ShapeDtypeStruct((rows_here, HD), F32),
            jax.ShapeDtypeStruct(weight.shape, BF16),
        ],
        [
            pltpu.SMEM((HD,), jnp.int32),
            pltpu.VMEM(cache_keys.shape, BF16),
            pltpu.VMEM(cache_values.shape, BF16),
            pltpu.VMEM((row_count, H, local_len), F32),
            pltpu.VMEM((row_count, H, local_len), BF16),
            pltpu.SemaphoreType.DMA((4,)),
        ],
        flops=4 * row_count * H * HD * local_len,
        moved=4 * cache_keys.size + 2 * weight.size,
    )


def project_rows(kept, landed, weight, span_code, tensor_count):
    slot_rows, depth = kept.shape
    width = weight.shape[1]
    rows_here = slot_rows // tensor_count
    span_width = span_code.shape[1]
    heads_here = H // tensor_count
    share_width = width + span_width + HD
    step_width = 512

    def kernel(kept_ref, landed_ref, weight_ref, span_ref, own_ref, *refs):
        share_refs, rows_ref, held = refs[: tensor_count - 1], refs[-2], refs[-1]
        far = lax.axis_index("section") >= 2
        rank = lax.axis_index("tensor")
        rows_ref[...] = jnp.where(far, landed_ref[...], kept_ref[...])
        for c in range(width // step_width):
            columns = pl.ds(c * step_width, step_width)
            held[:, columns] = jnp.dot(rows_ref[...], weight_ref[:, columns], preferred_element_type=F32)
        own_ref[...] = held[pl.ds(pl.multiple_of(rank * rows_here, rows_here), rows_here), :]
        lane = lax.broadcasted_iota(jnp.int32, (rows_here, HD), 1)
        for step in range(1, tensor_count):
            share_ref = share_refs[step - 1]
            rows = pl.ds(pl.multiple_of((rank ^ step) * rows_here, rows_here), rows_here)
            heads = pl.ds(pl.multiple_of((rank ^ step) * heads_here, heads_here), heads_here)
            levels = jnp.zeros((rows_here, HD), F32)
            for n in range(width // HD):
                peak = jnp.max(jnp.abs(held[rows, pl.ds(n * HD, HD)]), axis=1, keepdims=True)
                levels = jnp.where(lane == n, peak, levels)
            levels = level_of(levels)
            scale = TOP * jnp.exp(levels * (-LN2 / OCTAVE))
            for n in range(width // HD):
                columns = pl.ds(n * HD, HD)
                share_ref[:, columns] = as_int16(held[rows, columns] * scale[:, n : n + 1])
            share_ref[:, pl.ds(width, span_width)] = span_ref[heads, :]
            share_ref[:, pl.ds(width + span_width, HD)] = as_int16(levels)

    return on_chip(
        kernel,
        (kept, landed, weight, span_code),
        [VMEM] * 4,
        [jax.ShapeDtypeStruct((rows_here, width), F32)]
        + [jax.ShapeDtypeStruct((rows_here, share_width), I16)] * (tensor_count - 1),
        [pltpu.VMEM((slot_rows, depth), BF16), pltpu.VMEM((slot_rows, width), F32)],
        flops=2 * slot_rows * depth * width,
        moved=2 * weight.size,
    )


def finish_rows(own, shares, cosine, sine, gain):
    rows, width = own.shape
    share_count = len(shares)
    share_width = shares[0].shape[1]

    def kernel(own_ref, *refs):
        share_refs = refs[:share_count]
        cosine_ref, sine_ref, gain_ref, out_ref = refs[share_count:]
        scales = [
            jnp.exp(as_float(ref[:, pl.ds(share_width - HD, HD)]) * (LN2 / OCTAVE)) * (1.0 / TOP)
            for ref in share_refs
        ]
        for n in range(width // HD):
            columns = pl.ds(n * HD, HD)
            total = own_ref[:, columns]
            for ref, scale in zip(share_refs, scales):
                total = total + as_float(ref[:, columns]) * scale[:, n : n + 1]
            if n < KVH:
                mean = jnp.sum(total * total, axis=1, keepdims=True) * (1.0 / HD)
                total = total * lax.rsqrt(mean + NORM_EPSILON) * gain_ref[...]
                total = total * cosine_ref[...] + pltpu.roll(total, HD // 2, 1) * sine_ref[...]
            out_ref[:, columns] = total.astype(BF16)

    return on_chip(
        kernel,
        (own, *shares, cosine, sine, gain),
        [VMEM] * (share_count + 4),
        [jax.ShapeDtypeStruct((rows, width), BF16)],
    )[0]


def merge_spans(span_float, shares, queries, new_keys, new_values, width):
    row_count = queries.shape[0]
    share_count = len(shares)
    heads_here = shares[0].shape[0]
    keys_here = heads_here // G
    span_width = row_count * HD

    def kernel(own_ref, *refs):
        share_refs = refs[:share_count]
        query_ref, key_ref, value_ref, out_ref = refs[share_count:]
        rank = lax.axis_index("tensor")
        heads = pl.ds(pl.multiple_of(rank * heads_here, heads_here), heads_here)
        columns = pl.ds(pl.multiple_of(rank * keys_here * HD, HD), keys_here * HD)
        new_key, new_value = key_ref[:, columns].astype(F32), value_ref[:, columns].astype(F32)

        def spread(tile, r):
            return jnp.concatenate(
                [
                    jnp.broadcast_to(tile[r : r + 1, kk * HD : (kk + 1) * HD], (G, HD))
                    for kk in range(keys_here)
                ],
                axis=0,
            )

        stats = [own_ref[heads, pl.ds(span_width, HD)]]
        scales = [None]
        for ref in share_refs:
            code = as_float(ref[:, pl.ds(width + span_width, HD)])
            fine = code + pltpu.roll(code, HD - 2 * row_count, 1) * (1.0 / TOP)
            column = lax.broadcasted_iota(jnp.int32, code.shape, 1)
            stats.append(jnp.where(column < row_count, fine, fine * (1.0 / HD)))
            scales.append(jnp.exp(code * (LN2 / OCTAVE)) * (1.0 / TOP))
        for r in range(row_count):
            query = query_ref[r, heads, :].astype(F32)
            self_score = jnp.sum(query * spread(new_key, r), axis=1, keepdims=True) * HD ** (-0.5)
            row_peak = self_score
            for tile in stats:
                row_peak = jnp.maximum(row_peak, tile[:, r : r + 1])
            self_weight = jnp.exp(self_score - row_peak)
            numerator = self_weight * spread(new_value, r)
            denominator = self_weight
            for k, tile in enumerate(stats):
                factor = jnp.exp(tile[:, r : r + 1] - row_peak)
                if k == 0:
                    out = own_ref[heads, pl.ds(r * HD, HD)]
                else:
                    out = as_float(share_refs[k - 1][:, pl.ds(width + r * HD, HD)])
                    out = out * scales[k][:, 4 * row_count + r : 4 * row_count + r + 1]
                numerator += factor * out
                denominator += factor * tile[:, row_count + r : row_count + r + 1]
            out_ref[r] = (numerator / denominator).astype(BF16)

    attended = on_chip(
        kernel,
        (span_float, *shares, queries.reshape(row_count, H, HD), new_keys, new_values),
        [VMEM] * (share_count + 4),
        [jax.ShapeDtypeStruct((row_count, heads_here, HD), BF16)],
    )[0]
    return attended.reshape(row_count, heads_here * HD)


def join_rows(pieces):
    count = len(pieces)
    rows, width = pieces[0].shape

    def kernel(*refs):
        piece_refs, out_hbm, sems = refs[:count], refs[count], refs[count + 1]
        rank = lax.axis_index("tensor")
        copies = []
        for step in range(count):
            place = pl.ds(pl.multiple_of((rank ^ step) * rows, rows), rows)
            copies.append(pltpu.make_async_copy(piece_refs[step], out_hbm.at[place], sems.at[step]))
        for copy in copies:
            copy.start()
        for copy in copies:
            copy.wait()

    return on_chip(
        kernel,
        pieces,
        [VMEM] * count,
        [jax.ShapeDtypeStruct((count * rows, width), BF16)],
        [pltpu.SemaphoreType.DMA((count,))],
        out_specs=[HBM],
    )[0]


def swap(piece, axis, step):
    return lax.ppermute(piece, axis, [(i, i ^ step) for i in range(lax.axis_size(axis))])


def local(
    prompt,
    key_value_weight,
    key_gain,
    prompt_blocks,
    block_owner,
    block_slot,
    queries,
    cache_keys,
    cache_values,
    new_keys,
    new_values,
    decode_lengths,
):
    tensor_count = lax.axis_size("tensor")
    near_states = swap(prompt[0], "section", 1)
    table = table_of(block_owner, block_slot, prompt_blocks, decode_lengths)
    kept, sent = place_rows(prompt[0], near_states, table)
    landed = swap(sent, "section", 2)
    span_float, span_code, cosine, sine, weight = attend_span(
        queries, cache_keys, cache_values, key_value_weight, table, prompt_blocks.shape[0]
    )
    own, *shares = project_rows(kept, landed, weight, span_code, tensor_count)
    shares = [swap(share, "tensor", k + 1) for k, share in enumerate(shares)]
    finished = finish_rows(own, shares, cosine, sine, key_gain[None, :])
    pieces = [finished] + [swap(finished, "tensor", k) for k in range(1, tensor_count)]
    block_pool = join_rows(pieces)
    attended = merge_spans(span_float, shares, queries, new_keys, new_values, key_value_weight.shape[1])
    return (attended, block_pool.reshape(1, CAP, BLK, -1))


def solution(mesh):
    in_specs = (
        P(("parts", "section"), None, "tensor"),
        P("tensor", None),
        P(),
        P("parts"),
        P("parts"),
        P("parts"),
        P(("parts", "section"), None),
        P(("parts", "section"), "tensor", None),
        P(("parts", "section"), "tensor", None),
        P(("parts", "section"), None),
        P(("parts", "section"), None),
        P(("parts", "section")),
    )
    out_specs = (P(("parts", "section"), "tensor"), P(("parts", "section"), None, None, None))
    tensor_count = mesh.shape["tensor"]
    whole_tiles = tensor_count == 4 and mesh.shape["section"] == 4
    program = local if whole_tiles else local_small_shares
    return jax.shard_map(program, mesh=mesh, in_specs=in_specs, out_specs=out_specs, check_vma=False)
```

```python
import math

import jax
import jax.numpy as jnp
from jax import lax
from jax.experimental import pallas as pl
from jax.experimental.pallas import tpu as pltpu
from jax.sharding import PartitionSpec as P

H = 64
KVH = 8
HD = 128
BLK = 16
SPAN = 128
KVW = 1024
G = 8
NB = 16
CAP = 4


NORM_EPSILON = 1e-06
ROPE_BASE = 1000000.0
MASKED_SCORE = -1e30


def exchange(pieces, axis):
    count = lax.axis_size(axis)
    rank = lax.axis_index(axis)
    landed = [lax.dynamic_index_in_dim(pieces, rank, 0, keepdims=False)]
    for step in range(1, count):
        piece = lax.dynamic_index_in_dim(pieces, rank ^ step, 0, keepdims=False)
        landed.append(lax.ppermute(piece, axis, [(i, i ^ step) for i in range(count)]))
    return landed


def collected(own, axis):
    count = lax.axis_size(axis)
    rank = lax.axis_index(axis)
    landed = [own]
    for step in range(1, count):
        landed.append(lax.ppermute(own, axis, [(i, i ^ step) for i in range(count)]))
    stacked = jnp.zeros((count,) + own.shape, own.dtype)
    for step, piece in enumerate(landed):
        stacked = lax.dynamic_update_index_in_dim(stacked, piece, rank ^ step, 0)
    return stacked


def rows_for_groups(states, block_owner, block_slot, group_count):
    slot_ids = jnp.arange(group_count * CAP, dtype=jnp.int32)
    selector = (block_owner * CAP + block_slot)[None, :] == slot_ids[:, None]
    filled = jnp.any(selector, axis=1)
    source = jnp.argmax(selector, axis=1)
    blocks = states.reshape(NB, BLK, states.shape[1])
    chosen = jnp.where(filled[:, None, None], blocks[source], jnp.zeros((), states.dtype))
    return chosen.reshape(group_count, CAP * BLK, states.shape[1])


def spread(rows, axis):
    count = lax.axis_size(axis)
    landed = jnp.where(lax.axis_index(axis) == 0, rows[0], jnp.zeros_like(rows[0]))
    for k in range(1, count):
        landed = landed + lax.ppermute(rows[k], axis, [(0, k)])
    return landed


def slot_positions(prompt_blocks, block_owner, block_slot, group_index):
    prompt_ends = jnp.cumsum(prompt_blocks)
    prompt_starts = prompt_ends - prompt_blocks
    slot_ids = jnp.arange(CAP, dtype=jnp.int32)
    selector = (block_owner[None, :] == group_index) & (block_slot[None, :] == slot_ids[:, None])
    block = jnp.sum(jnp.where(selector, jnp.arange(NB, dtype=jnp.int32)[None, :], 0), axis=1)
    inside = (block[:, None] >= prompt_starts[None, :]) & (block[:, None] < prompt_ends[None, :])
    first = jnp.sum(jnp.where(inside, prompt_starts[None, :], 0), axis=1)
    return (((block - first) * BLK)[:, None] + jnp.arange(BLK, dtype=jnp.int32)[None, :]).reshape(-1)


def finish_keys(projected, positions, key_gain):
    token_count = projected.shape[0]
    key_heads = projected[:, :KVW].reshape(token_count, KVH, HD)
    inv_root = lax.rsqrt(jnp.mean(key_heads * key_heads, axis=-1, keepdims=True) + NORM_EPSILON)
    key_heads = key_heads * inv_root * key_gain
    half_dim = HD // 2
    frequency = ROPE_BASE ** (jnp.arange(half_dim, dtype=jnp.float32) * (-2.0 / HD))
    angles = positions.astype(jnp.float32)[:, None, None] * frequency[None, None, :]
    cosine = jnp.cos(angles)
    sine_part = jnp.sin(angles)
    lower_half = key_heads[..., :half_dim]
    upper_half = key_heads[..., half_dim:]
    rotated = jnp.concatenate(
        [
            lower_half * cosine - upper_half * sine_part,
            upper_half * cosine + lower_half * sine_part,
        ],
        axis=-1,
    )
    return jnp.concatenate([rotated.reshape(token_count, KVW), projected[:, KVW:]], axis=1).astype(
        jnp.bfloat16
    )


def partial_attention(queries, cache_keys, cache_values, decode_lengths, first_position):
    row_count = queries.shape[0]
    local_len = cache_keys.shape[1]
    span_count = local_len // SPAN
    query_heads = queries.reshape(row_count, KVH, G, HD)
    key_heads = cache_keys.reshape(row_count, local_len, KVH, HD)
    scores = jnp.einsum(
        "rkgd,rpkd->rkgp", query_heads, key_heads, preferred_element_type=jnp.float32
    ) * HD ** (-0.5)
    live_mask = (first_position + jnp.arange(local_len, dtype=jnp.int32))[None, :] < decode_lengths[
        :, None
    ]
    scores = jnp.where(live_mask[:, None, None, :], scores, MASKED_SCORE)
    spans = scores.reshape(row_count, KVH, G, span_count, SPAN)
    span_max = jnp.max(spans, axis=-1)
    live_spans = live_mask.reshape(row_count, 1, 1, span_count, SPAN)
    weights = jnp.where(live_spans, jnp.exp(spans - span_max[..., None]), 0.0)
    span_sum = jnp.sum(weights, axis=-1)
    value_spans = cache_values.reshape(row_count, span_count, SPAN, KVH, HD)
    span_out = jnp.einsum(
        "rkgns,rnskd->rkgnd",
        weights.astype(jnp.bfloat16),
        value_spans,
        preferred_element_type=jnp.float32,
    )
    row_peak = jnp.max(span_max, axis=-1)
    factor = jnp.exp(span_max - row_peak[..., None])
    partial_out = jnp.sum(span_out * factor[..., None], axis=3)
    partial_sum = jnp.sum(span_sum * factor, axis=-1)
    return (
        partial_out.reshape(row_count, H, HD),
        row_peak.reshape(row_count, H),
        partial_sum.reshape(row_count, H),
    )


def combine_partials(former, latter):
    former_out, former_peak, former_sum = former
    latter_out, latter_peak, latter_sum = latter
    highest = jnp.maximum(former_peak, latter_peak)
    former_factor = jnp.exp(former_peak - highest)
    latter_factor = jnp.exp(latter_peak - highest)
    merged_out = former_out * former_factor[..., None] + latter_out * latter_factor[..., None]
    return (merged_out, highest, former_sum * former_factor + latter_sum * latter_factor)


def finish_heads(
    own_out, own_peak, own_sum, queries, new_keys, new_values, tensor_rank, heads_here
):
    row_count = queries.shape[0]
    own_width = heads_here * HD
    own_queries = (
        lax.dynamic_slice_in_dim(queries, tensor_rank * own_width, own_width, 1)
        .reshape(row_count, heads_here, HD)
        .astype(jnp.float32)
    )
    head_ids = tensor_rank * heads_here + jnp.arange(heads_here, dtype=jnp.int32)
    selector = (head_ids[:, None] // G == jnp.arange(KVH, dtype=jnp.int32)[None, :]).astype(
        jnp.float32
    )
    own_keys = jnp.einsum(
        "jk,rkd->rjd",
        selector,
        new_keys.reshape(row_count, KVH, HD).astype(jnp.float32),
        precision=lax.Precision.HIGHEST,
    )
    own_values = jnp.einsum(
        "jk,rkd->rjd",
        selector,
        new_values.reshape(row_count, KVH, HD).astype(jnp.float32),
        precision=lax.Precision.HIGHEST,
    )
    self_score = jnp.sum(own_queries * own_keys, axis=-1) * HD ** (-0.5)
    row_peak = jnp.maximum(own_peak, self_score)
    factor = jnp.exp(own_peak - row_peak)
    self_weight = jnp.exp(self_score - row_peak)
    numerator = own_out * factor[..., None] + self_weight[..., None] * own_values
    denominator = own_sum * factor + self_weight
    return (numerator / denominator[..., None]).reshape(row_count, own_width).astype(jnp.bfloat16)


def local_small_shares(
    prompt,
    key_value_weight,
    key_gain,
    prompt_blocks,
    block_owner,
    block_slot,
    queries,
    cache_keys,
    cache_values,
    new_keys,
    new_values,
    decode_lengths,
):
    tensor_count = lax.axis_size("tensor")
    tensor_rank = lax.axis_index("tensor")
    group_index = lax.axis_index("section")
    group_count = lax.axis_size("section")
    slot_rows = CAP * BLK
    rows_here = slot_rows // tensor_count
    rows = rows_for_groups(prompt[0], block_owner, block_slot, group_count)
    own_rows = spread(rows, "section")
    local_len = cache_keys.shape[1]
    row_count = queries.shape[0]
    heads_here = H // tensor_count
    partial_out, partial_peak, partial_sum = partial_attention(
        queries, cache_keys, cache_values, decode_lengths, tensor_rank * local_len
    )
    stats = jnp.stack([partial_peak, partial_sum], axis=-1).reshape(row_count, tensor_count, heads_here, 2)
    outs = partial_out.reshape(row_count, tensor_count, heads_here, HD)
    packed = jnp.concatenate([outs, jnp.pad(stats, ((0, 0), (0, 0), (0, 0), (0, HD - 2)))], axis=-1)
    shares = exchange(packed.transpose(1, 0, 2, 3), "tensor")
    merged = (shares[0][..., :HD], shares[0][..., HD], shares[0][..., HD + 1])
    for share in shares[1:]:
        merged = combine_partials(merged, (share[..., :HD], share[..., HD], share[..., HD + 1]))
    own_out, own_peak, own_sum = merged
    partial_terms = jnp.dot(own_rows, key_value_weight, preferred_element_type=jnp.float32)
    terms = exchange(partial_terms.reshape(tensor_count, rows_here, -1), "tensor")
    summed = sum(terms[1:], terms[0])
    positions = lax.dynamic_slice_in_dim(
        slot_positions(prompt_blocks, block_owner, block_slot, group_index), tensor_rank * rows_here, rows_here, 0
    )
    prompt_kv = finish_keys(summed, positions, key_gain)
    block_pool = collected(prompt_kv, "tensor").reshape(1, CAP, BLK, -1)
    attended = finish_heads(
        own_out, own_peak, own_sum, queries, new_keys, new_values, tensor_rank, heads_here
    )
    return (attended, block_pool)


VMEM = pl.BlockSpec(memory_space=pltpu.VMEM)
HBM = pl.BlockSpec(memory_space=pltpu.HBM)
F32 = jnp.float32
BF16 = jnp.bfloat16
I16 = jnp.int16
TOP = 32000.0
OCTAVE = 256.0
LN2 = math.log(2.0)
TINY = 1e-30
LEVELS = 64


def on_chip(kernel, operands, in_specs, out_shapes, scratch=(), out_specs=None, flops=0, moved=0):
    return pl.pallas_call(
        kernel,
        out_shape=out_shapes,
        in_specs=in_specs,
        out_specs=out_specs or [VMEM] * len(out_shapes),
        scratch_shapes=list(scratch),
        compiler_params=pltpu.CompilerParams(vmem_limit_bytes=40 * 1024 * 1024),
        cost_estimate=pl.CostEstimate(flops=flops, bytes_accessed=moved, transcendentals=0),
    )(*operands)


def stays(array):
    return pltpu.with_memory_space_constraint(array, pltpu.HBM)


def level_of(peak):
    return jnp.ceil(jnp.log(jnp.maximum(peak, TINY)) * (OCTAVE / LN2))


def as_int16(value):
    return jnp.round(value).astype(jnp.int32).astype(I16)


def as_float(value):
    return value.astype(jnp.int32).astype(F32)


def prepare(states, key_gain, block_owner, block_slot, prompt_blocks):
    rows_here = CAP * BLK // lax.axis_size("tensor")
    slots_here = rows_here // BLK
    prompt_count = prompt_blocks.shape[0]
    fetched = [block_owner, block_slot, prompt_blocks, key_gain[None, :]]
    count = len(fetched)

    def kernel(*refs):
        sources, states_hbm = refs[:count], refs[count]
        cosine_ref, sine_ref, states_ref, table_ref = refs[count + 1 : count + 5]
        held, (source, sems) = refs[count + 5 : 2 * count + 5], refs[2 * count + 5 :]
        owner, slot, prompts, gain = held
        copies = [pltpu.make_async_copy(s, d, sems.at[i]) for i, (s, d) in enumerate(zip(sources, held))]
        copies.append(pltpu.make_async_copy(states_hbm, states_ref, sems.at[count]))
        for copy in copies:
            copy.start()
        group = lax.axis_index("section")
        rank = lax.axis_index("tensor")
        core = lax.rem(group, 2)
        for copy in copies[:count]:
            copy.wait()

        for j in range(2 * CAP):
            source[j] = -1
        for b in range(NB):

            @pl.when(owner[b] == core)
            def _():
                source[slot[b]] = b

            @pl.when(owner[b] == 3 - core)
            def _():
                source[CAP + slot[b]] = b

        column = lax.broadcasted_iota(jnp.int32, (8, HD), 1)
        table = jnp.zeros((8, HD), jnp.int32)
        for j in range(2 * CAP):
            table = jnp.where(column == j, source[j], table)
        table_ref[...] = table

        lane = lax.broadcasted_iota(jnp.int32, (BLK, HD), 1)
        row = lax.broadcasted_iota(jnp.int32, (BLK, HD), 0)
        half = lax.rem(lane, HD // 2).astype(F32)
        frequency = jnp.exp(half * (-2.0 / HD * math.log(ROPE_BASE)))
        far_gain = pltpu.roll(jnp.broadcast_to(gain[...], (8, HD)), HD // 2, 1)[0:1]
        for s in range(slots_here):
            block = 0
            for b in range(NB):
                block = jnp.where((owner[b] == group) & (slot[b] == rank * slots_here + s), b, block)
            first, begin = 0, 0
            for j in range(prompt_count):
                first = jnp.where(block >= begin, begin, first)
                begin = begin + prompts[j]
            angles = ((block - first) * BLK + row).astype(F32) * frequency
            cosine_ref[pl.ds(s * BLK, BLK), :] = jnp.cos(angles) * gain[...]
            sine = jnp.sin(angles) * far_gain
            sine_ref[pl.ds(s * BLK, BLK), :] = jnp.where(lane < HD // 2, -sine, sine)
        copies[count].wait()

    return on_chip(
        kernel,
        [stays(array) for array in (*fetched, states)],
        [HBM] * (count + 1),
        [
            jax.ShapeDtypeStruct((rows_here, HD), F32),
            jax.ShapeDtypeStruct((rows_here, HD), F32),
            jax.ShapeDtypeStruct(states.shape, BF16),
            jax.ShapeDtypeStruct((8, HD), jnp.int32),
        ],
        [pltpu.SMEM(array.shape, jnp.int32) for array in fetched[:3]]
        + [
            pltpu.VMEM((1, HD), F32),
            pltpu.SMEM((2 * CAP,), jnp.int32),
            pltpu.SemaphoreType.DMA((count + 1,)),
        ],
        moved=2 * states.size,
    )


def place_rows(own_states, near_states, table):
    width = own_states.shape[1]

    def kernel(own_ref, near_ref, table_ref, keep_ref, send_ref, source, sem):
        core = lax.rem(lax.axis_index("section"), 2)
        copy = pltpu.make_async_copy(table_ref, source, sem)
        copy.start()
        copy.wait()

        def place(states):
            for j in range(2 * CAP):
                b = source[0, j]
                start = pl.multiple_of(jnp.maximum(b, 0) * BLK, BLK)
                target = (keep_ref, send_ref)[j // CAP]
                target[pl.ds((j % CAP) * BLK, BLK), :] = states[pl.ds(start, BLK), :]

                @pl.when(b < 0)
                def _():
                    target[pl.ds((j % CAP) * BLK, BLK), :] = jnp.zeros((BLK, width), BF16)

        @pl.when(core == 0)
        def _():
            place(own_ref)

        @pl.when(core == 1)
        def _():
            place(near_ref)

    return on_chip(
        kernel,
        (own_states, near_states, table),
        [VMEM] * 3,
        [jax.ShapeDtypeStruct((CAP * BLK, width), BF16)] * 2,
        [pltpu.SMEM((8, HD), jnp.int32), pltpu.SemaphoreType.DMA(())],
        moved=own_states.size * 2,
    )


def attend_span(queries, cache_keys, cache_values, decode_lengths, weight, after):
    row_count, local_len = cache_keys.shape[0], cache_keys.shape[1]
    width = row_count * HD
    fetched = [decode_lengths, queries, cache_keys, cache_values]
    count = len(fetched)

    def kernel(*refs):
        sources, weight_hbm = refs[:count], refs[count]
        span_ref, code_ref, query_ref, weight_ref = refs[count + 2 : count + 6]
        held, (scores, weights, sems) = refs[count + 6 : 2 * count + 6], refs[2 * count + 6 :]
        length, packed, keys, values = held
        copies = [pltpu.make_async_copy(s, d, sems.at[i]) for i, (s, d) in enumerate(zip(sources, held))]
        copies.append(pltpu.make_async_copy(weight_hbm, weight_ref, sems.at[count]))
        for copy in copies:
            copy.start()
        rank = lax.axis_index("tensor")
        copies[0].wait()
        copies[1].wait()
        for h in range(H):
            piece = packed[:, pl.ds(h * HD, HD)].astype(F32)
            query_ref[pl.ds(h, row_count, stride=H), :] = piece
        copies[2].wait()
        for r in range(row_count):
            for pair in range(KVH // 2):
                pair_queries = query_ref[pl.ds(r * H + pair * 2 * G, 2 * G), :].astype(BF16)
                for n in (2 * pair, 2 * pair + 1):
                    both = lax.dot_general(
                        pair_queries,
                        keys[r, :, n * HD : (n + 1) * HD],
                        (((1,), (1,)), ((), ())),
                        preferred_element_type=F32,
                    )
                    scores[r, pl.ds(n * G, G), :] = both[(n % 2) * G : (n % 2 + 1) * G]
        place = lax.broadcasted_iota(jnp.int32, (H, local_len), 1) + rank * local_len
        column = lax.broadcasted_iota(jnp.int32, (H, HD), 1)
        stats = jnp.zeros((H, HD), F32)
        for r in range(row_count):
            live = place < length[r]
            row_scores = jnp.where(live, scores[r] * HD ** (-0.5), MASKED_SCORE)
            peak = jnp.max(row_scores, axis=1, keepdims=True)
            weight = jnp.where(live, jnp.exp(row_scores - peak), 0.0)
            total = jnp.sum(weight, axis=1, keepdims=True)
            weights[r] = weight.astype(BF16)
            stats = jnp.where(column == r, peak, stats)
            stats = jnp.where(column == row_count + r, total, stats)
        span_ref[:, pl.ds(width, HD)] = stats
        copies[3].wait()
        levels = jnp.zeros((H, HD), F32)
        for r in range(row_count):
            for pair in range(KVH // 2):
                pair_weights = weights[r, pl.ds(pair * 2 * G, 2 * G), :]
                for n in (2 * pair, 2 * pair + 1):
                    both = jnp.dot(
                        pair_weights, values[r, :, n * HD : (n + 1) * HD], preferred_element_type=F32
                    )
                    span_ref[pl.ds(n * G, G), pl.ds(r * HD, HD)] = both[(n % 2) * G : (n % 2 + 1) * G]
        for r in range(row_count):
            peak = jnp.max(jnp.abs(span_ref[:, pl.ds(r * HD, HD)]), axis=1, keepdims=True)
            levels = jnp.where(column == r, peak, levels)
        levels = level_of(levels)
        scale = TOP * jnp.exp(levels * (-LN2 / OCTAVE))
        for r in range(row_count):
            out = span_ref[:, pl.ds(r * HD, HD)]
            code_ref[:, pl.ds(r * HD, HD)] = as_int16(out * scale[:, r : r + 1])
        peaks = jnp.maximum(stats, -TOP)
        fine = jnp.where(column < row_count, peaks, stats * HD)
        whole = jnp.floor(fine)
        part = (fine - whole) * TOP
        coded = jnp.where(column < 2 * row_count, whole, 0.0)
        shifted = pltpu.roll(jnp.where(column < 2 * row_count, part, 0.0), 2 * row_count, 1)
        moved = pltpu.roll(jnp.where(column < row_count, levels, 0.0), 4 * row_count, 1)
        code_ref[:, pl.ds(width, HD)] = as_int16(coded + shifted + moved)
        copies[count].wait()

    return on_chip(
        kernel,
        [stays(array) for array in (*fetched, weight)] + [after],
        [HBM] * (count + 1) + [pl.BlockSpec(memory_space=pl.ANY)],
        [
            jax.ShapeDtypeStruct((H, width + HD), F32),
            jax.ShapeDtypeStruct((H, width + HD), I16),
            jax.ShapeDtypeStruct((row_count * H, HD), F32),
            jax.ShapeDtypeStruct(weight.shape, BF16),
        ],
        [pltpu.SMEM((row_count,), jnp.int32)]
        + [pltpu.VMEM(array.shape, array.dtype) for array in fetched[1:]]
        + [
            pltpu.VMEM((row_count, H, local_len), F32),
            pltpu.VMEM((row_count, H, local_len), BF16),
            pltpu.SemaphoreType.DMA((count + 1,)),
        ],
        flops=4 * row_count * H * HD * local_len,
        moved=4 * cache_keys.size + 2 * weight.size,
    )


def project_rows(kept, landed, weight, span_code, steps):
    slot_rows, depth = kept.shape
    width = weight.shape[1]
    rows_here = slot_rows // len(steps)
    heads_here = H // len(steps)
    span_width = span_code.shape[1] - HD
    share_width = width + span_width + HD
    step_width = 256

    def kernel(kept_ref, landed_ref, weight_ref, span_ref, own_ref, *refs):
        share_refs, (held, code) = refs[:-2], refs[-2:]
        far = lax.axis_index("section") >= 2
        rank = lax.axis_index("tensor")
        rows = jnp.where(far, landed_ref[...], kept_ref[...])
        lane = lax.broadcasted_iota(jnp.int32, (slot_rows, HD), 1)
        levels = jnp.zeros((slot_rows, HD), F32)
        for c in range(0, width, step_width):
            product = jnp.dot(rows, weight_ref[:, c : c + step_width], preferred_element_type=F32)
            held[:, c : c + step_width] = product
            for m in range(0, step_width, HD):
                tile = product[:, m : m + HD]
                level = level_of(jnp.max(jnp.abs(tile), axis=1, keepdims=True))
                levels = jnp.where(lane == LEVELS + (c + m) // HD, level, levels)
                scaled = tile * (TOP * jnp.exp(level * (-LN2 / OCTAVE)))
                code[:, c + m : c + m + HD] = as_int16(scaled)
        code[:, width:] = as_int16(levels)

        def rows_of(step):
            return pl.ds(pl.multiple_of((rank ^ step) * rows_here, rows_here), rows_here)

        own_ref[...] = held[rows_of(0), :]
        for k, step in enumerate(steps[1:]):
            heads = pl.ds(pl.multiple_of((rank ^ step) * heads_here, heads_here), heads_here)
            share_refs[k][:, pl.ds(0, width)] = code[rows_of(step), pl.ds(0, width)]
            share_refs[k][:, pl.ds(width, span_width)] = span_ref[heads, pl.ds(0, span_width)]
            stats = as_float(span_ref[heads, pl.ds(span_width, HD)])
            both = jnp.where(lane[:rows_here] < LEVELS, stats, as_float(code[rows_of(step), pl.ds(width, HD)]))
            share_refs[k][:, pl.ds(width + span_width, HD)] = as_int16(both)

    return on_chip(
        kernel,
        (kept, landed, weight, span_code),
        [VMEM] * 4,
        [jax.ShapeDtypeStruct((rows_here, width), F32)]
        + [jax.ShapeDtypeStruct((rows_here, share_width), I16)] * (len(steps) - 1),
        [pltpu.VMEM((slot_rows, width), F32), pltpu.VMEM((slot_rows, width + HD), I16)],
        flops=2 * slot_rows * depth * width,
        moved=2 * weight.size,
    )


def finish_rows(own, shares, cosine, sine):
    rows, width = own.shape
    share_count = len(shares)
    share_width = shares[0].shape[1]

    def kernel(own_ref, *refs):
        share_refs = refs[:share_count]
        cosine_ref, sine_ref, out_ref = refs[share_count:]
        scales = [
            jnp.exp(as_float(ref[:, pl.ds(share_width - HD, HD)]) * (LN2 / OCTAVE)) * (1.0 / TOP)
            for ref in share_refs
        ]
        for n in range(width // HD):
            columns = pl.ds(n * HD, HD)
            total = own_ref[:, columns]
            for ref, scale in zip(share_refs, scales):
                total = total + as_float(ref[:, columns]) * scale[:, LEVELS + n : LEVELS + n + 1]
            if n < KVH:
                mean = jnp.sum(total * total, axis=1, keepdims=True) * (1.0 / HD)
                total = total * cosine_ref[...] + pltpu.roll(total, HD // 2, 1) * sine_ref[...]
                total = total * lax.rsqrt(mean + NORM_EPSILON)
            out_ref[:, columns] = total.astype(BF16)

    return on_chip(
        kernel,
        (own, *shares, cosine, sine),
        [VMEM] * (share_count + 3),
        [jax.ShapeDtypeStruct((rows, width), BF16)],
    )[0]


def merge_spans(span, shares, queries, new_keys, new_values, begin):
    row_count = new_keys.shape[0]
    share_count = len(shares)
    heads_here = shares[0].shape[0]
    keys_here = heads_here // G
    width = row_count * HD

    def kernel(span_ref, *refs):
        share_refs = refs[:share_count]
        query_ref, key_ref, value_ref, out_ref = refs[share_count:]
        rank = lax.axis_index("tensor")
        heads = pl.ds(pl.multiple_of(rank * heads_here, heads_here), heads_here)
        columns = pl.ds(pl.multiple_of(rank * keys_here * HD, HD), keys_here * HD)
        new_key, new_value = key_ref[:, columns].astype(F32), value_ref[:, columns].astype(F32)

        def spread(tile, r):
            return jnp.concatenate(
                [
                    jnp.broadcast_to(tile[r : r + 1, kk * HD : (kk + 1) * HD], (G, HD))
                    for kk in range(keys_here)
                ],
                axis=0,
            )

        stats, scales = [span_ref[heads, pl.ds(width, HD)]], []
        for ref in share_refs:
            code = as_float(ref[:, pl.ds(begin + width, HD)])
            column = lax.broadcasted_iota(jnp.int32, code.shape, 1)
            fine = code + pltpu.roll(code, HD - 2 * row_count, 1) * (1.0 / TOP)
            stats.append(jnp.where(column < row_count, fine, fine * (1.0 / HD)))
            scales.append(jnp.exp(code * (LN2 / OCTAVE)) * (1.0 / TOP))

        def part(k, r):
            if k == 0:
                return span_ref[heads, pl.ds(r * HD, HD)]
            coded = as_float(share_refs[k - 1][:, pl.ds(begin + r * HD, HD)])
            return coded * scales[k - 1][:, 4 * row_count + r : 4 * row_count + r + 1]

        for r in range(row_count):
            query = query_ref[pl.ds(pl.multiple_of(r * H + rank * heads_here, heads_here), heads_here), :]
            self_score = jnp.sum(query * spread(new_key, r), axis=1, keepdims=True) * HD ** (-0.5)
            row_peak = self_score
            for tile in stats:
                row_peak = jnp.maximum(row_peak, tile[:, r : r + 1])
            self_weight = jnp.exp(self_score - row_peak)
            numerator = self_weight * spread(new_value, r)
            denominator = self_weight
            for k, tile in enumerate(stats):
                factor = jnp.exp(tile[:, r : r + 1] - row_peak)
                numerator += factor * part(k, r)
                denominator += factor * tile[:, row_count + r : row_count + r + 1]
            out_ref[r] = (numerator / denominator).astype(BF16)

    attended = on_chip(
        kernel,
        (span, *shares, queries, new_keys, new_values),
        [VMEM] * (share_count + 4),
        [jax.ShapeDtypeStruct((row_count, heads_here, HD), BF16)],
    )[0]
    return attended.reshape(row_count, heads_here * HD)


def join_rows(pieces, steps):
    count = len(pieces)
    rows, width = pieces[0].shape

    def kernel(*refs):
        piece_refs, out_hbm, sems = refs[:count], refs[count], refs[count + 1]
        rank = lax.axis_index("tensor")
        copies = []
        for step in range(count):
            place = pl.ds(pl.multiple_of(lax.rem(rank + count - steps[step], count) * rows, rows), rows)
            copies.append(pltpu.make_async_copy(piece_refs[step], out_hbm.at[place], sems.at[step]))
        for copy in copies:
            copy.start()
        for copy in copies:
            copy.wait()

    return on_chip(
        kernel,
        pieces,
        [VMEM] * count,
        [jax.ShapeDtypeStruct((count * rows, width), BF16)],
        [pltpu.SemaphoreType.DMA((count,))],
        out_specs=[HBM],
    )[0]


def swap(piece, axis, step):
    return lax.ppermute(piece, axis, [(i, i ^ step) for i in range(lax.axis_size(axis))])


def turn(piece, axis, step):
    count = lax.axis_size(axis)
    return lax.ppermute(piece, axis, [(i, (i + step) % count) for i in range(count)])


def local(
    prompt,
    key_value_weight,
    key_gain,
    prompt_blocks,
    block_owner,
    block_slot,
    queries,
    cache_keys,
    cache_values,
    new_keys,
    new_values,
    decode_lengths,
):
    tensor_count = lax.axis_size("tensor")
    near_states = swap(prompt[0], "section", 1)
    cosine, sine, states, table = prepare(prompt[0], key_gain, block_owner, block_slot, prompt_blocks)
    kept, sent = place_rows(states, near_states, table)
    landed = swap(sent, "section", 3)
    span, span_code, row_queries, weight = attend_span(
        queries, cache_keys, cache_values, decode_lengths, key_value_weight, kept
    )
    steps = (0,) + tuple(range(tensor_count - 1, 0, -1))
    own, *shares = project_rows(kept, landed, weight, span_code, steps)
    shares = [swap(share, "tensor", step) for share, step in zip(shares, steps[1:])]
    finished = finish_rows(own, shares, cosine, sine)
    pieces = [finished] + [turn(finished, "tensor", step) for step in steps[1:]]
    block_pool = join_rows(pieces, steps)
    attended = merge_spans(span, shares, row_queries, new_keys, new_values, key_value_weight.shape[1])
    return (attended, block_pool.reshape(1, CAP, BLK, -1))


def solution(mesh):
    in_specs = (
        P(("parts", "section"), None, "tensor"),
        P("tensor", None),
        P(),
        P("parts"),
        P("parts"),
        P("parts"),
        P(("parts", "section"), None),
        P(("parts", "section"), "tensor", None),
        P(("parts", "section"), "tensor", None),
        P(("parts", "section"), None),
        P(("parts", "section"), None),
        P(("parts", "section")),
    )
    out_specs = (P(("parts", "section"), "tensor"), P(("parts", "section"), None, None, None))
    tensor_count = mesh.shape["tensor"]
    whole_tiles = tensor_count == 4 and mesh.shape["section"] == 4
    program = local if whole_tiles else local_small_shares
    return jax.shard_map(program, mesh=mesh, in_specs=in_specs, out_specs=out_specs, check_vma=False)
```

```python
import math

import jax
import jax.numpy as jnp
from jax import lax
from jax.experimental import pallas as pl
from jax.experimental.pallas import tpu as pltpu
from jax.sharding import PartitionSpec as P

H = 64
KVH = 8
HD = 128
BLK = 16
SPAN = 128
KVW = 1024
G = 8
NB = 16
CAP = 4


NORM_EPSILON = 1e-06
ROPE_BASE = 1000000.0
MASKED_SCORE = -1e30


def exchange(pieces, axis):
    count = lax.axis_size(axis)
    rank = lax.axis_index(axis)
    landed = [lax.dynamic_index_in_dim(pieces, rank, 0, keepdims=False)]
    for step in range(1, count):
        piece = lax.dynamic_index_in_dim(pieces, rank ^ step, 0, keepdims=False)
        landed.append(lax.ppermute(piece, axis, [(i, i ^ step) for i in range(count)]))
    return landed


def collected(own, axis):
    count = lax.axis_size(axis)
    rank = lax.axis_index(axis)
    landed = [own]
    for step in range(1, count):
        landed.append(lax.ppermute(own, axis, [(i, i ^ step) for i in range(count)]))
    stacked = jnp.zeros((count,) + own.shape, own.dtype)
    for step, piece in enumerate(landed):
        stacked = lax.dynamic_update_index_in_dim(stacked, piece, rank ^ step, 0)
    return stacked


def rows_for_groups(states, block_owner, block_slot, group_count):
    slot_ids = jnp.arange(group_count * CAP, dtype=jnp.int32)
    selector = (block_owner * CAP + block_slot)[None, :] == slot_ids[:, None]
    filled = jnp.any(selector, axis=1)
    source = jnp.argmax(selector, axis=1)
    blocks = states.reshape(NB, BLK, states.shape[1])
    chosen = jnp.where(filled[:, None, None], blocks[source], jnp.zeros((), states.dtype))
    return chosen.reshape(group_count, CAP * BLK, states.shape[1])


def spread(rows, axis):
    count = lax.axis_size(axis)
    landed = jnp.where(lax.axis_index(axis) == 0, rows[0], jnp.zeros_like(rows[0]))
    for k in range(1, count):
        landed = landed + lax.ppermute(rows[k], axis, [(0, k)])
    return landed


def slot_positions(prompt_blocks, block_owner, block_slot, group_index):
    prompt_ends = jnp.cumsum(prompt_blocks)
    prompt_starts = prompt_ends - prompt_blocks
    slot_ids = jnp.arange(CAP, dtype=jnp.int32)
    selector = (block_owner[None, :] == group_index) & (block_slot[None, :] == slot_ids[:, None])
    block = jnp.sum(jnp.where(selector, jnp.arange(NB, dtype=jnp.int32)[None, :], 0), axis=1)
    inside = (block[:, None] >= prompt_starts[None, :]) & (block[:, None] < prompt_ends[None, :])
    first = jnp.sum(jnp.where(inside, prompt_starts[None, :], 0), axis=1)
    return (((block - first) * BLK)[:, None] + jnp.arange(BLK, dtype=jnp.int32)[None, :]).reshape(-1)


def finish_keys(projected, positions, key_gain):
    token_count = projected.shape[0]
    key_heads = projected[:, :KVW].reshape(token_count, KVH, HD)
    inv_root = lax.rsqrt(jnp.mean(key_heads * key_heads, axis=-1, keepdims=True) + NORM_EPSILON)
    key_heads = key_heads * inv_root * key_gain
    half_dim = HD // 2
    frequency = ROPE_BASE ** (jnp.arange(half_dim, dtype=jnp.float32) * (-2.0 / HD))
    angles = positions.astype(jnp.float32)[:, None, None] * frequency[None, None, :]
    cosine = jnp.cos(angles)
    sine_part = jnp.sin(angles)
    lower_half = key_heads[..., :half_dim]
    upper_half = key_heads[..., half_dim:]
    rotated = jnp.concatenate(
        [
            lower_half * cosine - upper_half * sine_part,
            upper_half * cosine + lower_half * sine_part,
        ],
        axis=-1,
    )
    return jnp.concatenate([rotated.reshape(token_count, KVW), projected[:, KVW:]], axis=1).astype(
        jnp.bfloat16
    )


def partial_attention(queries, cache_keys, cache_values, decode_lengths, first_position):
    row_count = queries.shape[0]
    local_len = cache_keys.shape[1]
    span_count = local_len // SPAN
    query_heads = queries.reshape(row_count, KVH, G, HD)
    key_heads = cache_keys.reshape(row_count, local_len, KVH, HD)
    scores = jnp.einsum(
        "rkgd,rpkd->rkgp", query_heads, key_heads, preferred_element_type=jnp.float32
    ) * HD ** (-0.5)
    live_mask = (first_position + jnp.arange(local_len, dtype=jnp.int32))[None, :] < decode_lengths[
        :, None
    ]
    scores = jnp.where(live_mask[:, None, None, :], scores, MASKED_SCORE)
    spans = scores.reshape(row_count, KVH, G, span_count, SPAN)
    span_max = jnp.max(spans, axis=-1)
    live_spans = live_mask.reshape(row_count, 1, 1, span_count, SPAN)
    weights = jnp.where(live_spans, jnp.exp(spans - span_max[..., None]), 0.0)
    span_sum = jnp.sum(weights, axis=-1)
    value_spans = cache_values.reshape(row_count, span_count, SPAN, KVH, HD)
    span_out = jnp.einsum(
        "rkgns,rnskd->rkgnd",
        weights.astype(jnp.bfloat16),
        value_spans,
        preferred_element_type=jnp.float32,
    )
    row_peak = jnp.max(span_max, axis=-1)
    factor = jnp.exp(span_max - row_peak[..., None])
    partial_out = jnp.sum(span_out * factor[..., None], axis=3)
    partial_sum = jnp.sum(span_sum * factor, axis=-1)
    return (
        partial_out.reshape(row_count, H, HD),
        row_peak.reshape(row_count, H),
        partial_sum.reshape(row_count, H),
    )


def combine_partials(former, latter):
    former_out, former_peak, former_sum = former
    latter_out, latter_peak, latter_sum = latter
    highest = jnp.maximum(former_peak, latter_peak)
    former_factor = jnp.exp(former_peak - highest)
    latter_factor = jnp.exp(latter_peak - highest)
    merged_out = former_out * former_factor[..., None] + latter_out * latter_factor[..., None]
    return (merged_out, highest, former_sum * former_factor + latter_sum * latter_factor)


def finish_heads(
    own_out, own_peak, own_sum, queries, new_keys, new_values, tensor_rank, heads_here
):
    row_count = queries.shape[0]
    own_width = heads_here * HD
    own_queries = (
        lax.dynamic_slice_in_dim(queries, tensor_rank * own_width, own_width, 1)
        .reshape(row_count, heads_here, HD)
        .astype(jnp.float32)
    )
    head_ids = tensor_rank * heads_here + jnp.arange(heads_here, dtype=jnp.int32)
    selector = (head_ids[:, None] // G == jnp.arange(KVH, dtype=jnp.int32)[None, :]).astype(
        jnp.float32
    )
    own_keys = jnp.einsum(
        "jk,rkd->rjd",
        selector,
        new_keys.reshape(row_count, KVH, HD).astype(jnp.float32),
        precision=lax.Precision.HIGHEST,
    )
    own_values = jnp.einsum(
        "jk,rkd->rjd",
        selector,
        new_values.reshape(row_count, KVH, HD).astype(jnp.float32),
        precision=lax.Precision.HIGHEST,
    )
    self_score = jnp.sum(own_queries * own_keys, axis=-1) * HD ** (-0.5)
    row_peak = jnp.maximum(own_peak, self_score)
    factor = jnp.exp(own_peak - row_peak)
    self_weight = jnp.exp(self_score - row_peak)
    numerator = own_out * factor[..., None] + self_weight[..., None] * own_values
    denominator = own_sum * factor + self_weight
    return (numerator / denominator[..., None]).reshape(row_count, own_width).astype(jnp.bfloat16)


def local_small_shares(
    prompt,
    key_value_weight,
    key_gain,
    prompt_blocks,
    block_owner,
    block_slot,
    queries,
    cache_keys,
    cache_values,
    new_keys,
    new_values,
    decode_lengths,
):
    tensor_count = lax.axis_size("tensor")
    tensor_rank = lax.axis_index("tensor")
    group_index = lax.axis_index("section")
    group_count = lax.axis_size("section")
    slot_rows = CAP * BLK
    rows_here = slot_rows // tensor_count
    rows = rows_for_groups(prompt[0], block_owner, block_slot, group_count)
    own_rows = spread(rows, "section")
    local_len = cache_keys.shape[1]
    row_count = queries.shape[0]
    heads_here = H // tensor_count
    partial_out, partial_peak, partial_sum = partial_attention(
        queries, cache_keys, cache_values, decode_lengths, tensor_rank * local_len
    )
    stats = jnp.stack([partial_peak, partial_sum], axis=-1).reshape(row_count, tensor_count, heads_here, 2)
    outs = partial_out.reshape(row_count, tensor_count, heads_here, HD)
    packed = jnp.concatenate([outs, jnp.pad(stats, ((0, 0), (0, 0), (0, 0), (0, HD - 2)))], axis=-1)
    shares = exchange(packed.transpose(1, 0, 2, 3), "tensor")
    merged = (shares[0][..., :HD], shares[0][..., HD], shares[0][..., HD + 1])
    for share in shares[1:]:
        merged = combine_partials(merged, (share[..., :HD], share[..., HD], share[..., HD + 1]))
    own_out, own_peak, own_sum = merged
    partial_terms = jnp.dot(own_rows, key_value_weight, preferred_element_type=jnp.float32)
    terms = exchange(partial_terms.reshape(tensor_count, rows_here, -1), "tensor")
    summed = sum(terms[1:], terms[0])
    positions = lax.dynamic_slice_in_dim(
        slot_positions(prompt_blocks, block_owner, block_slot, group_index), tensor_rank * rows_here, rows_here, 0
    )
    prompt_kv = finish_keys(summed, positions, key_gain)
    block_pool = collected(prompt_kv, "tensor").reshape(1, CAP, BLK, -1)
    attended = finish_heads(
        own_out, own_peak, own_sum, queries, new_keys, new_values, tensor_rank, heads_here
    )
    return (attended, block_pool)


VMEM = pl.BlockSpec(memory_space=pltpu.VMEM)
HBM = pl.BlockSpec(memory_space=pltpu.HBM)
F32 = jnp.float32
BF16 = jnp.bfloat16
I16 = jnp.int16
TOP = 32000.0
OCTAVE = 256.0
LN2 = math.log(2.0)
TINY = 1e-30
LEVELS = 64


def on_chip(kernel, operands, in_specs, out_shapes, scratch=(), out_specs=None, flops=0, moved=0):
    return pl.pallas_call(
        kernel,
        out_shape=out_shapes,
        in_specs=in_specs,
        out_specs=out_specs or [VMEM] * len(out_shapes),
        scratch_shapes=list(scratch),
        compiler_params=pltpu.CompilerParams(vmem_limit_bytes=40 * 1024 * 1024),
        cost_estimate=pl.CostEstimate(flops=flops, bytes_accessed=moved, transcendentals=0),
    )(*operands)


def stays(array):
    return pltpu.with_memory_space_constraint(array, pltpu.HBM)


def level_of(peak):
    return jnp.ceil(jnp.log(jnp.maximum(peak, TINY)) * (OCTAVE / LN2))


def as_int16(value):
    return jnp.round(value).astype(jnp.int32).astype(I16)


def as_float(value):
    return value.astype(jnp.int32).astype(F32)


def prepare(states, key_gain, block_owner, block_slot, prompt_blocks):
    token_count = states.shape[0]
    rows_here = CAP * BLK // lax.axis_size("tensor")
    slots_here = rows_here // BLK
    prompt_count = prompt_blocks.shape[0]
    fetched = [block_owner, block_slot, prompt_blocks, key_gain[None, :]]
    count = len(fetched)

    def kernel(*refs):
        sources, states_hbm = refs[:count], refs[count]
        cosine_ref, sine_ref, states_ref, table_ref = refs[count + 1 : count + 5]
        held, (source, sems) = refs[count + 5 : 2 * count + 5], refs[2 * count + 5 :]
        owner, slot, prompts, gain = held
        copies = [pltpu.make_async_copy(s, d, sems.at[i]) for i, (s, d) in enumerate(zip(sources, held))]
        copies.append(pltpu.make_async_copy(states_hbm, states_ref, sems.at[count]))
        for copy in copies:
            copy.start()
        group = lax.axis_index("section")
        rank = lax.axis_index("tensor")
        core = lax.rem(group, 2)
        for copy in copies[:count]:
            copy.wait()

        for j in range(2 * CAP):
            source[j] = -1
        for b in range(NB):

            @pl.when(owner[b] == core)
            def _():
                source[slot[b]] = b

            @pl.when(owner[b] == 3 - core)
            def _():
                source[CAP + slot[b]] = b

        token = lax.broadcasted_iota(jnp.int32, (BLK, token_count), 1)
        inner = lax.broadcasted_iota(jnp.int32, (BLK, token_count), 0)
        for j in range(2 * CAP):
            chosen = token == source[j] * BLK + inner
            table_ref[pl.ds(j * BLK, BLK), :] = jnp.where(chosen, 1.0, 0.0).astype(BF16)

        lane = lax.broadcasted_iota(jnp.int32, (BLK, HD), 1)
        row = lax.broadcasted_iota(jnp.int32, (BLK, HD), 0)
        half = lax.rem(lane, HD // 2).astype(F32)
        frequency = jnp.exp(half * (-2.0 / HD * math.log(ROPE_BASE)))
        far_gain = pltpu.roll(jnp.broadcast_to(gain[...], (8, HD)), HD // 2, 1)[0:1]
        for s in range(slots_here):
            block = 0
            for b in range(NB):
                block = jnp.where((owner[b] == group) & (slot[b] == rank * slots_here + s), b, block)
            first, begin = 0, 0
            for j in range(prompt_count):
                first = jnp.where(block >= begin, begin, first)
                begin = begin + prompts[j]
            angles = ((block - first) * BLK + row).astype(F32) * frequency
            cosine_ref[pl.ds(s * BLK, BLK), :] = jnp.cos(angles) * gain[...]
            sine = jnp.sin(angles) * far_gain
            sine_ref[pl.ds(s * BLK, BLK), :] = jnp.where(lane < HD // 2, -sine, sine)
        copies[count].wait()

    return on_chip(
        kernel,
        [stays(array) for array in (*fetched, states)],
        [HBM] * (count + 1),
        [
            jax.ShapeDtypeStruct((rows_here, HD), F32),
            jax.ShapeDtypeStruct((rows_here, HD), F32),
            jax.ShapeDtypeStruct(states.shape, BF16),
            jax.ShapeDtypeStruct((2 * CAP * BLK, token_count), BF16),
        ],
        [pltpu.SMEM(array.shape, jnp.int32) for array in fetched[:3]]
        + [
            pltpu.VMEM((1, HD), F32),
            pltpu.SMEM((2 * CAP,), jnp.int32),
            pltpu.SemaphoreType.DMA((count + 1,)),
        ],
        moved=2 * states.size,
    )


def place_rows(own_states, near_states, table):
    width = own_states.shape[1]
    rows = CAP * BLK

    def kernel(own_ref, near_ref, table_ref, keep_ref, send_ref):
        core = lax.rem(lax.axis_index("section"), 2)

        def place(states):
            placed = jnp.dot(table_ref[...], states[...], preferred_element_type=F32).astype(BF16)
            keep_ref[...] = placed[:rows]
            send_ref[...] = placed[rows:]

        @pl.when(core == 0)
        def _():
            place(own_ref)

        @pl.when(core == 1)
        def _():
            place(near_ref)

    return on_chip(
        kernel,
        (own_states, near_states, table),
        [VMEM] * 3,
        [jax.ShapeDtypeStruct((rows, width), BF16)] * 2,
        moved=own_states.size * 2,
    )


def attend_span(queries, cache_keys, cache_values, decode_lengths, weight, after):
    row_count, local_len = cache_keys.shape[0], cache_keys.shape[1]
    width = row_count * HD
    fetched = [decode_lengths, queries, cache_keys, cache_values]
    count = len(fetched)

    def kernel(*refs):
        sources, weight_hbm = refs[:count], refs[count]
        span_ref, code_ref, query_ref, weight_ref = refs[count + 2 : count + 6]
        held, (scores, weights, sems) = refs[count + 6 : 2 * count + 6], refs[2 * count + 6 :]
        length, packed, keys, values = held
        copies = [pltpu.make_async_copy(s, d, sems.at[i]) for i, (s, d) in enumerate(zip(sources, held))]
        copies.append(pltpu.make_async_copy(weight_hbm, weight_ref, sems.at[count]))
        for copy in copies:
            copy.start()
        rank = lax.axis_index("tensor")
        copies[0].wait()
        copies[1].wait()
        for h in range(H):
            piece = packed[:, pl.ds(h * HD, HD)].astype(F32)
            query_ref[pl.ds(h, row_count, stride=H), :] = piece
        copies[2].wait()
        for r in range(row_count):
            for pair in range(KVH // 2):
                pair_queries = query_ref[pl.ds(r * H + pair * 2 * G, 2 * G), :].astype(BF16)
                for n in (2 * pair, 2 * pair + 1):
                    both = lax.dot_general(
                        pair_queries,
                        keys[r, :, n * HD : (n + 1) * HD],
                        (((1,), (1,)), ((), ())),
                        preferred_element_type=F32,
                    )
                    scores[r, pl.ds(n * G, G), :] = both[(n % 2) * G : (n % 2 + 1) * G]
        place = lax.broadcasted_iota(jnp.int32, (H, local_len), 1) + rank * local_len
        column = lax.broadcasted_iota(jnp.int32, (H, HD), 1)
        stats = jnp.zeros((H, HD), F32)
        for r in range(row_count):
            live = place < length[r]
            row_scores = jnp.where(live, scores[r] * HD ** (-0.5), MASKED_SCORE)
            peak = jnp.max(row_scores, axis=1, keepdims=True)
            weight = jnp.where(live, jnp.exp(row_scores - peak), 0.0)
            total = jnp.sum(weight, axis=1, keepdims=True)
            weights[r] = weight.astype(BF16)
            stats = jnp.where(column == r, peak, stats)
            stats = jnp.where(column == row_count + r, total, stats)
        span_ref[:, pl.ds(width, HD)] = stats
        copies[3].wait()
        levels = jnp.zeros((H, HD), F32)
        for r in range(row_count):
            for pair in range(KVH // 2):
                pair_weights = weights[r, pl.ds(pair * 2 * G, 2 * G), :]
                for n in (2 * pair, 2 * pair + 1):
                    both = jnp.dot(
                        pair_weights, values[r, :, n * HD : (n + 1) * HD], preferred_element_type=F32
                    )
                    span_ref[pl.ds(n * G, G), pl.ds(r * HD, HD)] = both[(n % 2) * G : (n % 2 + 1) * G]
        for r in range(row_count):
            peak = jnp.max(jnp.abs(span_ref[:, pl.ds(r * HD, HD)]), axis=1, keepdims=True)
            levels = jnp.where(column == r, peak, levels)
        levels = level_of(levels)
        scale = TOP * jnp.exp(levels * (-LN2 / OCTAVE))
        for r in range(row_count):
            out = span_ref[:, pl.ds(r * HD, HD)]
            code_ref[:, pl.ds(r * HD, HD)] = as_int16(out * scale[:, r : r + 1])
        peaks = jnp.maximum(stats, -TOP)
        fine = jnp.where(column < row_count, peaks, stats * HD)
        whole = jnp.floor(fine)
        part = (fine - whole) * TOP
        coded = jnp.where(column < 2 * row_count, whole, 0.0)
        shifted = pltpu.roll(jnp.where(column < 2 * row_count, part, 0.0), 2 * row_count, 1)
        moved = pltpu.roll(jnp.where(column < row_count, levels, 0.0), 4 * row_count, 1)
        code_ref[:, pl.ds(width, HD)] = as_int16(coded + shifted + moved)
        copies[count].wait()

    return on_chip(
        kernel,
        [stays(array) for array in (*fetched, weight)] + [after],
        [HBM] * (count + 1) + [pl.BlockSpec(memory_space=pl.ANY)],
        [
            jax.ShapeDtypeStruct((H, width + HD), F32),
            jax.ShapeDtypeStruct((H, width + HD), I16),
            jax.ShapeDtypeStruct((row_count * H, HD), F32),
            jax.ShapeDtypeStruct(weight.shape, BF16),
        ],
        [pltpu.SMEM((row_count,), jnp.int32)]
        + [pltpu.VMEM(array.shape, array.dtype) for array in fetched[1:]]
        + [
            pltpu.VMEM((row_count, H, local_len), F32),
            pltpu.VMEM((row_count, H, local_len), BF16),
            pltpu.SemaphoreType.DMA((count + 1,)),
        ],
        flops=4 * row_count * H * HD * local_len,
        moved=4 * cache_keys.size + 2 * weight.size,
    )


def project_rows(kept, landed, weight, span_code, steps):
    slot_rows, depth = kept.shape
    width = weight.shape[1]
    rows_here = slot_rows // len(steps)
    heads_here = H // len(steps)
    span_width = span_code.shape[1] - HD
    share_width = width + span_width + HD
    step_width = 256

    def kernel(kept_ref, landed_ref, weight_ref, span_ref, own_ref, *refs):
        share_refs, (held, code) = refs[:-2], refs[-2:]
        far = lax.axis_index("section") >= 2
        rank = lax.axis_index("tensor")
        rows = jnp.where(far, landed_ref[...], kept_ref[...])
        lane = lax.broadcasted_iota(jnp.int32, (slot_rows, HD), 1)
        levels = jnp.zeros((slot_rows, HD), F32)
        for c in range(0, width, step_width):
            product = jnp.dot(rows, weight_ref[:, c : c + step_width], preferred_element_type=F32)
            held[:, c : c + step_width] = product
            for m in range(0, step_width, HD):
                tile = product[:, m : m + HD]
                level = level_of(jnp.max(jnp.abs(tile), axis=1, keepdims=True))
                levels = jnp.where(lane == LEVELS + (c + m) // HD, level, levels)
                scaled = tile * (TOP * jnp.exp(level * (-LN2 / OCTAVE)))
                code[:, c + m : c + m + HD] = as_int16(scaled)
        code[:, width:] = as_int16(levels)

        def rows_of(step):
            return pl.ds(pl.multiple_of((rank ^ step) * rows_here, rows_here), rows_here)

        own_ref[...] = held[rows_of(0), :]
        for k, step in enumerate(steps[1:]):
            heads = pl.ds(pl.multiple_of((rank ^ step) * heads_here, heads_here), heads_here)
            share_refs[k][:, pl.ds(0, width)] = code[rows_of(step), pl.ds(0, width)]
            share_refs[k][:, pl.ds(width, span_width)] = span_ref[heads, pl.ds(0, span_width)]
            stats = as_float(span_ref[heads, pl.ds(span_width, HD)])
            both = jnp.where(lane[:rows_here] < LEVELS, stats, as_float(code[rows_of(step), pl.ds(width, HD)]))
            share_refs[k][:, pl.ds(width + span_width, HD)] = as_int16(both)

    return on_chip(
        kernel,
        (kept, landed, weight, span_code),
        [VMEM] * 4,
        [jax.ShapeDtypeStruct((rows_here, width), F32)]
        + [jax.ShapeDtypeStruct((rows_here, share_width), I16)] * (len(steps) - 1),
        [pltpu.VMEM((slot_rows, width), F32), pltpu.VMEM((slot_rows, width + HD), I16)],
        flops=2 * slot_rows * depth * width,
        moved=2 * weight.size,
    )


def add_shares(total, shares):
    rows, width = total.shape
    count = len(shares)
    share_width = shares[0].shape[1]

    def kernel(total_ref, *refs):
        share_refs, out_ref = refs[:count], refs[count]
        scales = [
            jnp.exp(as_float(ref[:, pl.ds(share_width - HD, HD)]) * (LN2 / OCTAVE)) * (1.0 / TOP)
            for ref in share_refs
        ]
        for n in range(width // HD):
            columns = pl.ds(n * HD, HD)
            part = total_ref[:, columns]
            for ref, scale in zip(share_refs, scales):
                part = part + as_float(ref[:, columns]) * scale[:, LEVELS + n : LEVELS + n + 1]
            out_ref[:, columns] = part

    return on_chip(
        kernel, (total, *shares), [VMEM] * (count + 1), [jax.ShapeDtypeStruct((rows, width), F32)]
    )[0]


def finish_rows(own, shares, cosine, sine):
    rows, width = own.shape
    share_count = len(shares)
    share_width = shares[0].shape[1]

    def kernel(own_ref, *refs):
        share_refs = refs[:share_count]
        cosine_ref, sine_ref, out_ref = refs[share_count:]
        scales = [
            jnp.exp(as_float(ref[:, pl.ds(share_width - HD, HD)]) * (LN2 / OCTAVE)) * (1.0 / TOP)
            for ref in share_refs
        ]
        for n in range(width // HD):
            columns = pl.ds(n * HD, HD)
            total = own_ref[:, columns]
            for ref, scale in zip(share_refs, scales):
                total = total + as_float(ref[:, columns]) * scale[:, LEVELS + n : LEVELS + n + 1]
            if n < KVH:
                mean = jnp.sum(total * total, axis=1, keepdims=True) * (1.0 / HD)
                total = total * cosine_ref[...] + pltpu.roll(total, HD // 2, 1) * sine_ref[...]
                total = total * lax.rsqrt(mean + NORM_EPSILON)
            out_ref[:, columns] = total.astype(BF16)

    return on_chip(
        kernel,
        (own, *shares, cosine, sine),
        [VMEM] * (share_count + 3),
        [jax.ShapeDtypeStruct((rows, width), BF16)],
    )[0]


def merge_spans(span, shares, queries, new_keys, new_values, begin):
    row_count = new_keys.shape[0]
    share_count = len(shares)
    heads_here = shares[0].shape[0]
    keys_here = heads_here // G
    width = row_count * HD

    def kernel(span_ref, *refs):
        share_refs = refs[:share_count]
        query_ref, key_ref, value_ref, out_ref = refs[share_count:]
        rank = lax.axis_index("tensor")
        heads = pl.ds(pl.multiple_of(rank * heads_here, heads_here), heads_here)
        columns = pl.ds(pl.multiple_of(rank * keys_here * HD, HD), keys_here * HD)
        new_key, new_value = key_ref[:, columns].astype(F32), value_ref[:, columns].astype(F32)

        def spread(tile, r):
            return jnp.concatenate(
                [
                    jnp.broadcast_to(tile[r : r + 1, kk * HD : (kk + 1) * HD], (G, HD))
                    for kk in range(keys_here)
                ],
                axis=0,
            )

        stats, scales = [span_ref[heads, pl.ds(width, HD)]], []
        for ref in share_refs:
            code = as_float(ref[:, pl.ds(begin + width, HD)])
            column = lax.broadcasted_iota(jnp.int32, code.shape, 1)
            fine = code + pltpu.roll(code, HD - 2 * row_count, 1) * (1.0 / TOP)
            stats.append(jnp.where(column < row_count, fine, fine * (1.0 / HD)))
            scales.append(jnp.exp(code * (LN2 / OCTAVE)) * (1.0 / TOP))

        def part(k, r):
            if k == 0:
                return span_ref[heads, pl.ds(r * HD, HD)]
            coded = as_float(share_refs[k - 1][:, pl.ds(begin + r * HD, HD)])
            return coded * scales[k - 1][:, 4 * row_count + r : 4 * row_count + r + 1]

        for r in range(row_count):
            query = query_ref[pl.ds(pl.multiple_of(r * H + rank * heads_here, heads_here), heads_here), :]
            self_score = jnp.sum(query * spread(new_key, r), axis=1, keepdims=True) * HD ** (-0.5)
            row_peak = self_score
            for tile in stats:
                row_peak = jnp.maximum(row_peak, tile[:, r : r + 1])
            self_weight = jnp.exp(self_score - row_peak)
            numerator = self_weight * spread(new_value, r)
            denominator = self_weight
            for k, tile in enumerate(stats):
                factor = jnp.exp(tile[:, r : r + 1] - row_peak)
                numerator += factor * part(k, r)
                denominator += factor * tile[:, row_count + r : row_count + r + 1]
            out_ref[r] = (numerator / denominator).astype(BF16)

    attended = on_chip(
        kernel,
        (span, *shares, queries, new_keys, new_values),
        [VMEM] * (share_count + 4),
        [jax.ShapeDtypeStruct((row_count, heads_here, HD), BF16)],
    )[0]
    return attended.reshape(row_count, heads_here * HD)


def join_rows(pieces, steps):
    count = len(pieces)
    rows, width = pieces[0].shape

    def kernel(*refs):
        piece_refs, out_hbm, sems = refs[:count], refs[count], refs[count + 1]
        rank = lax.axis_index("tensor")
        copies = []
        for step in range(count):
            place = pl.ds(pl.multiple_of(lax.rem(rank + count - steps[step], count) * rows, rows), rows)
            copies.append(pltpu.make_async_copy(piece_refs[step], out_hbm.at[place], sems.at[step]))
        for copy in copies:
            copy.start()
        for copy in copies:
            copy.wait()

    return on_chip(
        kernel,
        pieces,
        [VMEM] * count,
        [jax.ShapeDtypeStruct((count * rows, width), BF16)],
        [pltpu.SemaphoreType.DMA((count,))],
        out_specs=[HBM],
    )[0]


def swap(piece, axis, step):
    return lax.ppermute(piece, axis, [(i, i ^ step) for i in range(lax.axis_size(axis))])


def turn(piece, axis, step):
    count = lax.axis_size(axis)
    return lax.ppermute(piece, axis, [(i, (i + step) % count) for i in range(count)])


def local(
    prompt,
    key_value_weight,
    key_gain,
    prompt_blocks,
    block_owner,
    block_slot,
    queries,
    cache_keys,
    cache_values,
    new_keys,
    new_values,
    decode_lengths,
):
    tensor_count = lax.axis_size("tensor")
    near_states = swap(prompt[0], "section", 1)
    cosine, sine, states, table = prepare(prompt[0], key_gain, block_owner, block_slot, prompt_blocks)
    kept, sent = place_rows(states, near_states, table)
    landed = swap(sent, "section", 3)
    span, span_code, row_queries, weight = attend_span(
        queries, cache_keys, cache_values, decode_lengths, key_value_weight, kept
    )
    steps = (0,) + tuple(range(tensor_count - 1, 0, -1))
    own, *shares = project_rows(kept, landed, weight, span_code, steps)
    shares = [swap(share, "tensor", step) for share, step in zip(shares, steps[1:])]
    finished = finish_rows(add_shares(own, [shares[0], shares[2]]), [shares[1]], cosine, sine)
    pieces = [finished] + [turn(finished, "tensor", step) for step in steps[1:]]
    block_pool = join_rows(pieces, steps)
    attended = merge_spans(span, shares, row_queries, new_keys, new_values, key_value_weight.shape[1])
    return (attended, block_pool.reshape(1, CAP, BLK, -1))


def solution(mesh):
    in_specs = (
        P(("parts", "section"), None, "tensor"),
        P("tensor", None),
        P(),
        P("parts"),
        P("parts"),
        P("parts"),
        P(("parts", "section"), None),
        P(("parts", "section"), "tensor", None),
        P(("parts", "section"), "tensor", None),
        P(("parts", "section"), None),
        P(("parts", "section"), None),
        P(("parts", "section")),
    )
    out_specs = (P(("parts", "section"), "tensor"), P(("parts", "section"), None, None, None))
    tensor_count = mesh.shape["tensor"]
    whole_tiles = tensor_count == 4 and mesh.shape["section"] == 4
    program = local if whole_tiles else local_small_shares
    return jax.shard_map(program, mesh=mesh, in_specs=in_specs, out_specs=out_specs, check_vma=False)
```

```python
import math

import jax
import jax.numpy as jnp
from jax import lax
from jax.experimental import pallas as pl
from jax.experimental.pallas import tpu as pltpu
from jax.sharding import PartitionSpec as P

H = 64
KVH = 8
HD = 128
BLK = 16
SPAN = 128
KVW = 1024
G = 8
NB = 16
CAP = 4


NORM_EPSILON = 1e-06
ROPE_BASE = 1000000.0
MASKED_SCORE = -1e30


def exchange(pieces, axis):
    count = lax.axis_size(axis)
    rank = lax.axis_index(axis)
    landed = [lax.dynamic_index_in_dim(pieces, rank, 0, keepdims=False)]
    for step in range(1, count):
        piece = lax.dynamic_index_in_dim(pieces, rank ^ step, 0, keepdims=False)
        landed.append(lax.ppermute(piece, axis, [(i, i ^ step) for i in range(count)]))
    return landed


def collected(own, axis):
    count = lax.axis_size(axis)
    rank = lax.axis_index(axis)
    landed = [own]
    for step in range(1, count):
        landed.append(lax.ppermute(own, axis, [(i, i ^ step) for i in range(count)]))
    stacked = jnp.zeros((count,) + own.shape, own.dtype)
    for step, piece in enumerate(landed):
        stacked = lax.dynamic_update_index_in_dim(stacked, piece, rank ^ step, 0)
    return stacked


def rows_for_groups(states, block_owner, block_slot, group_count):
    slot_ids = jnp.arange(group_count * CAP, dtype=jnp.int32)
    selector = (block_owner * CAP + block_slot)[None, :] == slot_ids[:, None]
    filled = jnp.any(selector, axis=1)
    source = jnp.argmax(selector, axis=1)
    blocks = states.reshape(NB, BLK, states.shape[1])
    chosen = jnp.where(filled[:, None, None], blocks[source], jnp.zeros((), states.dtype))
    return chosen.reshape(group_count, CAP * BLK, states.shape[1])


def spread(rows, axis):
    count = lax.axis_size(axis)
    landed = jnp.where(lax.axis_index(axis) == 0, rows[0], jnp.zeros_like(rows[0]))
    for k in range(1, count):
        landed = landed + lax.ppermute(rows[k], axis, [(0, k)])
    return landed


def slot_positions(prompt_blocks, block_owner, block_slot, group_index):
    prompt_ends = jnp.cumsum(prompt_blocks)
    prompt_starts = prompt_ends - prompt_blocks
    slot_ids = jnp.arange(CAP, dtype=jnp.int32)
    selector = (block_owner[None, :] == group_index) & (block_slot[None, :] == slot_ids[:, None])
    block = jnp.sum(jnp.where(selector, jnp.arange(NB, dtype=jnp.int32)[None, :], 0), axis=1)
    inside = (block[:, None] >= prompt_starts[None, :]) & (block[:, None] < prompt_ends[None, :])
    first = jnp.sum(jnp.where(inside, prompt_starts[None, :], 0), axis=1)
    return (((block - first) * BLK)[:, None] + jnp.arange(BLK, dtype=jnp.int32)[None, :]).reshape(-1)


def finish_keys(projected, positions, key_gain):
    token_count = projected.shape[0]
    key_heads = projected[:, :KVW].reshape(token_count, KVH, HD)
    inv_root = lax.rsqrt(jnp.mean(key_heads * key_heads, axis=-1, keepdims=True) + NORM_EPSILON)
    key_heads = key_heads * inv_root * key_gain
    half_dim = HD // 2
    frequency = ROPE_BASE ** (jnp.arange(half_dim, dtype=jnp.float32) * (-2.0 / HD))
    angles = positions.astype(jnp.float32)[:, None, None] * frequency[None, None, :]
    cosine = jnp.cos(angles)
    sine_part = jnp.sin(angles)
    lower_half = key_heads[..., :half_dim]
    upper_half = key_heads[..., half_dim:]
    rotated = jnp.concatenate(
        [
            lower_half * cosine - upper_half * sine_part,
            upper_half * cosine + lower_half * sine_part,
        ],
        axis=-1,
    )
    return jnp.concatenate([rotated.reshape(token_count, KVW), projected[:, KVW:]], axis=1).astype(
        jnp.bfloat16
    )


def partial_attention(queries, cache_keys, cache_values, decode_lengths, first_position):
    row_count = queries.shape[0]
    local_len = cache_keys.shape[1]
    span_count = local_len // SPAN
    query_heads = queries.reshape(row_count, KVH, G, HD)
    key_heads = cache_keys.reshape(row_count, local_len, KVH, HD)
    scores = jnp.einsum(
        "rkgd,rpkd->rkgp", query_heads, key_heads, preferred_element_type=jnp.float32
    ) * HD ** (-0.5)
    live_mask = (first_position + jnp.arange(local_len, dtype=jnp.int32))[None, :] < decode_lengths[
        :, None
    ]
    scores = jnp.where(live_mask[:, None, None, :], scores, MASKED_SCORE)
    spans = scores.reshape(row_count, KVH, G, span_count, SPAN)
    span_max = jnp.max(spans, axis=-1)
    live_spans = live_mask.reshape(row_count, 1, 1, span_count, SPAN)
    weights = jnp.where(live_spans, jnp.exp(spans - span_max[..., None]), 0.0)
    span_sum = jnp.sum(weights, axis=-1)
    value_spans = cache_values.reshape(row_count, span_count, SPAN, KVH, HD)
    span_out = jnp.einsum(
        "rkgns,rnskd->rkgnd",
        weights.astype(jnp.bfloat16),
        value_spans,
        preferred_element_type=jnp.float32,
    )
    row_peak = jnp.max(span_max, axis=-1)
    factor = jnp.exp(span_max - row_peak[..., None])
    partial_out = jnp.sum(span_out * factor[..., None], axis=3)
    partial_sum = jnp.sum(span_sum * factor, axis=-1)
    return (
        partial_out.reshape(row_count, H, HD),
        row_peak.reshape(row_count, H),
        partial_sum.reshape(row_count, H),
    )


def combine_partials(former, latter):
    former_out, former_peak, former_sum = former
    latter_out, latter_peak, latter_sum = latter
    highest = jnp.maximum(former_peak, latter_peak)
    former_factor = jnp.exp(former_peak - highest)
    latter_factor = jnp.exp(latter_peak - highest)
    merged_out = former_out * former_factor[..., None] + latter_out * latter_factor[..., None]
    return (merged_out, highest, former_sum * former_factor + latter_sum * latter_factor)


def finish_heads(
    own_out, own_peak, own_sum, queries, new_keys, new_values, tensor_rank, heads_here
):
    row_count = queries.shape[0]
    own_width = heads_here * HD
    own_queries = (
        lax.dynamic_slice_in_dim(queries, tensor_rank * own_width, own_width, 1)
        .reshape(row_count, heads_here, HD)
        .astype(jnp.float32)
    )
    head_ids = tensor_rank * heads_here + jnp.arange(heads_here, dtype=jnp.int32)
    selector = (head_ids[:, None] // G == jnp.arange(KVH, dtype=jnp.int32)[None, :]).astype(
        jnp.float32
    )
    own_keys = jnp.einsum(
        "jk,rkd->rjd",
        selector,
        new_keys.reshape(row_count, KVH, HD).astype(jnp.float32),
        precision=lax.Precision.HIGHEST,
    )
    own_values = jnp.einsum(
        "jk,rkd->rjd",
        selector,
        new_values.reshape(row_count, KVH, HD).astype(jnp.float32),
        precision=lax.Precision.HIGHEST,
    )
    self_score = jnp.sum(own_queries * own_keys, axis=-1) * HD ** (-0.5)
    row_peak = jnp.maximum(own_peak, self_score)
    factor = jnp.exp(own_peak - row_peak)
    self_weight = jnp.exp(self_score - row_peak)
    numerator = own_out * factor[..., None] + self_weight[..., None] * own_values
    denominator = own_sum * factor + self_weight
    return (numerator / denominator[..., None]).reshape(row_count, own_width).astype(jnp.bfloat16)


def local_small_shares(
    prompt,
    key_value_weight,
    key_gain,
    prompt_blocks,
    block_owner,
    block_slot,
    queries,
    cache_keys,
    cache_values,
    new_keys,
    new_values,
    decode_lengths,
):
    tensor_count = lax.axis_size("tensor")
    tensor_rank = lax.axis_index("tensor")
    group_index = lax.axis_index("section")
    group_count = lax.axis_size("section")
    slot_rows = CAP * BLK
    rows_here = slot_rows // tensor_count
    rows = rows_for_groups(prompt[0], block_owner, block_slot, group_count)
    own_rows = spread(rows, "section")
    local_len = cache_keys.shape[1]
    row_count = queries.shape[0]
    heads_here = H // tensor_count
    partial_out, partial_peak, partial_sum = partial_attention(
        queries, cache_keys, cache_values, decode_lengths, tensor_rank * local_len
    )
    stats = jnp.stack([partial_peak, partial_sum], axis=-1).reshape(row_count, tensor_count, heads_here, 2)
    outs = partial_out.reshape(row_count, tensor_count, heads_here, HD)
    packed = jnp.concatenate([outs, jnp.pad(stats, ((0, 0), (0, 0), (0, 0), (0, HD - 2)))], axis=-1)
    shares = exchange(packed.transpose(1, 0, 2, 3), "tensor")
    merged = (shares[0][..., :HD], shares[0][..., HD], shares[0][..., HD + 1])
    for share in shares[1:]:
        merged = combine_partials(merged, (share[..., :HD], share[..., HD], share[..., HD + 1]))
    own_out, own_peak, own_sum = merged
    partial_terms = jnp.dot(own_rows, key_value_weight, preferred_element_type=jnp.float32)
    terms = exchange(partial_terms.reshape(tensor_count, rows_here, -1), "tensor")
    summed = sum(terms[1:], terms[0])
    positions = lax.dynamic_slice_in_dim(
        slot_positions(prompt_blocks, block_owner, block_slot, group_index), tensor_rank * rows_here, rows_here, 0
    )
    prompt_kv = finish_keys(summed, positions, key_gain)
    block_pool = collected(prompt_kv, "tensor").reshape(1, CAP, BLK, -1)
    attended = finish_heads(
        own_out, own_peak, own_sum, queries, new_keys, new_values, tensor_rank, heads_here
    )
    return (attended, block_pool)


VMEM = pl.BlockSpec(memory_space=pltpu.VMEM)
HBM = pl.BlockSpec(memory_space=pltpu.HBM)
F32 = jnp.float32
BF16 = jnp.bfloat16
I16 = jnp.int16
TOP = 32000.0
OCTAVE = 256.0
LN2 = math.log(2.0)
TINY = 1e-30
LEVELS = 64


def on_chip(kernel, operands, in_specs, out_shapes, scratch=(), out_specs=None, flops=0, moved=0):
    return pl.pallas_call(
        kernel,
        out_shape=out_shapes,
        in_specs=in_specs,
        out_specs=out_specs or [VMEM] * len(out_shapes),
        scratch_shapes=list(scratch),
        compiler_params=pltpu.CompilerParams(vmem_limit_bytes=40 * 1024 * 1024),
        cost_estimate=pl.CostEstimate(flops=flops, bytes_accessed=moved, transcendentals=0),
    )(*operands)


def stays(array):
    return pltpu.with_memory_space_constraint(array, pltpu.HBM)


def level_of(peak):
    return jnp.ceil(jnp.log(jnp.maximum(peak, TINY)) * (OCTAVE / LN2))


def as_int16(value):
    return jnp.round(value).astype(jnp.int32).astype(I16)


def as_float(value):
    return value.astype(jnp.int32).astype(F32)


def prepare(states, weight, key_gain, block_owner, block_slot, prompt_blocks):
    token_count = states.shape[0]
    half_depth = weight.shape[0] // 2
    rows_here = CAP * BLK // lax.axis_size("tensor")
    slots_here = rows_here // BLK
    prompt_count = prompt_blocks.shape[0]
    fetched = [block_owner, block_slot, prompt_blocks, key_gain[None, :]]
    count = len(fetched)

    def kernel(*refs):
        sources, states_hbm, weight_hbm = refs[:count], refs[count], refs[count + 1]
        cosine_ref, sine_ref, states_ref, table_ref, weight_ref = refs[count + 2 : count + 7]
        held, (source, sems) = refs[count + 7 : 2 * count + 7], refs[2 * count + 7 :]
        owner, slot, prompts, gain = held
        pairs = [*zip(sources, held), (states_hbm, states_ref), (weight_hbm.at[pl.ds(0, half_depth)], weight_ref)]
        copies = [pltpu.make_async_copy(s, d, sems.at[i]) for i, (s, d) in enumerate(pairs)]
        for copy in copies:
            copy.start()
        group = lax.axis_index("section")
        rank = lax.axis_index("tensor")
        core = lax.rem(group, 2)
        for copy in copies[:count]:
            copy.wait()

        for j in range(2 * CAP):
            source[j] = -1
        for b in range(NB):

            @pl.when(owner[b] == core)
            def _():
                source[slot[b]] = b

            @pl.when(owner[b] == 3 - core)
            def _():
                source[CAP + slot[b]] = b

        token = lax.broadcasted_iota(jnp.int32, (BLK, token_count), 1)
        inner = lax.broadcasted_iota(jnp.int32, (BLK, token_count), 0)
        for j in range(2 * CAP):
            chosen = token == source[j] * BLK + inner
            table_ref[pl.ds(j * BLK, BLK), :] = jnp.where(chosen, 1.0, 0.0).astype(BF16)

        lane = lax.broadcasted_iota(jnp.int32, (BLK, HD), 1)
        row = lax.broadcasted_iota(jnp.int32, (BLK, HD), 0)
        half = lax.rem(lane, HD // 2).astype(F32)
        frequency = jnp.exp(half * (-2.0 / HD * math.log(ROPE_BASE)))
        far_gain = pltpu.roll(jnp.broadcast_to(gain[...], (8, HD)), HD // 2, 1)[0:1]
        for s in range(slots_here):
            block = 0
            for b in range(NB):
                block = jnp.where((owner[b] == group) & (slot[b] == rank * slots_here + s), b, block)
            first, begin = 0, 0
            for j in range(prompt_count):
                first = jnp.where(block >= begin, begin, first)
                begin = begin + prompts[j]
            angles = ((block - first) * BLK + row).astype(F32) * frequency
            cosine_ref[pl.ds(s * BLK, BLK), :] = jnp.cos(angles) * gain[...]
            sine = jnp.sin(angles) * far_gain
            sine_ref[pl.ds(s * BLK, BLK), :] = jnp.where(lane < HD // 2, -sine, sine)
        copies[count].wait()
        copies[count + 1].wait()

    return on_chip(
        kernel,
        [stays(array) for array in (*fetched, states, weight)],
        [HBM] * (count + 2),
        [
            jax.ShapeDtypeStruct((rows_here, HD), F32),
            jax.ShapeDtypeStruct((rows_here, HD), F32),
            jax.ShapeDtypeStruct(states.shape, BF16),
            jax.ShapeDtypeStruct((2 * CAP * BLK, token_count), BF16),
            jax.ShapeDtypeStruct((half_depth, weight.shape[1]), BF16),
        ],
        [pltpu.SMEM(array.shape, jnp.int32) for array in fetched[:3]]
        + [
            pltpu.VMEM((1, HD), F32),
            pltpu.SMEM((2 * CAP,), jnp.int32),
            pltpu.SemaphoreType.DMA((count + 2,)),
        ],
        moved=2 * states.size + weight.size,
    )


def place_rows(own_states, near_states, table):
    width = own_states.shape[1]
    rows = CAP * BLK

    def kernel(own_ref, near_ref, table_ref, keep_ref, *send_refs):
        core = lax.rem(lax.axis_index("section"), 2)

        def place(states):
            placed = jnp.dot(table_ref[...], states[...], preferred_element_type=F32).astype(BF16)
            keep_ref[...] = placed[:rows]
            for k, send_ref in enumerate(send_refs):
                send_ref[...] = placed[rows:, k * width // 2 : (k + 1) * width // 2]

        @pl.when(core == 0)
        def _():
            place(own_ref)

        @pl.when(core == 1)
        def _():
            place(near_ref)

    return on_chip(
        kernel,
        (own_states, near_states, table),
        [VMEM] * 3,
        [jax.ShapeDtypeStruct((rows, width), BF16)] + [jax.ShapeDtypeStruct((rows, width // 2), BF16)] * 2,
        moved=own_states.size * 2,
    )


def attend_span(queries, cache_keys, cache_values, decode_lengths, weight, after):
    half_depth = weight.shape[0] // 2
    row_count, local_len = cache_keys.shape[0], cache_keys.shape[1]
    width = row_count * HD
    fetched = [decode_lengths, queries, cache_keys, cache_values]
    count = len(fetched)

    def kernel(*refs):
        sources, weight_hbm = refs[:count], refs[count]
        span_ref, code_ref, query_ref, weight_ref = refs[count + 2 : count + 6]
        held, (scores, weights, sems) = refs[count + 6 : 2 * count + 6], refs[2 * count + 6 :]
        length, packed, keys, values = held
        copies = [pltpu.make_async_copy(s, d, sems.at[i]) for i, (s, d) in enumerate(zip(sources, held))]
        rest = weight_hbm.at[pl.ds(half_depth, half_depth)]
        copies.append(pltpu.make_async_copy(rest, weight_ref, sems.at[count]))
        for copy in copies:
            copy.start()
        rank = lax.axis_index("tensor")
        copies[0].wait()
        copies[1].wait()
        for h in range(H):
            piece = packed[:, pl.ds(h * HD, HD)].astype(F32)
            query_ref[pl.ds(h, row_count, stride=H), :] = piece
        copies[2].wait()
        for r in range(row_count):
            for pair in range(KVH // 2):
                pair_queries = query_ref[pl.ds(r * H + pair * 2 * G, 2 * G), :].astype(BF16)
                for n in (2 * pair, 2 * pair + 1):
                    both = lax.dot_general(
                        pair_queries,
                        keys[r, :, n * HD : (n + 1) * HD],
                        (((1,), (1,)), ((), ())),
                        preferred_element_type=F32,
                    )
                    scores[r, pl.ds(n * G, G), :] = both[(n % 2) * G : (n % 2 + 1) * G]
        place = lax.broadcasted_iota(jnp.int32, (H, local_len), 1) + rank * local_len
        column = lax.broadcasted_iota(jnp.int32, (H, HD), 1)
        stats = jnp.zeros((H, HD), F32)
        for r in range(row_count):
            live = place < length[r]
            row_scores = jnp.where(live, scores[r] * HD ** (-0.5), MASKED_SCORE)
            peak = jnp.max(row_scores, axis=1, keepdims=True)
            weight = jnp.where(live, jnp.exp(row_scores - peak), 0.0)
            total = jnp.sum(weight, axis=1, keepdims=True)
            weights[r] = weight.astype(BF16)
            stats = jnp.where(column == r, peak, stats)
            stats = jnp.where(column == row_count + r, total, stats)
        span_ref[:, pl.ds(width, HD)] = stats
        copies[3].wait()
        levels = jnp.zeros((H, HD), F32)
        for r in range(row_count):
            for pair in range(KVH // 2):
                pair_weights = weights[r, pl.ds(pair * 2 * G, 2 * G), :]
                for n in (2 * pair, 2 * pair + 1):
                    both = jnp.dot(
                        pair_weights, values[r, :, n * HD : (n + 1) * HD], preferred_element_type=F32
                    )
                    span_ref[pl.ds(n * G, G), pl.ds(r * HD, HD)] = both[(n % 2) * G : (n % 2 + 1) * G]
        for r in range(row_count):
            peak = jnp.max(jnp.abs(span_ref[:, pl.ds(r * HD, HD)]), axis=1, keepdims=True)
            levels = jnp.where(column == r, peak, levels)
        levels = level_of(levels)
        scale = TOP * jnp.exp(levels * (-LN2 / OCTAVE))
        for r in range(row_count):
            out = span_ref[:, pl.ds(r * HD, HD)]
            code_ref[:, pl.ds(r * HD, HD)] = as_int16(out * scale[:, r : r + 1])
        peaks = jnp.maximum(stats, -TOP)
        fine = jnp.where(column < row_count, peaks, stats * HD)
        whole = jnp.floor(fine)
        part = (fine - whole) * TOP
        coded = jnp.where(column < 2 * row_count, whole, 0.0)
        shifted = pltpu.roll(jnp.where(column < 2 * row_count, part, 0.0), 2 * row_count, 1)
        moved = pltpu.roll(jnp.where(column < row_count, levels, 0.0), 4 * row_count, 1)
        code_ref[:, pl.ds(width, HD)] = as_int16(coded + shifted + moved)
        copies[count].wait()

    return on_chip(
        kernel,
        [stays(array) for array in (*fetched, weight)] + [after],
        [HBM] * (count + 1) + [pl.BlockSpec(memory_space=pl.ANY)],
        [
            jax.ShapeDtypeStruct((H, width + HD), F32),
            jax.ShapeDtypeStruct((H, width + HD), I16),
            jax.ShapeDtypeStruct((row_count * H, HD), F32),
            jax.ShapeDtypeStruct((half_depth, weight.shape[1]), BF16),
        ],
        [pltpu.SMEM((row_count,), jnp.int32)]
        + [pltpu.VMEM(array.shape, array.dtype) for array in fetched[1:]]
        + [
            pltpu.VMEM((row_count, H, local_len), F32),
            pltpu.VMEM((row_count, H, local_len), BF16),
            pltpu.SemaphoreType.DMA((count + 1,)),
        ],
        flops=4 * row_count * H * HD * local_len,
        moved=4 * cache_keys.size + weight.size,
    )


def begin_rows(kept, landed, weight):
    slot_rows, depth = landed.shape
    width = weight.shape[1]

    def kernel(kept_ref, landed_ref, weight_ref, out_ref):
        far = lax.axis_index("section") >= 2
        rows = jnp.where(far, landed_ref[...], kept_ref[:, pl.ds(0, depth)])
        for c in range(0, width, 512):
            columns = pl.ds(c, 512)
            out_ref[:, columns] = jnp.dot(rows, weight_ref[:, columns], preferred_element_type=F32)

    return on_chip(
        kernel,
        (kept, landed, weight),
        [VMEM] * 3,
        [jax.ShapeDtypeStruct((slot_rows, width), F32)],
        flops=2 * slot_rows * depth * width,
        moved=2 * weight.size,
    )[0]


def project_rows(begun, kept, landed, weight, span_code, steps):
    slot_rows, depth = landed.shape
    width = weight.shape[1]
    rows_here = slot_rows // len(steps)
    heads_here = H // len(steps)
    span_width = span_code.shape[1] - HD
    share_width = width + span_width + HD
    step_width = 256

    def kernel(begun_ref, kept_ref, landed_ref, weight_ref, span_ref, own_ref, *refs):
        share_refs, (held, code) = refs[:-2], refs[-2:]
        far = lax.axis_index("section") >= 2
        rank = lax.axis_index("tensor")
        rows = jnp.where(far, landed_ref[...], kept_ref[:, pl.ds(depth, depth)])
        lane = lax.broadcasted_iota(jnp.int32, (slot_rows, HD), 1)
        levels = jnp.zeros((slot_rows, HD), F32)
        for c in range(0, width, step_width):
            product = begun_ref[:, c : c + step_width] + jnp.dot(
                rows, weight_ref[:, c : c + step_width], preferred_element_type=F32
            )
            held[:, c : c + step_width] = product
            for m in range(0, step_width, HD):
                tile = product[:, m : m + HD]
                level = level_of(jnp.max(jnp.abs(tile), axis=1, keepdims=True))
                levels = jnp.where(lane == LEVELS + (c + m) // HD, level, levels)
                scaled = tile * (TOP * jnp.exp(level * (-LN2 / OCTAVE)))
                code[:, c + m : c + m + HD] = as_int16(scaled)
        code[:, width:] = as_int16(levels)

        def rows_of(step):
            return pl.ds(pl.multiple_of((rank ^ step) * rows_here, rows_here), rows_here)

        own_ref[...] = held[rows_of(0), :]
        for k, step in enumerate(steps[1:]):
            heads = pl.ds(pl.multiple_of((rank ^ step) * heads_here, heads_here), heads_here)
            share_refs[k][:, pl.ds(0, width)] = code[rows_of(step), pl.ds(0, width)]
            share_refs[k][:, pl.ds(width, span_width)] = span_ref[heads, pl.ds(0, span_width)]
            stats = as_float(span_ref[heads, pl.ds(span_width, HD)])
            both = jnp.where(lane[:rows_here] < LEVELS, stats, as_float(code[rows_of(step), pl.ds(width, HD)]))
            share_refs[k][:, pl.ds(width + span_width, HD)] = as_int16(both)

    return on_chip(
        kernel,
        (begun, kept, landed, weight, span_code),
        [VMEM] * 5,
        [jax.ShapeDtypeStruct((rows_here, width), F32)]
        + [jax.ShapeDtypeStruct((rows_here, share_width), I16)] * (len(steps) - 1),
        [pltpu.VMEM((slot_rows, width), F32), pltpu.VMEM((slot_rows, width + HD), I16)],
        flops=2 * slot_rows * depth * width,
        moved=2 * weight.size,
    )


def add_shares(total, shares):
    rows, width = total.shape
    count = len(shares)
    share_width = shares[0].shape[1]

    def kernel(total_ref, *refs):
        share_refs, out_ref = refs[:count], refs[count]
        scales = [
            jnp.exp(as_float(ref[:, pl.ds(share_width - HD, HD)]) * (LN2 / OCTAVE)) * (1.0 / TOP)
            for ref in share_refs
        ]
        for n in range(width // HD):
            columns = pl.ds(n * HD, HD)
            part = total_ref[:, columns]
            for ref, scale in zip(share_refs, scales):
                part = part + as_float(ref[:, columns]) * scale[:, LEVELS + n : LEVELS + n + 1]
            out_ref[:, columns] = part

    return on_chip(
        kernel, (total, *shares), [VMEM] * (count + 1), [jax.ShapeDtypeStruct((rows, width), F32)]
    )[0]


def finish_rows(own, shares, cosine, sine):
    rows, width = own.shape
    share_count = len(shares)
    share_width = shares[0].shape[1]

    def kernel(own_ref, *refs):
        share_refs = refs[:share_count]
        cosine_ref, sine_ref, out_ref = refs[share_count:]
        scales = [
            jnp.exp(as_float(ref[:, pl.ds(share_width - HD, HD)]) * (LN2 / OCTAVE)) * (1.0 / TOP)
            for ref in share_refs
        ]
        for n in range(width // HD):
            columns = pl.ds(n * HD, HD)
            total = own_ref[:, columns]
            for ref, scale in zip(share_refs, scales):
                total = total + as_float(ref[:, columns]) * scale[:, LEVELS + n : LEVELS + n + 1]
            if n < KVH:
                mean = jnp.sum(total * total, axis=1, keepdims=True) * (1.0 / HD)
                total = total * cosine_ref[...] + pltpu.roll(total, HD // 2, 1) * sine_ref[...]
                total = total * lax.rsqrt(mean + NORM_EPSILON)
            out_ref[:, columns] = total.astype(BF16)

    return on_chip(
        kernel,
        (own, *shares, cosine, sine),
        [VMEM] * (share_count + 3),
        [jax.ShapeDtypeStruct((rows, width), BF16)],
    )[0]


def merge_spans(span, shares, queries, new_keys, new_values, begin):
    row_count = new_keys.shape[0]
    share_count = len(shares)
    heads_here = shares[0].shape[0]
    keys_here = heads_here // G
    width = row_count * HD

    def kernel(span_ref, *refs):
        share_refs = refs[:share_count]
        query_ref, key_ref, value_ref, out_ref = refs[share_count:]
        rank = lax.axis_index("tensor")
        heads = pl.ds(pl.multiple_of(rank * heads_here, heads_here), heads_here)
        columns = pl.ds(pl.multiple_of(rank * keys_here * HD, HD), keys_here * HD)
        new_key, new_value = key_ref[:, columns].astype(F32), value_ref[:, columns].astype(F32)

        def spread(tile, r):
            return jnp.concatenate(
                [
                    jnp.broadcast_to(tile[r : r + 1, kk * HD : (kk + 1) * HD], (G, HD))
                    for kk in range(keys_here)
                ],
                axis=0,
            )

        stats, scales = [span_ref[heads, pl.ds(width, HD)]], []
        for ref in share_refs:
            code = as_float(ref[:, pl.ds(begin + width, HD)])
            column = lax.broadcasted_iota(jnp.int32, code.shape, 1)
            fine = code + pltpu.roll(code, HD - 2 * row_count, 1) * (1.0 / TOP)
            stats.append(jnp.where(column < row_count, fine, fine * (1.0 / HD)))
            scales.append(jnp.exp(code * (LN2 / OCTAVE)) * (1.0 / TOP))

        def part(k, r):
            if k == 0:
                return span_ref[heads, pl.ds(r * HD, HD)]
            coded = as_float(share_refs[k - 1][:, pl.ds(begin + r * HD, HD)])
            return coded * scales[k - 1][:, 4 * row_count + r : 4 * row_count + r + 1]

        for r in range(row_count):
            query = query_ref[pl.ds(pl.multiple_of(r * H + rank * heads_here, heads_here), heads_here), :]
            self_score = jnp.sum(query * spread(new_key, r), axis=1, keepdims=True) * HD ** (-0.5)
            row_peak = self_score
            for tile in stats:
                row_peak = jnp.maximum(row_peak, tile[:, r : r + 1])
            self_weight = jnp.exp(self_score - row_peak)
            numerator = self_weight * spread(new_value, r)
            denominator = self_weight
            for k, tile in enumerate(stats):
                factor = jnp.exp(tile[:, r : r + 1] - row_peak)
                numerator += factor * part(k, r)
                denominator += factor * tile[:, row_count + r : row_count + r + 1]
            out_ref[r] = (numerator / denominator).astype(BF16)

    attended = on_chip(
        kernel,
        (span, *shares, queries, new_keys, new_values),
        [VMEM] * (share_count + 4),
        [jax.ShapeDtypeStruct((row_count, heads_here, HD), BF16)],
    )[0]
    return attended.reshape(row_count, heads_here * HD)


def join_rows(pieces, steps):
    count = len(pieces)
    rows, width = pieces[0].shape

    def kernel(*refs):
        piece_refs, out_hbm, sems = refs[:count], refs[count], refs[count + 1]
        rank = lax.axis_index("tensor")
        copies = []
        for step in range(count):
            place = pl.ds(pl.multiple_of(lax.rem(rank + count - steps[step], count) * rows, rows), rows)
            copies.append(pltpu.make_async_copy(piece_refs[step], out_hbm.at[place], sems.at[step]))
        for copy in copies:
            copy.start()
        for copy in copies:
            copy.wait()

    return on_chip(
        kernel,
        pieces,
        [VMEM] * count,
        [jax.ShapeDtypeStruct((count * rows, width), BF16)],
        [pltpu.SemaphoreType.DMA((count,))],
        out_specs=[HBM],
    )[0]


def swap(piece, axis, step):
    return lax.ppermute(piece, axis, [(i, i ^ step) for i in range(lax.axis_size(axis))])


def turn(piece, axis, step):
    count = lax.axis_size(axis)
    return lax.ppermute(piece, axis, [(i, (i + step) % count) for i in range(count)])


def local(
    prompt,
    key_value_weight,
    key_gain,
    prompt_blocks,
    block_owner,
    block_slot,
    queries,
    cache_keys,
    cache_values,
    new_keys,
    new_values,
    decode_lengths,
):
    tensor_count = lax.axis_size("tensor")
    near_states = swap(prompt[0], "section", 1)
    cosine, sine, states, table, first_weight = prepare(
        prompt[0], key_value_weight, key_gain, block_owner, block_slot, prompt_blocks
    )
    kept, *sent = place_rows(states, near_states, table)
    landed = [swap(half, "section", 3) for half in sent]
    span, span_code, row_queries, rest_weight = attend_span(
        queries, cache_keys, cache_values, decode_lengths, key_value_weight, kept
    )
    steps = (0,) + tuple(range(tensor_count - 1, 0, -1))
    begun = begin_rows(kept, landed[0], first_weight)
    own, *shares = project_rows(begun, kept, landed[1], rest_weight, span_code, steps)
    shares = [swap(share, "tensor", step) for share, step in zip(shares, steps[1:])]
    finished = finish_rows(add_shares(own, [shares[0], shares[2]]), [shares[1]], cosine, sine)
    pieces = [finished] + [turn(finished, "tensor", step) for step in steps[1:]]
    block_pool = join_rows(pieces, steps)
    attended = merge_spans(span, shares, row_queries, new_keys, new_values, key_value_weight.shape[1])
    return (attended, block_pool.reshape(1, CAP, BLK, -1))


def solution(mesh):
    in_specs = (
        P(("parts", "section"), None, "tensor"),
        P("tensor", None),
        P(),
        P("parts"),
        P("parts"),
        P("parts"),
        P(("parts", "section"), None),
        P(("parts", "section"), "tensor", None),
        P(("parts", "section"), "tensor", None),
        P(("parts", "section"), None),
        P(("parts", "section"), None),
        P(("parts", "section")),
    )
    out_specs = (P(("parts", "section"), "tensor"), P(("parts", "section"), None, None, None))
    tensor_count = mesh.shape["tensor"]
    whole_tiles = tensor_count == 4 and mesh.shape["section"] == 4
    program = local if whole_tiles else local_small_shares
    return jax.shard_map(program, mesh=mesh, in_specs=in_specs, out_specs=out_specs, check_vma=False)
```

```python
import math

import jax
import jax.numpy as jnp
from jax import lax
from jax.experimental import pallas as pl
from jax.experimental.pallas import tpu as pltpu
from jax.sharding import PartitionSpec as P

H = 64
KVH = 8
HD = 128
BLK = 16
SPAN = 128
KVW = 1024
G = 8
NB = 16
CAP = 4


NORM_EPSILON = 1e-06
ROPE_BASE = 1000000.0
MASKED_SCORE = -1e30


def exchange(pieces, axis):
    count = lax.axis_size(axis)
    rank = lax.axis_index(axis)
    landed = [lax.dynamic_index_in_dim(pieces, rank, 0, keepdims=False)]
    for step in range(1, count):
        piece = lax.dynamic_index_in_dim(pieces, rank ^ step, 0, keepdims=False)
        landed.append(lax.ppermute(piece, axis, [(i, i ^ step) for i in range(count)]))
    return landed


def collected(own, axis):
    count = lax.axis_size(axis)
    rank = lax.axis_index(axis)
    landed = [own]
    for step in range(1, count):
        landed.append(lax.ppermute(own, axis, [(i, i ^ step) for i in range(count)]))
    stacked = jnp.zeros((count,) + own.shape, own.dtype)
    for step, piece in enumerate(landed):
        stacked = lax.dynamic_update_index_in_dim(stacked, piece, rank ^ step, 0)
    return stacked


def rows_for_groups(states, block_owner, block_slot, group_count):
    slot_ids = jnp.arange(group_count * CAP, dtype=jnp.int32)
    selector = (block_owner * CAP + block_slot)[None, :] == slot_ids[:, None]
    filled = jnp.any(selector, axis=1)
    source = jnp.argmax(selector, axis=1)
    blocks = states.reshape(NB, BLK, states.shape[1])
    chosen = jnp.where(filled[:, None, None], blocks[source], jnp.zeros((), states.dtype))
    return chosen.reshape(group_count, CAP * BLK, states.shape[1])


def spread(rows, axis):
    count = lax.axis_size(axis)
    landed = jnp.where(lax.axis_index(axis) == 0, rows[0], jnp.zeros_like(rows[0]))
    for k in range(1, count):
        landed = landed + lax.ppermute(rows[k], axis, [(0, k)])
    return landed


def slot_positions(prompt_blocks, block_owner, block_slot, group_index):
    prompt_ends = jnp.cumsum(prompt_blocks)
    prompt_starts = prompt_ends - prompt_blocks
    slot_ids = jnp.arange(CAP, dtype=jnp.int32)
    selector = (block_owner[None, :] == group_index) & (block_slot[None, :] == slot_ids[:, None])
    block = jnp.sum(jnp.where(selector, jnp.arange(NB, dtype=jnp.int32)[None, :], 0), axis=1)
    inside = (block[:, None] >= prompt_starts[None, :]) & (block[:, None] < prompt_ends[None, :])
    first = jnp.sum(jnp.where(inside, prompt_starts[None, :], 0), axis=1)
    return (((block - first) * BLK)[:, None] + jnp.arange(BLK, dtype=jnp.int32)[None, :]).reshape(-1)


def finish_keys(projected, positions, key_gain):
    token_count = projected.shape[0]
    key_heads = projected[:, :KVW].reshape(token_count, KVH, HD)
    inv_root = lax.rsqrt(jnp.mean(key_heads * key_heads, axis=-1, keepdims=True) + NORM_EPSILON)
    key_heads = key_heads * inv_root * key_gain
    half_dim = HD // 2
    frequency = ROPE_BASE ** (jnp.arange(half_dim, dtype=jnp.float32) * (-2.0 / HD))
    angles = positions.astype(jnp.float32)[:, None, None] * frequency[None, None, :]
    cosine = jnp.cos(angles)
    sine_part = jnp.sin(angles)
    lower_half = key_heads[..., :half_dim]
    upper_half = key_heads[..., half_dim:]
    rotated = jnp.concatenate(
        [
            lower_half * cosine - upper_half * sine_part,
            upper_half * cosine + lower_half * sine_part,
        ],
        axis=-1,
    )
    return jnp.concatenate([rotated.reshape(token_count, KVW), projected[:, KVW:]], axis=1).astype(
        jnp.bfloat16
    )


def partial_attention(queries, cache_keys, cache_values, decode_lengths, first_position):
    row_count = queries.shape[0]
    local_len = cache_keys.shape[1]
    span_count = local_len // SPAN
    query_heads = queries.reshape(row_count, KVH, G, HD)
    key_heads = cache_keys.reshape(row_count, local_len, KVH, HD)
    scores = jnp.einsum(
        "rkgd,rpkd->rkgp", query_heads, key_heads, preferred_element_type=jnp.float32
    ) * HD ** (-0.5)
    live_mask = (first_position + jnp.arange(local_len, dtype=jnp.int32))[None, :] < decode_lengths[
        :, None
    ]
    scores = jnp.where(live_mask[:, None, None, :], scores, MASKED_SCORE)
    spans = scores.reshape(row_count, KVH, G, span_count, SPAN)
    span_max = jnp.max(spans, axis=-1)
    live_spans = live_mask.reshape(row_count, 1, 1, span_count, SPAN)
    weights = jnp.where(live_spans, jnp.exp(spans - span_max[..., None]), 0.0)
    span_sum = jnp.sum(weights, axis=-1)
    value_spans = cache_values.reshape(row_count, span_count, SPAN, KVH, HD)
    span_out = jnp.einsum(
        "rkgns,rnskd->rkgnd",
        weights.astype(jnp.bfloat16),
        value_spans,
        preferred_element_type=jnp.float32,
    )
    row_peak = jnp.max(span_max, axis=-1)
    factor = jnp.exp(span_max - row_peak[..., None])
    partial_out = jnp.sum(span_out * factor[..., None], axis=3)
    partial_sum = jnp.sum(span_sum * factor, axis=-1)
    return (
        partial_out.reshape(row_count, H, HD),
        row_peak.reshape(row_count, H),
        partial_sum.reshape(row_count, H),
    )


def combine_partials(former, latter):
    former_out, former_peak, former_sum = former
    latter_out, latter_peak, latter_sum = latter
    highest = jnp.maximum(former_peak, latter_peak)
    former_factor = jnp.exp(former_peak - highest)
    latter_factor = jnp.exp(latter_peak - highest)
    merged_out = former_out * former_factor[..., None] + latter_out * latter_factor[..., None]
    return (merged_out, highest, former_sum * former_factor + latter_sum * latter_factor)


def finish_heads(
    own_out, own_peak, own_sum, queries, new_keys, new_values, tensor_rank, heads_here
):
    row_count = queries.shape[0]
    own_width = heads_here * HD
    own_queries = (
        lax.dynamic_slice_in_dim(queries, tensor_rank * own_width, own_width, 1)
        .reshape(row_count, heads_here, HD)
        .astype(jnp.float32)
    )
    head_ids = tensor_rank * heads_here + jnp.arange(heads_here, dtype=jnp.int32)
    selector = (head_ids[:, None] // G == jnp.arange(KVH, dtype=jnp.int32)[None, :]).astype(
        jnp.float32
    )
    own_keys = jnp.einsum(
        "jk,rkd->rjd",
        selector,
        new_keys.reshape(row_count, KVH, HD).astype(jnp.float32),
        precision=lax.Precision.HIGHEST,
    )
    own_values = jnp.einsum(
        "jk,rkd->rjd",
        selector,
        new_values.reshape(row_count, KVH, HD).astype(jnp.float32),
        precision=lax.Precision.HIGHEST,
    )
    self_score = jnp.sum(own_queries * own_keys, axis=-1) * HD ** (-0.5)
    row_peak = jnp.maximum(own_peak, self_score)
    factor = jnp.exp(own_peak - row_peak)
    self_weight = jnp.exp(self_score - row_peak)
    numerator = own_out * factor[..., None] + self_weight[..., None] * own_values
    denominator = own_sum * factor + self_weight
    return (numerator / denominator[..., None]).reshape(row_count, own_width).astype(jnp.bfloat16)


def local_small_shares(
    prompt,
    key_value_weight,
    key_gain,
    prompt_blocks,
    block_owner,
    block_slot,
    queries,
    cache_keys,
    cache_values,
    new_keys,
    new_values,
    decode_lengths,
):
    tensor_count = lax.axis_size("tensor")
    tensor_rank = lax.axis_index("tensor")
    group_index = lax.axis_index("section")
    group_count = lax.axis_size("section")
    slot_rows = CAP * BLK
    rows_here = slot_rows // tensor_count
    rows = rows_for_groups(prompt[0], block_owner, block_slot, group_count)
    own_rows = spread(rows, "section")
    local_len = cache_keys.shape[1]
    row_count = queries.shape[0]
    heads_here = H // tensor_count
    partial_out, partial_peak, partial_sum = partial_attention(
        queries, cache_keys, cache_values, decode_lengths, tensor_rank * local_len
    )
    stats = jnp.stack([partial_peak, partial_sum], axis=-1).reshape(row_count, tensor_count, heads_here, 2)
    outs = partial_out.reshape(row_count, tensor_count, heads_here, HD)
    packed = jnp.concatenate([outs, jnp.pad(stats, ((0, 0), (0, 0), (0, 0), (0, HD - 2)))], axis=-1)
    shares = exchange(packed.transpose(1, 0, 2, 3), "tensor")
    merged = (shares[0][..., :HD], shares[0][..., HD], shares[0][..., HD + 1])
    for share in shares[1:]:
        merged = combine_partials(merged, (share[..., :HD], share[..., HD], share[..., HD + 1]))
    own_out, own_peak, own_sum = merged
    partial_terms = jnp.dot(own_rows, key_value_weight, preferred_element_type=jnp.float32)
    terms = exchange(partial_terms.reshape(tensor_count, rows_here, -1), "tensor")
    summed = sum(terms[1:], terms[0])
    positions = lax.dynamic_slice_in_dim(
        slot_positions(prompt_blocks, block_owner, block_slot, group_index), tensor_rank * rows_here, rows_here, 0
    )
    prompt_kv = finish_keys(summed, positions, key_gain)
    block_pool = collected(prompt_kv, "tensor").reshape(1, CAP, BLK, -1)
    attended = finish_heads(
        own_out, own_peak, own_sum, queries, new_keys, new_values, tensor_rank, heads_here
    )
    return (attended, block_pool)


VMEM = pl.BlockSpec(memory_space=pltpu.VMEM)
HBM = pl.BlockSpec(memory_space=pltpu.HBM)
F32 = jnp.float32
BF16 = jnp.bfloat16
I16 = jnp.int16
TOP = 32000.0
OCTAVE = 256.0
LN2 = math.log(2.0)
TINY = 1e-30
LEVELS = 64


def on_chip(kernel, operands, in_specs, out_shapes, scratch=(), out_specs=None, flops=0, moved=0):
    return pl.pallas_call(
        kernel,
        out_shape=out_shapes,
        in_specs=in_specs,
        out_specs=out_specs or [VMEM] * len(out_shapes),
        scratch_shapes=list(scratch),
        compiler_params=pltpu.CompilerParams(vmem_limit_bytes=40 * 1024 * 1024),
        cost_estimate=pl.CostEstimate(flops=flops, bytes_accessed=moved, transcendentals=0),
    )(*operands)


def stays(array):
    return pltpu.with_memory_space_constraint(array, pltpu.HBM)


def level_of(peak):
    return jnp.ceil(jnp.log(jnp.maximum(peak, TINY)) * (OCTAVE / LN2))


def as_int16(value):
    return jnp.round(value).astype(jnp.int32).astype(I16)


def as_float(value):
    return value.astype(jnp.int32).astype(F32)


def prepare(
    states, key_gain, block_owner, block_slot, prompt_blocks, queries, cache_keys, cache_values, decode_lengths
):
    token_count = states.shape[0]
    rows_here = CAP * BLK // lax.axis_size("tensor")
    slots_here = rows_here // BLK
    prompt_count = prompt_blocks.shape[0]
    row_count, local_len = cache_keys.shape[0], cache_keys.shape[1]
    fetched = [block_owner, block_slot, prompt_blocks, decode_lengths, key_gain[None, :], queries, cache_keys]
    count = len(fetched)

    def kernel(*refs):
        sources, states_hbm, value_hbm = refs[:count], refs[count], refs[count + 1]
        outs, rest = refs[count + 2 : count + 10], refs[count + 10 :]
        cosine_ref, sine_ref, states_ref, table_ref, weight_ref, stats_ref, query_ref, value_ref = outs
        held, (source, scores, sems) = rest[:count], rest[count:]
        owner, slot, prompts, length, gain, packed, keys = held
        pairs = [*zip(sources, held), (states_hbm, states_ref), (value_hbm, value_ref)]
        copies = [pltpu.make_async_copy(s, d, sems.at[i]) for i, (s, d) in enumerate(pairs)]
        for copy in copies:
            copy.start()
        group = lax.axis_index("section")
        rank = lax.axis_index("tensor")
        core = lax.rem(group, 2)
        for copy in copies[:6]:
            copy.wait()

        for j in range(2 * CAP):
            source[j] = -1
        for b in range(NB):

            @pl.when(owner[b] == core)
            def _():
                source[slot[b]] = b

            @pl.when(owner[b] == 3 - core)
            def _():
                source[CAP + slot[b]] = b

        token = lax.broadcasted_iota(jnp.int32, (BLK, token_count), 1)
        inner = lax.broadcasted_iota(jnp.int32, (BLK, token_count), 0)
        for j in range(2 * CAP):
            chosen = token == source[j] * BLK + inner
            table_ref[pl.ds(j * BLK, BLK), :] = jnp.where(chosen, 1.0, 0.0).astype(BF16)

        lane = lax.broadcasted_iota(jnp.int32, (BLK, HD), 1)
        row = lax.broadcasted_iota(jnp.int32, (BLK, HD), 0)
        half = lax.rem(lane, HD // 2).astype(F32)
        frequency = jnp.exp(half * (-2.0 / HD * math.log(ROPE_BASE)))
        far_gain = pltpu.roll(jnp.broadcast_to(gain[...], (8, HD)), HD // 2, 1)[0:1]
        for s in range(slots_here):
            block = 0
            for b in range(NB):
                block = jnp.where((owner[b] == group) & (slot[b] == rank * slots_here + s), b, block)
            first, begin = 0, 0
            for j in range(prompt_count):
                first = jnp.where(block >= begin, begin, first)
                begin = begin + prompts[j]
            angles = ((block - first) * BLK + row).astype(F32) * frequency
            cosine_ref[pl.ds(s * BLK, BLK), :] = jnp.cos(angles) * gain[...]
            sine = jnp.sin(angles) * far_gain
            sine_ref[pl.ds(s * BLK, BLK), :] = jnp.where(lane < HD // 2, -sine, sine)

        for h in range(H):
            piece = packed[:, pl.ds(h * HD, HD)].astype(F32)
            query_ref[pl.ds(h, row_count, stride=H), :] = piece
        copies[6].wait()
        for r in range(row_count):
            for pair in range(KVH // 2):
                pair_queries = query_ref[pl.ds(r * H + pair * 2 * G, 2 * G), :].astype(BF16)
                for n in (2 * pair, 2 * pair + 1):
                    both = lax.dot_general(
                        pair_queries,
                        keys[r, :, n * HD : (n + 1) * HD],
                        (((1,), (1,)), ((), ())),
                        preferred_element_type=F32,
                    )
                    scores[r, pl.ds(n * G, G), :] = both[(n % 2) * G : (n % 2 + 1) * G]
        place = lax.broadcasted_iota(jnp.int32, (H, local_len), 1) + rank * local_len
        column = lax.broadcasted_iota(jnp.int32, (H, HD), 1)
        stats = jnp.zeros((H, HD), F32)
        for r in range(row_count):
            live = place < length[r]
            row_scores = jnp.where(live, scores[r] * HD ** (-0.5), MASKED_SCORE)
            peak = jnp.max(row_scores, axis=1, keepdims=True)
            weight = jnp.where(live, jnp.exp(row_scores - peak), 0.0)
            total = jnp.sum(weight, axis=1, keepdims=True)
            weight_ref[r] = weight.astype(BF16)
            stats = jnp.where(column == r, peak, stats)
            stats = jnp.where(column == row_count + r, total, stats)
        stats_ref[...] = stats
        copies[count].wait()
        copies[count + 1].wait()

    return on_chip(
        kernel,
        [stays(array) for array in (*fetched, states, cache_values)],
        [HBM] * (count + 2),
        [
            jax.ShapeDtypeStruct((rows_here, HD), F32),
            jax.ShapeDtypeStruct((rows_here, HD), F32),
            jax.ShapeDtypeStruct(states.shape, BF16),
            jax.ShapeDtypeStruct((2 * CAP * BLK, token_count), BF16),
            jax.ShapeDtypeStruct((row_count, H, local_len), BF16),
            jax.ShapeDtypeStruct((H, HD), F32),
            jax.ShapeDtypeStruct((row_count * H, HD), F32),
            jax.ShapeDtypeStruct(cache_values.shape, BF16),
        ],
        [pltpu.SMEM(array.shape, jnp.int32) for array in fetched[:4]]
        + [pltpu.VMEM(array.shape, array.dtype) for array in fetched[4:]]
        + [
            pltpu.SMEM((2 * CAP,), jnp.int32),
            pltpu.VMEM((row_count, H, local_len), F32),
            pltpu.SemaphoreType.DMA((count + 2,)),
        ],
        flops=2 * row_count * H * HD * local_len,
        moved=2 * (states.size + cache_keys.size + cache_values.size),
    )


def place_rows(own_states, near_states, table):
    width = own_states.shape[1]
    rows = CAP * BLK

    def kernel(own_ref, near_ref, table_ref, keep_ref, *send_refs):
        core = lax.rem(lax.axis_index("section"), 2)

        def place(states):
            placed = jnp.dot(table_ref[...], states[...], preferred_element_type=F32).astype(BF16)
            keep_ref[...] = placed[:rows]
            for k, send_ref in enumerate(send_refs):
                send_ref[...] = placed[rows:, k * width // 2 : (k + 1) * width // 2]

        @pl.when(core == 0)
        def _():
            place(own_ref)

        @pl.when(core == 1)
        def _():
            place(near_ref)

    return on_chip(
        kernel,
        (own_states, near_states, table),
        [VMEM] * 3,
        [jax.ShapeDtypeStruct((rows, width), BF16)] + [jax.ShapeDtypeStruct((rows, width // 2), BF16)] * 2,
        moved=own_states.size * 2,
    )


def span_sums(weights, stats, values, after, steps):
    row_count, _, local_len = weights.shape
    width = row_count * HD
    heads_here = H // len(steps)

    def kernel(weight_ref, stats_ref, value_ref, after_ref, span_ref, *refs):
        share_refs, code = refs[:-1], refs[-1]
        rank = lax.axis_index("tensor")
        column = lax.broadcasted_iota(jnp.int32, (H, HD), 1)
        for r in range(row_count):
            for pair in range(KVH // 2):
                pair_weights = weight_ref[r, pl.ds(pair * 2 * G, 2 * G), :]
                for n in (2 * pair, 2 * pair + 1):
                    both = jnp.dot(
                        pair_weights, value_ref[r, :, n * HD : (n + 1) * HD], preferred_element_type=F32
                    )
                    span_ref[pl.ds(n * G, G), pl.ds(r * HD, HD)] = both[(n % 2) * G : (n % 2 + 1) * G]
        stats = stats_ref[...]
        span_ref[:, pl.ds(width, HD)] = stats
        levels = jnp.zeros((H, HD), F32)
        for r in range(row_count):
            peak = jnp.max(jnp.abs(span_ref[:, pl.ds(r * HD, HD)]), axis=1, keepdims=True)
            levels = jnp.where(column == r, peak, levels)
        levels = level_of(levels)
        scale = TOP * jnp.exp(levels * (-LN2 / OCTAVE))
        for r in range(row_count):
            code[:, pl.ds(r * HD, HD)] = as_int16(span_ref[:, pl.ds(r * HD, HD)] * scale[:, r : r + 1])
        peaks = jnp.maximum(stats, -TOP)
        fine = jnp.where(column < row_count, peaks, stats * HD)
        whole = jnp.floor(fine)
        part = (fine - whole) * TOP
        coded = jnp.where(column < 2 * row_count, whole, 0.0)
        shifted = pltpu.roll(jnp.where(column < 2 * row_count, part, 0.0), 2 * row_count, 1)
        moved = pltpu.roll(jnp.where(column < row_count, levels, 0.0), 4 * row_count, 1)
        code[:, pl.ds(width, HD)] = as_int16(coded + shifted + moved)
        for k, step in enumerate(steps[1:]):
            start = pl.multiple_of((rank ^ step) * heads_here, heads_here)
            share_refs[k][...] = code[pl.ds(start, heads_here), :]

    return on_chip(
        kernel,
        [weights, stats, values, after],
        [VMEM] * 3 + [pl.BlockSpec(memory_space=pl.ANY)],
        [jax.ShapeDtypeStruct((H, width + HD), F32)]
        + [jax.ShapeDtypeStruct((heads_here, width + HD), I16)] * (len(steps) - 1),
        [pltpu.VMEM((H, width + HD), I16)],
        flops=2 * row_count * H * HD * local_len,
        moved=12 * values.size,
    )


def begin_rows(kept, landed, weight):
    slot_rows, depth = landed.shape
    width = weight.shape[1]

    def kernel(kept_ref, landed_ref, weight_ref, out_ref):
        far = lax.axis_index("section") >= 2
        rows = jnp.where(far, landed_ref[...], kept_ref[:, pl.ds(0, depth)])
        for c in range(0, width, 512):
            columns = pl.ds(c, 512)
            out_ref[:, columns] = jnp.dot(rows, weight_ref[pl.ds(0, depth), columns], preferred_element_type=F32)

    return on_chip(
        kernel,
        (kept, landed, weight),
        [VMEM] * 3,
        [jax.ShapeDtypeStruct((slot_rows, width), F32)],
        flops=2 * slot_rows * depth * width,
        moved=2 * weight.size,
    )[0]


def project_rows(begun, kept, landed, weight, steps):
    slot_rows, depth = landed.shape
    width = weight.shape[1]
    rows_here = slot_rows // len(steps)
    share_width = width + HD
    step_width = 256

    def kernel(begun_ref, kept_ref, landed_ref, weight_ref, own_ref, *refs):
        share_refs, (held, code) = refs[:-2], refs[-2:]
        far = lax.axis_index("section") >= 2
        rank = lax.axis_index("tensor")
        rows = jnp.where(far, landed_ref[...], kept_ref[:, pl.ds(depth, depth)])
        lane = lax.broadcasted_iota(jnp.int32, (slot_rows, HD), 1)
        levels = jnp.zeros((slot_rows, HD), F32)
        for c in range(0, width, step_width):
            product = begun_ref[:, c : c + step_width] + jnp.dot(
                rows, weight_ref[pl.ds(depth, depth), pl.ds(c, step_width)], preferred_element_type=F32
            )
            held[:, c : c + step_width] = product
            for m in range(0, step_width, HD):
                tile = product[:, m : m + HD]
                level = level_of(jnp.max(jnp.abs(tile), axis=1, keepdims=True))
                levels = jnp.where(lane == LEVELS + (c + m) // HD, level, levels)
                scaled = tile * (TOP * jnp.exp(level * (-LN2 / OCTAVE)))
                code[:, c + m : c + m + HD] = as_int16(scaled)
        code[:, width:] = as_int16(levels)

        def rows_of(step):
            return pl.ds(pl.multiple_of((rank ^ step) * rows_here, rows_here), rows_here)

        own_ref[...] = held[rows_of(0), :]
        for k, step in enumerate(steps[1:]):
            levels_code = code[rows_of(step), pl.ds(width, HD)]
            share_refs[k][:, pl.ds(0, width)] = code[rows_of(step), pl.ds(0, width)]
            share_refs[k][:, pl.ds(width, HD)] = levels_code

    return on_chip(
        kernel,
        (begun, kept, landed, weight),
        [VMEM] * 4,
        [jax.ShapeDtypeStruct((rows_here, width), F32)]
        + [jax.ShapeDtypeStruct((rows_here, share_width), I16)] * (len(steps) - 1),
        [pltpu.VMEM((slot_rows, width), F32), pltpu.VMEM((slot_rows, width + HD), I16)],
        flops=2 * slot_rows * depth * width,
        moved=2 * weight.size,
    )


def hand_on(piece, ahead):
    count = len(ahead)

    def kernel(piece_ref, *refs):
        refs[count][...] = piece_ref[...]

    return on_chip(
        kernel,
        (piece, *ahead),
        [VMEM] + [pl.BlockSpec(memory_space=pl.ANY)] * count,
        [jax.ShapeDtypeStruct(piece.shape, piece.dtype)],
    )[0]


def add_shares(total, shares):
    rows, width = total.shape
    count = len(shares)

    def kernel(total_ref, *refs):
        share_refs, out_ref = refs[:count], refs[count]
        scales = [
            jnp.exp(as_float(ref[:, pl.ds(ref.shape[1] - HD, HD)]) * (LN2 / OCTAVE)) * (1.0 / TOP)
            for ref in share_refs
        ]
        for n in range(width // HD):
            columns = pl.ds(n * HD, HD)
            part = total_ref[:, columns]
            for ref, scale in zip(share_refs, scales):
                part = part + as_float(ref[:, columns]) * scale[:, LEVELS + n : LEVELS + n + 1]
            out_ref[:, columns] = part

    return on_chip(
        kernel, (total, *shares), [VMEM] * (count + 1), [jax.ShapeDtypeStruct((rows, width), F32)]
    )[0]


def finish_rows(own, shares, cosine, sine):
    rows, width = own.shape
    share_count = len(shares)

    def kernel(own_ref, *refs):
        share_refs = refs[:share_count]
        cosine_ref, sine_ref, out_ref = refs[share_count:]
        scales = [
            jnp.exp(as_float(ref[:, pl.ds(ref.shape[1] - HD, HD)]) * (LN2 / OCTAVE)) * (1.0 / TOP)
            for ref in share_refs
        ]
        for n in range(width // HD):
            columns = pl.ds(n * HD, HD)
            total = own_ref[:, columns]
            for ref, scale in zip(share_refs, scales):
                total = total + as_float(ref[:, columns]) * scale[:, LEVELS + n : LEVELS + n + 1]
            if n < KVH:
                mean = jnp.sum(total * total, axis=1, keepdims=True) * (1.0 / HD)
                total = total * cosine_ref[...] + pltpu.roll(total, HD // 2, 1) * sine_ref[...]
                total = total * lax.rsqrt(mean + NORM_EPSILON)
            out_ref[:, columns] = total.astype(BF16)

    return on_chip(
        kernel,
        (own, *shares, cosine, sine),
        [VMEM] * (share_count + 3),
        [jax.ShapeDtypeStruct((rows, width), BF16)],
    )[0]


def merge_spans(span, shares, queries, new_keys, new_values):
    row_count = new_keys.shape[0]
    share_count = len(shares)
    heads_here = shares[0].shape[0]
    keys_here = heads_here // G
    width = row_count * HD

    def kernel(span_ref, *refs):
        share_refs = refs[:share_count]
        query_ref, key_ref, value_ref, out_ref = refs[share_count:]
        rank = lax.axis_index("tensor")
        heads = pl.ds(pl.multiple_of(rank * heads_here, heads_here), heads_here)
        columns = pl.ds(pl.multiple_of(rank * keys_here * HD, HD), keys_here * HD)
        new_key, new_value = key_ref[:, columns].astype(F32), value_ref[:, columns].astype(F32)

        def spread(tile, r):
            return jnp.concatenate(
                [
                    jnp.broadcast_to(tile[r : r + 1, kk * HD : (kk + 1) * HD], (G, HD))
                    for kk in range(keys_here)
                ],
                axis=0,
            )

        stats, scales = [span_ref[heads, pl.ds(width, HD)]], []
        for ref in share_refs:
            code = as_float(ref[:, pl.ds(width, HD)])
            column = lax.broadcasted_iota(jnp.int32, code.shape, 1)
            fine = code + pltpu.roll(code, HD - 2 * row_count, 1) * (1.0 / TOP)
            stats.append(jnp.where(column < row_count, fine, fine * (1.0 / HD)))
            scales.append(jnp.exp(code * (LN2 / OCTAVE)) * (1.0 / TOP))

        def part(k, r):
            if k == 0:
                return span_ref[heads, pl.ds(r * HD, HD)]
            coded = as_float(share_refs[k - 1][:, pl.ds(r * HD, HD)])
            return coded * scales[k - 1][:, 4 * row_count + r : 4 * row_count + r + 1]

        for r in range(row_count):
            query = query_ref[pl.ds(pl.multiple_of(r * H + rank * heads_here, heads_here), heads_here), :]
            self_score = jnp.sum(query * spread(new_key, r), axis=1, keepdims=True) * HD ** (-0.5)
            row_peak = self_score
            for tile in stats:
                row_peak = jnp.maximum(row_peak, tile[:, r : r + 1])
            self_weight = jnp.exp(self_score - row_peak)
            numerator = self_weight * spread(new_value, r)
            denominator = self_weight
            for k, tile in enumerate(stats):
                factor = jnp.exp(tile[:, r : r + 1] - row_peak)
                numerator += factor * part(k, r)
                denominator += factor * tile[:, row_count + r : row_count + r + 1]
            out_ref[r] = (numerator / denominator).astype(BF16)

    attended = on_chip(
        kernel,
        (span, *shares, queries, new_keys, new_values),
        [VMEM] * (share_count + 4),
        [jax.ShapeDtypeStruct((row_count, heads_here, HD), BF16)],
    )[0]
    return attended.reshape(row_count, heads_here * HD)


def join_rows(pieces, steps):
    count = len(pieces)
    rows, width = pieces[0].shape

    def kernel(*refs):
        piece_refs, out_hbm, sems = refs[:count], refs[count], refs[count + 1]
        rank = lax.axis_index("tensor")
        copies = []
        for step in range(count):
            place = pl.ds(pl.multiple_of(lax.rem(rank + count - steps[step], count) * rows, rows), rows)
            copies.append(pltpu.make_async_copy(piece_refs[step], out_hbm.at[place], sems.at[step]))
        for copy in copies:
            copy.start()
        for copy in copies:
            copy.wait()

    return on_chip(
        kernel,
        pieces,
        [VMEM] * count,
        [jax.ShapeDtypeStruct((count * rows, width), BF16)],
        [pltpu.SemaphoreType.DMA((count,))],
        out_specs=[HBM],
    )[0]


def swap(piece, axis, step):
    return lax.ppermute(piece, axis, [(i, i ^ step) for i in range(lax.axis_size(axis))])


def turn(piece, axis, step):
    count = lax.axis_size(axis)
    return lax.ppermute(piece, axis, [(i, (i + step) % count) for i in range(count)])


def local(
    prompt,
    key_value_weight,
    key_gain,
    prompt_blocks,
    block_owner,
    block_slot,
    queries,
    cache_keys,
    cache_values,
    new_keys,
    new_values,
    decode_lengths,
):
    tensor_count = lax.axis_size("tensor")
    near_states = swap(prompt[0], "section", 1)
    cosine, sine, states, table, weights, stats, row_queries, values = prepare(
        prompt[0], key_gain, block_owner, block_slot, prompt_blocks, queries, cache_keys, cache_values, decode_lengths
    )
    kept, *sent = place_rows(states, near_states, table)
    landed = [swap(half, "section", 3) for half in sent]
    steps = (0, 3, 2, 1)
    span, *span_codes = span_sums(weights, stats, values, kept, steps)
    span_shares = [swap(code, "tensor", step) for code, step in zip(span_codes, steps[1:])]
    begun = begin_rows(kept, landed[0], key_value_weight)
    own, far, near, mid = project_rows(begun, kept, landed[1], key_value_weight, (0, 3, 1, 2))
    far, near = swap(far, "tensor", 3), swap(near, "tensor", 1)
    mid = swap(hand_on(mid, span_shares), "tensor", 2)
    finished = finish_rows(add_shares(own, [far, near]), [mid], cosine, sine)
    pieces = [finished] + [turn(finished, "tensor", step) for step in steps[1:]]
    block_pool = join_rows(pieces, steps)
    attended = merge_spans(span, span_shares, row_queries, new_keys, new_values)
    return (attended, block_pool.reshape(1, CAP, BLK, -1))


def solution(mesh):
    in_specs = (
        P(("parts", "section"), None, "tensor"),
        P("tensor", None),
        P(),
        P("parts"),
        P("parts"),
        P("parts"),
        P(("parts", "section"), None),
        P(("parts", "section"), "tensor", None),
        P(("parts", "section"), "tensor", None),
        P(("parts", "section"), None),
        P(("parts", "section"), None),
        P(("parts", "section")),
    )
    out_specs = (P(("parts", "section"), "tensor"), P(("parts", "section"), None, None, None))
    tensor_count = mesh.shape["tensor"]
    whole_tiles = tensor_count == 4 and mesh.shape["section"] == 4
    program = local if whole_tiles else local_small_shares
    return jax.shard_map(program, mesh=mesh, in_specs=in_specs, out_specs=out_specs, check_vma=False)
```

```python
import math

import jax
import jax.numpy as jnp
from jax import lax
from jax.experimental import pallas as pl
from jax.experimental.pallas import tpu as pltpu
from jax.sharding import PartitionSpec as P

H = 64
KVH = 8
HD = 128
BLK = 16
SPAN = 128
KVW = 1024
G = 8
NB = 16
CAP = 4


NORM_EPSILON = 1e-06
ROPE_BASE = 1000000.0
MASKED_SCORE = -1e30


def exchange(pieces, axis):
    count = lax.axis_size(axis)
    rank = lax.axis_index(axis)
    landed = [lax.dynamic_index_in_dim(pieces, rank, 0, keepdims=False)]
    for step in range(1, count):
        piece = lax.dynamic_index_in_dim(pieces, rank ^ step, 0, keepdims=False)
        landed.append(lax.ppermute(piece, axis, [(i, i ^ step) for i in range(count)]))
    return landed


def collected(own, axis):
    count = lax.axis_size(axis)
    rank = lax.axis_index(axis)
    landed = [own]
    for step in range(1, count):
        landed.append(lax.ppermute(own, axis, [(i, i ^ step) for i in range(count)]))
    stacked = jnp.zeros((count,) + own.shape, own.dtype)
    for step, piece in enumerate(landed):
        stacked = lax.dynamic_update_index_in_dim(stacked, piece, rank ^ step, 0)
    return stacked


def rows_for_groups(states, block_owner, block_slot, group_count):
    slot_ids = jnp.arange(group_count * CAP, dtype=jnp.int32)
    selector = (block_owner * CAP + block_slot)[None, :] == slot_ids[:, None]
    filled = jnp.any(selector, axis=1)
    source = jnp.argmax(selector, axis=1)
    blocks = states.reshape(NB, BLK, states.shape[1])
    chosen = jnp.where(filled[:, None, None], blocks[source], jnp.zeros((), states.dtype))
    return chosen.reshape(group_count, CAP * BLK, states.shape[1])


def spread(rows, axis):
    count = lax.axis_size(axis)
    landed = jnp.where(lax.axis_index(axis) == 0, rows[0], jnp.zeros_like(rows[0]))
    for k in range(1, count):
        landed = landed + lax.ppermute(rows[k], axis, [(0, k)])
    return landed


def slot_positions(prompt_blocks, block_owner, block_slot, group_index):
    prompt_ends = jnp.cumsum(prompt_blocks)
    prompt_starts = prompt_ends - prompt_blocks
    slot_ids = jnp.arange(CAP, dtype=jnp.int32)
    selector = (block_owner[None, :] == group_index) & (block_slot[None, :] == slot_ids[:, None])
    block = jnp.sum(jnp.where(selector, jnp.arange(NB, dtype=jnp.int32)[None, :], 0), axis=1)
    inside = (block[:, None] >= prompt_starts[None, :]) & (block[:, None] < prompt_ends[None, :])
    first = jnp.sum(jnp.where(inside, prompt_starts[None, :], 0), axis=1)
    return (((block - first) * BLK)[:, None] + jnp.arange(BLK, dtype=jnp.int32)[None, :]).reshape(-1)


def finish_keys(projected, positions, key_gain):
    token_count = projected.shape[0]
    key_heads = projected[:, :KVW].reshape(token_count, KVH, HD)
    inv_root = lax.rsqrt(jnp.mean(key_heads * key_heads, axis=-1, keepdims=True) + NORM_EPSILON)
    key_heads = key_heads * inv_root * key_gain
    half_dim = HD // 2
    frequency = ROPE_BASE ** (jnp.arange(half_dim, dtype=jnp.float32) * (-2.0 / HD))
    angles = positions.astype(jnp.float32)[:, None, None] * frequency[None, None, :]
    cosine = jnp.cos(angles)
    sine_part = jnp.sin(angles)
    lower_half = key_heads[..., :half_dim]
    upper_half = key_heads[..., half_dim:]
    rotated = jnp.concatenate(
        [
            lower_half * cosine - upper_half * sine_part,
            upper_half * cosine + lower_half * sine_part,
        ],
        axis=-1,
    )
    return jnp.concatenate([rotated.reshape(token_count, KVW), projected[:, KVW:]], axis=1).astype(
        jnp.bfloat16
    )


def partial_attention(queries, cache_keys, cache_values, decode_lengths, first_position):
    row_count = queries.shape[0]
    local_len = cache_keys.shape[1]
    span_count = local_len // SPAN
    query_heads = queries.reshape(row_count, KVH, G, HD)
    key_heads = cache_keys.reshape(row_count, local_len, KVH, HD)
    scores = jnp.einsum(
        "rkgd,rpkd->rkgp", query_heads, key_heads, preferred_element_type=jnp.float32
    ) * HD ** (-0.5)
    live_mask = (first_position + jnp.arange(local_len, dtype=jnp.int32))[None, :] < decode_lengths[
        :, None
    ]
    scores = jnp.where(live_mask[:, None, None, :], scores, MASKED_SCORE)
    spans = scores.reshape(row_count, KVH, G, span_count, SPAN)
    span_max = jnp.max(spans, axis=-1)
    live_spans = live_mask.reshape(row_count, 1, 1, span_count, SPAN)
    weights = jnp.where(live_spans, jnp.exp(spans - span_max[..., None]), 0.0)
    span_sum = jnp.sum(weights, axis=-1)
    value_spans = cache_values.reshape(row_count, span_count, SPAN, KVH, HD)
    span_out = jnp.einsum(
        "rkgns,rnskd->rkgnd",
        weights.astype(jnp.bfloat16),
        value_spans,
        preferred_element_type=jnp.float32,
    )
    row_peak = jnp.max(span_max, axis=-1)
    factor = jnp.exp(span_max - row_peak[..., None])
    partial_out = jnp.sum(span_out * factor[..., None], axis=3)
    partial_sum = jnp.sum(span_sum * factor, axis=-1)
    return (
        partial_out.reshape(row_count, H, HD),
        row_peak.reshape(row_count, H),
        partial_sum.reshape(row_count, H),
    )


def combine_partials(former, latter):
    former_out, former_peak, former_sum = former
    latter_out, latter_peak, latter_sum = latter
    highest = jnp.maximum(former_peak, latter_peak)
    former_factor = jnp.exp(former_peak - highest)
    latter_factor = jnp.exp(latter_peak - highest)
    merged_out = former_out * former_factor[..., None] + latter_out * latter_factor[..., None]
    return (merged_out, highest, former_sum * former_factor + latter_sum * latter_factor)


def finish_heads(
    own_out, own_peak, own_sum, queries, new_keys, new_values, tensor_rank, heads_here
):
    row_count = queries.shape[0]
    own_width = heads_here * HD
    own_queries = (
        lax.dynamic_slice_in_dim(queries, tensor_rank * own_width, own_width, 1)
        .reshape(row_count, heads_here, HD)
        .astype(jnp.float32)
    )
    head_ids = tensor_rank * heads_here + jnp.arange(heads_here, dtype=jnp.int32)
    selector = (head_ids[:, None] // G == jnp.arange(KVH, dtype=jnp.int32)[None, :]).astype(
        jnp.float32
    )
    own_keys = jnp.einsum(
        "jk,rkd->rjd",
        selector,
        new_keys.reshape(row_count, KVH, HD).astype(jnp.float32),
        precision=lax.Precision.HIGHEST,
    )
    own_values = jnp.einsum(
        "jk,rkd->rjd",
        selector,
        new_values.reshape(row_count, KVH, HD).astype(jnp.float32),
        precision=lax.Precision.HIGHEST,
    )
    self_score = jnp.sum(own_queries * own_keys, axis=-1) * HD ** (-0.5)
    row_peak = jnp.maximum(own_peak, self_score)
    factor = jnp.exp(own_peak - row_peak)
    self_weight = jnp.exp(self_score - row_peak)
    numerator = own_out * factor[..., None] + self_weight[..., None] * own_values
    denominator = own_sum * factor + self_weight
    return (numerator / denominator[..., None]).reshape(row_count, own_width).astype(jnp.bfloat16)


def local_small_shares(
    prompt,
    key_value_weight,
    key_gain,
    prompt_blocks,
    block_owner,
    block_slot,
    queries,
    cache_keys,
    cache_values,
    new_keys,
    new_values,
    decode_lengths,
):
    tensor_count = lax.axis_size("tensor")
    tensor_rank = lax.axis_index("tensor")
    group_index = lax.axis_index("section")
    group_count = lax.axis_size("section")
    slot_rows = CAP * BLK
    rows_here = slot_rows // tensor_count
    rows = rows_for_groups(prompt[0], block_owner, block_slot, group_count)
    own_rows = spread(rows, "section")
    local_len = cache_keys.shape[1]
    row_count = queries.shape[0]
    heads_here = H // tensor_count
    partial_out, partial_peak, partial_sum = partial_attention(
        queries, cache_keys, cache_values, decode_lengths, tensor_rank * local_len
    )
    stats = jnp.stack([partial_peak, partial_sum], axis=-1).reshape(row_count, tensor_count, heads_here, 2)
    outs = partial_out.reshape(row_count, tensor_count, heads_here, HD)
    packed = jnp.concatenate([outs, jnp.pad(stats, ((0, 0), (0, 0), (0, 0), (0, HD - 2)))], axis=-1)
    shares = exchange(packed.transpose(1, 0, 2, 3), "tensor")
    merged = (shares[0][..., :HD], shares[0][..., HD], shares[0][..., HD + 1])
    for share in shares[1:]:
        merged = combine_partials(merged, (share[..., :HD], share[..., HD], share[..., HD + 1]))
    own_out, own_peak, own_sum = merged
    partial_terms = jnp.dot(own_rows, key_value_weight, preferred_element_type=jnp.float32)
    terms = exchange(partial_terms.reshape(tensor_count, rows_here, -1), "tensor")
    summed = sum(terms[1:], terms[0])
    positions = lax.dynamic_slice_in_dim(
        slot_positions(prompt_blocks, block_owner, block_slot, group_index), tensor_rank * rows_here, rows_here, 0
    )
    prompt_kv = finish_keys(summed, positions, key_gain)
    block_pool = collected(prompt_kv, "tensor").reshape(1, CAP, BLK, -1)
    attended = finish_heads(
        own_out, own_peak, own_sum, queries, new_keys, new_values, tensor_rank, heads_here
    )
    return (attended, block_pool)


VMEM = pl.BlockSpec(memory_space=pltpu.VMEM)
HBM = pl.BlockSpec(memory_space=pltpu.HBM)
F32 = jnp.float32
BF16 = jnp.bfloat16
I16 = jnp.int16
TOP = 32000.0
OCTAVE = 256.0
LN2 = math.log(2.0)
TINY = 1e-30
LEVELS = 64


def on_chip(kernel, operands, in_specs, out_shapes, scratch=(), out_specs=None, flops=0, moved=0):
    return pl.pallas_call(
        kernel,
        out_shape=out_shapes,
        in_specs=in_specs,
        out_specs=out_specs or [VMEM] * len(out_shapes),
        scratch_shapes=list(scratch),
        compiler_params=pltpu.CompilerParams(vmem_limit_bytes=40 * 1024 * 1024),
        cost_estimate=pl.CostEstimate(flops=flops, bytes_accessed=moved, transcendentals=0),
    )(*operands)


def stays(array):
    return pltpu.with_memory_space_constraint(array, pltpu.HBM)


def level_of(peak):
    return jnp.ceil(jnp.log(jnp.maximum(peak, TINY)) * (OCTAVE / LN2))


def as_int16(value):
    return jnp.round(value).astype(jnp.int32).astype(I16)


def as_float(value):
    return value.astype(jnp.int32).astype(F32)


def prepare(
    states, key_gain, block_owner, block_slot, prompt_blocks, queries, cache_keys, cache_values, decode_lengths
):
    token_count = states.shape[0]
    rows_here = CAP * BLK // lax.axis_size("tensor")
    slots_here = rows_here // BLK
    prompt_count = prompt_blocks.shape[0]
    row_count, local_len = cache_keys.shape[0], cache_keys.shape[1]
    fetched = [block_owner, block_slot, prompt_blocks, decode_lengths, key_gain[None, :], queries, cache_keys]
    count = len(fetched)

    def kernel(*refs):
        sources, states_hbm, value_hbm = refs[:count], refs[count], refs[count + 1]
        outs, rest = refs[count + 2 : count + 10], refs[count + 10 :]
        cosine_ref, sine_ref, states_ref, table_ref, weight_ref, stats_ref, query_ref, value_ref = outs
        held, (source, scores, sems) = rest[:count], rest[count:]
        owner, slot, prompts, length, gain, packed, keys = held
        pairs = [*zip(sources, held), (states_hbm, states_ref), (value_hbm, value_ref)]
        copies = [pltpu.make_async_copy(s, d, sems.at[i]) for i, (s, d) in enumerate(pairs)]
        for copy in copies:
            copy.start()
        group = lax.axis_index("section")
        rank = lax.axis_index("tensor")
        core = lax.rem(group, 2)
        for copy in copies[:6]:
            copy.wait()

        for j in range(2 * CAP):
            source[j] = -1
        for b in range(NB):

            @pl.when(owner[b] == core)
            def _():
                source[slot[b]] = b

            @pl.when(owner[b] == 3 - core)
            def _():
                source[CAP + slot[b]] = b

        token = lax.broadcasted_iota(jnp.int32, (BLK, token_count), 1)
        inner = lax.broadcasted_iota(jnp.int32, (BLK, token_count), 0)
        for j in range(2 * CAP):
            chosen = token == source[j] * BLK + inner
            table_ref[pl.ds(j * BLK, BLK), :] = jnp.where(chosen, 1.0, 0.0).astype(BF16)

        lane = lax.broadcasted_iota(jnp.int32, (BLK, HD), 1)
        row = lax.broadcasted_iota(jnp.int32, (BLK, HD), 0)
        half = lax.rem(lane, HD // 2).astype(F32)
        frequency = jnp.exp(half * (-2.0 / HD * math.log(ROPE_BASE)))
        far_gain = pltpu.roll(jnp.broadcast_to(gain[...], (8, HD)), HD // 2, 1)[0:1]
        for s in range(slots_here):
            block = 0
            for b in range(NB):
                block = jnp.where((owner[b] == group) & (slot[b] == rank * slots_here + s), b, block)
            first, begin = 0, 0
            for j in range(prompt_count):
                first = jnp.where(block >= begin, begin, first)
                begin = begin + prompts[j]
            angles = ((block - first) * BLK + row).astype(F32) * frequency
            cosine_ref[pl.ds(s * BLK, BLK), :] = jnp.cos(angles) * gain[...]
            sine = jnp.sin(angles) * far_gain
            sine_ref[pl.ds(s * BLK, BLK), :] = jnp.where(lane < HD // 2, -sine, sine)

        for h in range(H):
            piece = packed[:, pl.ds(h * HD, HD)].astype(F32)
            query_ref[pl.ds(h, row_count, stride=H), :] = piece
        copies[6].wait()
        for r in range(row_count):
            for pair in range(KVH // 2):
                pair_queries = query_ref[pl.ds(r * H + pair * 2 * G, 2 * G), :].astype(BF16)
                for n in (2 * pair, 2 * pair + 1):
                    both = lax.dot_general(
                        pair_queries,
                        keys[r, :, n * HD : (n + 1) * HD],
                        (((1,), (1,)), ((), ())),
                        preferred_element_type=F32,
                    )
                    scores[r, pl.ds(n * G, G), :] = both[(n % 2) * G : (n % 2 + 1) * G]
        place = lax.broadcasted_iota(jnp.int32, (H, local_len), 1) + rank * local_len
        column = lax.broadcasted_iota(jnp.int32, (H, HD), 1)
        stats = jnp.zeros((H, HD), F32)
        for r in range(row_count):
            live = place < length[r]
            row_scores = jnp.where(live, scores[r] * HD ** (-0.5), MASKED_SCORE)
            peak = jnp.max(row_scores, axis=1, keepdims=True)
            weight = jnp.where(live, jnp.exp(row_scores - peak), 0.0)
            total = jnp.sum(weight, axis=1, keepdims=True)
            weight_ref[r] = weight.astype(BF16)
            stats = jnp.where(column == r, peak, stats)
            stats = jnp.where(column == row_count + r, total, stats)
        stats_ref[...] = stats
        copies[count].wait()
        copies[count + 1].wait()

    return on_chip(
        kernel,
        [stays(array) for array in (*fetched, states, cache_values)],
        [HBM] * (count + 2),
        [
            jax.ShapeDtypeStruct((rows_here, HD), F32),
            jax.ShapeDtypeStruct((rows_here, HD), F32),
            jax.ShapeDtypeStruct(states.shape, BF16),
            jax.ShapeDtypeStruct((2 * CAP * BLK, token_count), BF16),
            jax.ShapeDtypeStruct((row_count, H, local_len), BF16),
            jax.ShapeDtypeStruct((H, HD), F32),
            jax.ShapeDtypeStruct((row_count * H, HD), F32),
            jax.ShapeDtypeStruct(cache_values.shape, BF16),
        ],
        [pltpu.SMEM(array.shape, jnp.int32) for array in fetched[:4]]
        + [pltpu.VMEM(array.shape, array.dtype) for array in fetched[4:]]
        + [
            pltpu.SMEM((2 * CAP,), jnp.int32),
            pltpu.VMEM((row_count, H, local_len), F32),
            pltpu.SemaphoreType.DMA((count + 2,)),
        ],
        flops=2 * row_count * H * HD * local_len,
        moved=2 * (states.size + cache_keys.size + cache_values.size),
    )


def place_rows(own_states, near_states, table):
    width = own_states.shape[1]
    rows = CAP * BLK

    def kernel(own_ref, near_ref, table_ref, keep_ref, send_ref):
        core = lax.rem(lax.axis_index("section"), 2)

        def place(states):
            placed = jnp.dot(table_ref[...], states[...], preferred_element_type=F32).astype(BF16)
            keep_ref[...] = placed[:rows]
            send_ref[...] = placed[rows:]

        @pl.when(core == 0)
        def _():
            place(own_ref)

        @pl.when(core == 1)
        def _():
            place(near_ref)

    return on_chip(
        kernel,
        (own_states, near_states, table),
        [VMEM] * 3,
        [jax.ShapeDtypeStruct((rows, width), BF16)] * 2,
        moved=own_states.size * 2,
    )


def span_sums(weights, stats, values, after, steps):
    row_count, _, local_len = weights.shape
    width = row_count * HD
    heads_here = H // len(steps)

    def kernel(weight_ref, stats_ref, value_ref, after_ref, span_ref, *refs):
        share_refs, code = refs[:-1], refs[-1]
        rank = lax.axis_index("tensor")
        column = lax.broadcasted_iota(jnp.int32, (H, HD), 1)
        for r in range(row_count):
            for pair in range(KVH // 2):
                pair_weights = weight_ref[r, pl.ds(pair * 2 * G, 2 * G), :]
                for n in (2 * pair, 2 * pair + 1):
                    both = jnp.dot(
                        pair_weights, value_ref[r, :, n * HD : (n + 1) * HD], preferred_element_type=F32
                    )
                    span_ref[pl.ds(n * G, G), pl.ds(r * HD, HD)] = both[(n % 2) * G : (n % 2 + 1) * G]
        stats = stats_ref[...]
        span_ref[:, pl.ds(width, HD)] = stats
        levels = jnp.zeros((H, HD), F32)
        for r in range(row_count):
            peak = jnp.max(jnp.abs(span_ref[:, pl.ds(r * HD, HD)]), axis=1, keepdims=True)
            levels = jnp.where(column == r, peak, levels)
        levels = level_of(levels)
        scale = TOP * jnp.exp(levels * (-LN2 / OCTAVE))
        for r in range(row_count):
            code[:, pl.ds(r * HD, HD)] = as_int16(span_ref[:, pl.ds(r * HD, HD)] * scale[:, r : r + 1])
        peaks = jnp.maximum(stats, -TOP)
        fine = jnp.where(column < row_count, peaks, stats * HD)
        whole = jnp.floor(fine)
        part = (fine - whole) * TOP
        coded = jnp.where(column < 2 * row_count, whole, 0.0)
        shifted = pltpu.roll(jnp.where(column < 2 * row_count, part, 0.0), 2 * row_count, 1)
        moved = pltpu.roll(jnp.where(column < row_count, levels, 0.0), 4 * row_count, 1)
        code[:, pl.ds(width, HD)] = as_int16(coded + shifted + moved)
        for k, step in enumerate(steps[1:]):
            start = pl.multiple_of((rank ^ step) * heads_here, heads_here)
            share_refs[k][...] = code[pl.ds(start, heads_here), :]

    return on_chip(
        kernel,
        [weights, stats, values, after],
        [VMEM] * 3 + [pl.BlockSpec(memory_space=pl.ANY)],
        [jax.ShapeDtypeStruct((H, width + HD), F32)]
        + [jax.ShapeDtypeStruct((heads_here, width + HD), I16)] * (len(steps) - 1),
        [pltpu.VMEM((H, width + HD), I16)],
        flops=2 * row_count * H * HD * local_len,
        moved=12 * values.size,
    )


def project_rows(kept, landed, weight, steps):
    slot_rows, depth = landed.shape
    width = weight.shape[1]
    rows_here = slot_rows // len(steps)
    share_width = width + HD
    step_width = 256

    def kernel(kept_ref, landed_ref, weight_ref, own_ref, *refs):
        share_refs, (held, code) = refs[:-2], refs[-2:]
        far = lax.axis_index("section") >= 2
        rank = lax.axis_index("tensor")
        rows = jnp.where(far, landed_ref[...], kept_ref[...])
        lane = lax.broadcasted_iota(jnp.int32, (slot_rows, HD), 1)
        levels = jnp.zeros((slot_rows, HD), F32)
        for c in range(0, width, step_width):
            product = jnp.dot(rows, weight_ref[:, pl.ds(c, step_width)], preferred_element_type=F32)
            held[:, c : c + step_width] = product
            for m in range(0, step_width, HD):
                tile = product[:, m : m + HD]
                level = level_of(jnp.max(jnp.abs(tile), axis=1, keepdims=True))
                levels = jnp.where(lane == LEVELS + (c + m) // HD, level, levels)
                scaled = tile * (TOP * jnp.exp(level * (-LN2 / OCTAVE)))
                code[:, c + m : c + m + HD] = as_int16(scaled)
        code[:, width:] = as_int16(levels)

        def rows_of(step):
            return pl.ds(pl.multiple_of((rank ^ step) * rows_here, rows_here), rows_here)

        own_ref[...] = held[rows_of(0), :]
        for k, step in enumerate(steps[1:]):
            levels_code = code[rows_of(step), pl.ds(width, HD)]
            share_refs[k][:, pl.ds(0, width)] = code[rows_of(step), pl.ds(0, width)]
            share_refs[k][:, pl.ds(width, HD)] = levels_code

    return on_chip(
        kernel,
        (kept, landed, weight),
        [VMEM] * 3,
        [jax.ShapeDtypeStruct((rows_here, width), F32)]
        + [jax.ShapeDtypeStruct((rows_here, share_width), I16)] * (len(steps) - 1),
        [pltpu.VMEM((slot_rows, width), F32), pltpu.VMEM((slot_rows, width + HD), I16)],
        flops=2 * slot_rows * depth * width,
        moved=2 * weight.size,
    )


def hand_on(piece, ahead):
    count = len(ahead)

    def kernel(piece_ref, *refs):
        refs[count][...] = piece_ref[...]

    return on_chip(
        kernel,
        (piece, *ahead),
        [VMEM] + [pl.BlockSpec(memory_space=pl.ANY)] * count,
        [jax.ShapeDtypeStruct(piece.shape, piece.dtype)],
    )[0]


def add_shares(total, shares):
    rows, width = total.shape
    count = len(shares)

    def kernel(total_ref, *refs):
        share_refs, out_ref = refs[:count], refs[count]
        scales = [
            jnp.exp(as_float(ref[:, pl.ds(ref.shape[1] - HD, HD)]) * (LN2 / OCTAVE)) * (1.0 / TOP)
            for ref in share_refs
        ]
        for n in range(width // HD):
            columns = pl.ds(n * HD, HD)
            part = total_ref[:, columns]
            for ref, scale in zip(share_refs, scales):
                part = part + as_float(ref[:, columns]) * scale[:, LEVELS + n : LEVELS + n + 1]
            out_ref[:, columns] = part

    return on_chip(
        kernel, (total, *shares), [VMEM] * (count + 1), [jax.ShapeDtypeStruct((rows, width), F32)]
    )[0]


def finish_rows(own, shares, cosine, sine):
    rows, width = own.shape
    share_count = len(shares)

    def kernel(own_ref, *refs):
        share_refs = refs[:share_count]
        cosine_ref, sine_ref, out_ref = refs[share_count:]
        scales = [
            jnp.exp(as_float(ref[:, pl.ds(ref.shape[1] - HD, HD)]) * (LN2 / OCTAVE)) * (1.0 / TOP)
            for ref in share_refs
        ]
        for n in range(width // HD):
            columns = pl.ds(n * HD, HD)
            total = own_ref[:, columns]
            for ref, scale in zip(share_refs, scales):
                total = total + as_float(ref[:, columns]) * scale[:, LEVELS + n : LEVELS + n + 1]
            if n < KVH:
                mean = jnp.sum(total * total, axis=1, keepdims=True) * (1.0 / HD)
                total = total * cosine_ref[...] + pltpu.roll(total, HD // 2, 1) * sine_ref[...]
                total = total * lax.rsqrt(mean + NORM_EPSILON)
            out_ref[:, columns] = total.astype(BF16)

    return on_chip(
        kernel,
        (own, *shares, cosine, sine),
        [VMEM] * (share_count + 3),
        [jax.ShapeDtypeStruct((rows, width), BF16)],
    )[0]


def merge_spans(span, shares, queries, new_keys, new_values):
    row_count = new_keys.shape[0]
    share_count = len(shares)
    heads_here = shares[0].shape[0]
    keys_here = heads_here // G
    width = row_count * HD

    def kernel(span_ref, *refs):
        share_refs = refs[:share_count]
        query_ref, key_ref, value_ref, out_ref = refs[share_count:]
        rank = lax.axis_index("tensor")
        heads = pl.ds(pl.multiple_of(rank * heads_here, heads_here), heads_here)
        columns = pl.ds(pl.multiple_of(rank * keys_here * HD, HD), keys_here * HD)
        new_key, new_value = key_ref[:, columns].astype(F32), value_ref[:, columns].astype(F32)

        def spread(tile, r):
            return jnp.concatenate(
                [
                    jnp.broadcast_to(tile[r : r + 1, kk * HD : (kk + 1) * HD], (G, HD))
                    for kk in range(keys_here)
                ],
                axis=0,
            )

        stats, scales = [span_ref[heads, pl.ds(width, HD)]], []
        for ref in share_refs:
            code = as_float(ref[:, pl.ds(width, HD)])
            column = lax.broadcasted_iota(jnp.int32, code.shape, 1)
            fine = code + pltpu.roll(code, HD - 2 * row_count, 1) * (1.0 / TOP)
            stats.append(jnp.where(column < row_count, fine, fine * (1.0 / HD)))
            scales.append(jnp.exp(code * (LN2 / OCTAVE)) * (1.0 / TOP))

        def part(k, r):
            if k == 0:
                return span_ref[heads, pl.ds(r * HD, HD)]
            coded = as_float(share_refs[k - 1][:, pl.ds(r * HD, HD)])
            return coded * scales[k - 1][:, 4 * row_count + r : 4 * row_count + r + 1]

        for r in range(row_count):
            query = query_ref[pl.ds(pl.multiple_of(r * H + rank * heads_here, heads_here), heads_here), :]
            self_score = jnp.sum(query * spread(new_key, r), axis=1, keepdims=True) * HD ** (-0.5)
            row_peak = self_score
            for tile in stats:
                row_peak = jnp.maximum(row_peak, tile[:, r : r + 1])
            self_weight = jnp.exp(self_score - row_peak)
            numerator = self_weight * spread(new_value, r)
            denominator = self_weight
            for k, tile in enumerate(stats):
                factor = jnp.exp(tile[:, r : r + 1] - row_peak)
                numerator += factor * part(k, r)
                denominator += factor * tile[:, row_count + r : row_count + r + 1]
            out_ref[r] = (numerator / denominator).astype(BF16)

    attended = on_chip(
        kernel,
        (span, *shares, queries, new_keys, new_values),
        [VMEM] * (share_count + 4),
        [jax.ShapeDtypeStruct((row_count, heads_here, HD), BF16)],
    )[0]
    return attended.reshape(row_count, heads_here * HD)


def join_rows(pieces, steps):
    count = len(pieces)
    rows, width = pieces[0].shape

    def kernel(*refs):
        piece_refs, out_hbm, sems = refs[:count], refs[count], refs[count + 1]
        rank = lax.axis_index("tensor")
        copies = []
        for step in range(count):
            place = pl.ds(pl.multiple_of(lax.rem(rank + count - steps[step], count) * rows, rows), rows)
            copies.append(pltpu.make_async_copy(piece_refs[step], out_hbm.at[place], sems.at[step]))
        for copy in copies:
            copy.start()
        for copy in copies:
            copy.wait()

    return on_chip(
        kernel,
        pieces,
        [VMEM] * count,
        [jax.ShapeDtypeStruct((count * rows, width), BF16)],
        [pltpu.SemaphoreType.DMA((count,))],
        out_specs=[HBM],
    )[0]


def swap(piece, axis, step):
    return lax.ppermute(piece, axis, [(i, i ^ step) for i in range(lax.axis_size(axis))])


def turn(piece, axis, step):
    count = lax.axis_size(axis)
    return lax.ppermute(piece, axis, [(i, (i + step) % count) for i in range(count)])


def local(
    prompt,
    key_value_weight,
    key_gain,
    prompt_blocks,
    block_owner,
    block_slot,
    queries,
    cache_keys,
    cache_values,
    new_keys,
    new_values,
    decode_lengths,
):
    tensor_count = lax.axis_size("tensor")
    near_states = swap(prompt[0], "section", 1)
    cosine, sine, states, table, weights, stats, row_queries, values = prepare(
        prompt[0], key_gain, block_owner, block_slot, prompt_blocks, queries, cache_keys, cache_values, decode_lengths
    )
    kept, sent = place_rows(states, near_states, table)
    landed = swap(sent, "section", 3)
    steps = (0, 3, 2, 1)
    span, *span_codes = span_sums(weights, stats, values, kept, steps)
    span_shares = [swap(code, "tensor", step) for code, step in zip(span_codes, steps[1:])]
    own, far, near, mid = project_rows(kept, landed, key_value_weight, (0, 3, 1, 2))
    far, near = swap(far, "tensor", 3), swap(near, "tensor", 1)
    mid = swap(hand_on(mid, span_shares), "tensor", 2)
    finished = finish_rows(add_shares(own, [far, near]), [mid], cosine, sine)
    pieces = [finished] + [turn(finished, "tensor", step) for step in steps[1:]]
    block_pool = join_rows(pieces, steps)
    attended = merge_spans(span, span_shares, row_queries, new_keys, new_values)
    return (attended, block_pool.reshape(1, CAP, BLK, -1))


def solution(mesh):
    in_specs = (
        P(("parts", "section"), None, "tensor"),
        P("tensor", None),
        P(),
        P("parts"),
        P("parts"),
        P("parts"),
        P(("parts", "section"), None),
        P(("parts", "section"), "tensor", None),
        P(("parts", "section"), "tensor", None),
        P(("parts", "section"), None),
        P(("parts", "section"), None),
        P(("parts", "section")),
    )
    out_specs = (P(("parts", "section"), "tensor"), P(("parts", "section"), None, None, None))
    tensor_count = mesh.shape["tensor"]
    whole_tiles = tensor_count == 4 and mesh.shape["section"] == 4
    program = local if whole_tiles else local_small_shares
    return jax.shard_map(program, mesh=mesh, in_specs=in_specs, out_specs=out_specs, check_vma=False)
```

```python
import math

import jax
import jax.numpy as jnp
from jax import lax
from jax.experimental import pallas as pl
from jax.experimental.pallas import tpu as pltpu
from jax.sharding import PartitionSpec as P

H = 64
KVH = 8
HD = 128
BLK = 16
SPAN = 128
KVW = 1024
G = 8
NB = 16
CAP = 4


NORM_EPSILON = 1e-06
ROPE_BASE = 1000000.0
MASKED_SCORE = -1e30


def exchange(pieces, axis):
    count = lax.axis_size(axis)
    rank = lax.axis_index(axis)
    landed = [lax.dynamic_index_in_dim(pieces, rank, 0, keepdims=False)]
    for step in range(1, count):
        piece = lax.dynamic_index_in_dim(pieces, rank ^ step, 0, keepdims=False)
        landed.append(lax.ppermute(piece, axis, [(i, i ^ step) for i in range(count)]))
    return landed


def collected(own, axis):
    count = lax.axis_size(axis)
    rank = lax.axis_index(axis)
    landed = [own]
    for step in range(1, count):
        landed.append(lax.ppermute(own, axis, [(i, i ^ step) for i in range(count)]))
    stacked = jnp.zeros((count,) + own.shape, own.dtype)
    for step, piece in enumerate(landed):
        stacked = lax.dynamic_update_index_in_dim(stacked, piece, rank ^ step, 0)
    return stacked


def rows_for_groups(states, block_owner, block_slot, group_count):
    slot_ids = jnp.arange(group_count * CAP, dtype=jnp.int32)
    selector = (block_owner * CAP + block_slot)[None, :] == slot_ids[:, None]
    filled = jnp.any(selector, axis=1)
    source = jnp.argmax(selector, axis=1)
    blocks = states.reshape(NB, BLK, states.shape[1])
    chosen = jnp.where(filled[:, None, None], blocks[source], jnp.zeros((), states.dtype))
    return chosen.reshape(group_count, CAP * BLK, states.shape[1])


def spread(rows, axis):
    count = lax.axis_size(axis)
    landed = jnp.where(lax.axis_index(axis) == 0, rows[0], jnp.zeros_like(rows[0]))
    for k in range(1, count):
        landed = landed + lax.ppermute(rows[k], axis, [(0, k)])
    return landed


def slot_positions(prompt_blocks, block_owner, block_slot, group_index):
    prompt_ends = jnp.cumsum(prompt_blocks)
    prompt_starts = prompt_ends - prompt_blocks
    slot_ids = jnp.arange(CAP, dtype=jnp.int32)
    selector = (block_owner[None, :] == group_index) & (block_slot[None, :] == slot_ids[:, None])
    block = jnp.sum(jnp.where(selector, jnp.arange(NB, dtype=jnp.int32)[None, :], 0), axis=1)
    inside = (block[:, None] >= prompt_starts[None, :]) & (block[:, None] < prompt_ends[None, :])
    first = jnp.sum(jnp.where(inside, prompt_starts[None, :], 0), axis=1)
    return (((block - first) * BLK)[:, None] + jnp.arange(BLK, dtype=jnp.int32)[None, :]).reshape(-1)


def finish_keys(projected, positions, key_gain):
    token_count = projected.shape[0]
    key_heads = projected[:, :KVW].reshape(token_count, KVH, HD)
    inv_root = lax.rsqrt(jnp.mean(key_heads * key_heads, axis=-1, keepdims=True) + NORM_EPSILON)
    key_heads = key_heads * inv_root * key_gain
    half_dim = HD // 2
    frequency = ROPE_BASE ** (jnp.arange(half_dim, dtype=jnp.float32) * (-2.0 / HD))
    angles = positions.astype(jnp.float32)[:, None, None] * frequency[None, None, :]
    cosine = jnp.cos(angles)
    sine_part = jnp.sin(angles)
    lower_half = key_heads[..., :half_dim]
    upper_half = key_heads[..., half_dim:]
    rotated = jnp.concatenate(
        [
            lower_half * cosine - upper_half * sine_part,
            upper_half * cosine + lower_half * sine_part,
        ],
        axis=-1,
    )
    return jnp.concatenate([rotated.reshape(token_count, KVW), projected[:, KVW:]], axis=1).astype(
        jnp.bfloat16
    )


def partial_attention(queries, cache_keys, cache_values, decode_lengths, first_position):
    row_count = queries.shape[0]
    local_len = cache_keys.shape[1]
    span_count = local_len // SPAN
    query_heads = queries.reshape(row_count, KVH, G, HD)
    key_heads = cache_keys.reshape(row_count, local_len, KVH, HD)
    scores = jnp.einsum(
        "rkgd,rpkd->rkgp", query_heads, key_heads, preferred_element_type=jnp.float32
    ) * HD ** (-0.5)
    live_mask = (first_position + jnp.arange(local_len, dtype=jnp.int32))[None, :] < decode_lengths[
        :, None
    ]
    scores = jnp.where(live_mask[:, None, None, :], scores, MASKED_SCORE)
    spans = scores.reshape(row_count, KVH, G, span_count, SPAN)
    span_max = jnp.max(spans, axis=-1)
    live_spans = live_mask.reshape(row_count, 1, 1, span_count, SPAN)
    weights = jnp.where(live_spans, jnp.exp(spans - span_max[..., None]), 0.0)
    span_sum = jnp.sum(weights, axis=-1)
    value_spans = cache_values.reshape(row_count, span_count, SPAN, KVH, HD)
    span_out = jnp.einsum(
        "rkgns,rnskd->rkgnd",
        weights.astype(jnp.bfloat16),
        value_spans,
        preferred_element_type=jnp.float32,
    )
    row_peak = jnp.max(span_max, axis=-1)
    factor = jnp.exp(span_max - row_peak[..., None])
    partial_out = jnp.sum(span_out * factor[..., None], axis=3)
    partial_sum = jnp.sum(span_sum * factor, axis=-1)
    return (
        partial_out.reshape(row_count, H, HD),
        row_peak.reshape(row_count, H),
        partial_sum.reshape(row_count, H),
    )


def combine_partials(former, latter):
    former_out, former_peak, former_sum = former
    latter_out, latter_peak, latter_sum = latter
    highest = jnp.maximum(former_peak, latter_peak)
    former_factor = jnp.exp(former_peak - highest)
    latter_factor = jnp.exp(latter_peak - highest)
    merged_out = former_out * former_factor[..., None] + latter_out * latter_factor[..., None]
    return (merged_out, highest, former_sum * former_factor + latter_sum * latter_factor)


def finish_heads(
    own_out, own_peak, own_sum, queries, new_keys, new_values, tensor_rank, heads_here
):
    row_count = queries.shape[0]
    own_width = heads_here * HD
    own_queries = (
        lax.dynamic_slice_in_dim(queries, tensor_rank * own_width, own_width, 1)
        .reshape(row_count, heads_here, HD)
        .astype(jnp.float32)
    )
    head_ids = tensor_rank * heads_here + jnp.arange(heads_here, dtype=jnp.int32)
    selector = (head_ids[:, None] // G == jnp.arange(KVH, dtype=jnp.int32)[None, :]).astype(
        jnp.float32
    )
    own_keys = jnp.einsum(
        "jk,rkd->rjd",
        selector,
        new_keys.reshape(row_count, KVH, HD).astype(jnp.float32),
        precision=lax.Precision.HIGHEST,
    )
    own_values = jnp.einsum(
        "jk,rkd->rjd",
        selector,
        new_values.reshape(row_count, KVH, HD).astype(jnp.float32),
        precision=lax.Precision.HIGHEST,
    )
    self_score = jnp.sum(own_queries * own_keys, axis=-1) * HD ** (-0.5)
    row_peak = jnp.maximum(own_peak, self_score)
    factor = jnp.exp(own_peak - row_peak)
    self_weight = jnp.exp(self_score - row_peak)
    numerator = own_out * factor[..., None] + self_weight[..., None] * own_values
    denominator = own_sum * factor + self_weight
    return (numerator / denominator[..., None]).reshape(row_count, own_width).astype(jnp.bfloat16)


def local_small_shares(
    prompt,
    key_value_weight,
    key_gain,
    prompt_blocks,
    block_owner,
    block_slot,
    queries,
    cache_keys,
    cache_values,
    new_keys,
    new_values,
    decode_lengths,
):
    tensor_count = lax.axis_size("tensor")
    tensor_rank = lax.axis_index("tensor")
    group_index = lax.axis_index("section")
    group_count = lax.axis_size("section")
    slot_rows = CAP * BLK
    rows_here = slot_rows // tensor_count
    rows = rows_for_groups(prompt[0], block_owner, block_slot, group_count)
    own_rows = spread(rows, "section")
    local_len = cache_keys.shape[1]
    row_count = queries.shape[0]
    heads_here = H // tensor_count
    partial_out, partial_peak, partial_sum = partial_attention(
        queries, cache_keys, cache_values, decode_lengths, tensor_rank * local_len
    )
    stats = jnp.stack([partial_peak, partial_sum], axis=-1).reshape(row_count, tensor_count, heads_here, 2)
    outs = partial_out.reshape(row_count, tensor_count, heads_here, HD)
    packed = jnp.concatenate([outs, jnp.pad(stats, ((0, 0), (0, 0), (0, 0), (0, HD - 2)))], axis=-1)
    shares = exchange(packed.transpose(1, 0, 2, 3), "tensor")
    merged = (shares[0][..., :HD], shares[0][..., HD], shares[0][..., HD + 1])
    for share in shares[1:]:
        merged = combine_partials(merged, (share[..., :HD], share[..., HD], share[..., HD + 1]))
    own_out, own_peak, own_sum = merged
    partial_terms = jnp.dot(own_rows, key_value_weight, preferred_element_type=jnp.float32)
    terms = exchange(partial_terms.reshape(tensor_count, rows_here, -1), "tensor")
    summed = sum(terms[1:], terms[0])
    positions = lax.dynamic_slice_in_dim(
        slot_positions(prompt_blocks, block_owner, block_slot, group_index), tensor_rank * rows_here, rows_here, 0
    )
    prompt_kv = finish_keys(summed, positions, key_gain)
    block_pool = collected(prompt_kv, "tensor").reshape(1, CAP, BLK, -1)
    attended = finish_heads(
        own_out, own_peak, own_sum, queries, new_keys, new_values, tensor_rank, heads_here
    )
    return (attended, block_pool)


VMEM = pl.BlockSpec(memory_space=pltpu.VMEM)
HBM = pl.BlockSpec(memory_space=pltpu.HBM)
F32 = jnp.float32
BF16 = jnp.bfloat16
I16 = jnp.int16
TOP = 32000.0
OCTAVE = 256.0
LN2 = math.log(2.0)
TINY = 1e-30
LEVELS = 64


def on_chip(kernel, operands, in_specs, out_shapes, scratch=(), out_specs=None, flops=0, moved=0):
    return pl.pallas_call(
        kernel,
        out_shape=out_shapes,
        in_specs=in_specs,
        out_specs=out_specs or [VMEM] * len(out_shapes),
        scratch_shapes=list(scratch),
        compiler_params=pltpu.CompilerParams(vmem_limit_bytes=40 * 1024 * 1024),
        cost_estimate=pl.CostEstimate(flops=flops, bytes_accessed=moved, transcendentals=0),
    )(*operands)


def stays(array):
    return pltpu.with_memory_space_constraint(array, pltpu.HBM)


def level_of(peak):
    return jnp.ceil(jnp.log(jnp.maximum(peak, TINY)) * (OCTAVE / LN2))


def as_int16(value):
    return jnp.round(value).astype(jnp.int32).astype(I16)


def as_float(value):
    return value.astype(jnp.int32).astype(F32)


def prepare(
    states, key_gain, block_owner, block_slot, prompt_blocks, queries, cache_keys, cache_values, decode_lengths
):
    token_count = states.shape[0]
    rows_here = CAP * BLK // lax.axis_size("tensor")
    slots_here = rows_here // BLK
    prompt_count = prompt_blocks.shape[0]
    row_count, local_len = cache_keys.shape[0], cache_keys.shape[1]
    fetched = [block_owner, block_slot, prompt_blocks, decode_lengths, key_gain[None, :], queries, cache_keys]
    count = len(fetched)

    def kernel(*refs):
        sources, states_hbm, value_hbm = refs[:count], refs[count], refs[count + 1]
        outs, rest = refs[count + 2 : count + 10], refs[count + 10 :]
        cosine_ref, sine_ref, states_ref, table_ref, weight_ref, stats_ref, query_ref, value_ref = outs
        held, (source, sems) = rest[:count], rest[count:]
        owner, slot, prompts, length, gain, packed, keys = held
        pairs = [*zip(sources, held), (states_hbm, states_ref), (value_hbm, value_ref)]
        copies = [pltpu.make_async_copy(s, d, sems.at[i]) for i, (s, d) in enumerate(pairs)]
        for copy in copies:
            copy.start()
        group = lax.axis_index("section")
        rank = lax.axis_index("tensor")
        core = lax.rem(group, 2)
        for copy in copies[:6]:
            copy.wait()

        for j in range(2 * CAP):
            source[j] = -1
        for b in range(NB):

            @pl.when(owner[b] == core)
            def _():
                source[slot[b]] = b

            @pl.when(owner[b] == 3 - core)
            def _():
                source[CAP + slot[b]] = b

        token = lax.broadcasted_iota(jnp.int32, (BLK, token_count), 1)
        inner = lax.broadcasted_iota(jnp.int32, (BLK, token_count), 0)
        for j in range(2 * CAP):
            chosen = token == source[j] * BLK + inner
            table_ref[pl.ds(j * BLK, BLK), :] = jnp.where(chosen, 1.0, 0.0).astype(BF16)

        lane = lax.broadcasted_iota(jnp.int32, (BLK, HD), 1)
        row = lax.broadcasted_iota(jnp.int32, (BLK, HD), 0)
        half = lax.rem(lane, HD // 2).astype(F32)
        frequency = jnp.exp(half * (-2.0 / HD * math.log(ROPE_BASE)))
        far_gain = pltpu.roll(jnp.broadcast_to(gain[...], (8, HD)), HD // 2, 1)[0:1]
        for s in range(slots_here):
            block = 0
            for b in range(NB):
                block = jnp.where((owner[b] == group) & (slot[b] == rank * slots_here + s), b, block)
            first, begin = 0, 0
            for j in range(prompt_count):
                first = jnp.where(block >= begin, begin, first)
                begin = begin + prompts[j]
            angles = ((block - first) * BLK + row).astype(F32) * frequency
            cosine_ref[pl.ds(s * BLK, BLK), :] = jnp.cos(angles) * gain[...]
            sine = jnp.sin(angles) * far_gain
            sine_ref[pl.ds(s * BLK, BLK), :] = jnp.where(lane < HD // 2, -sine, sine)

        for h in range(H):
            piece = packed[:, pl.ds(h * HD, HD)].astype(F32)
            query_ref[pl.ds(h, row_count, stride=H), :] = piece
        copies[6].wait()
        place = lax.broadcasted_iota(jnp.int32, (H, local_len), 1) + rank * local_len
        column = lax.broadcasted_iota(jnp.int32, (H, HD), 1)
        stats = jnp.zeros((H, HD), F32)
        for r in range(row_count):
            parts = []
            for pair in range(KVH // 2):
                pair_queries = query_ref[pl.ds(r * H + pair * 2 * G, 2 * G), :].astype(BF16)
                for n in (2 * pair, 2 * pair + 1):
                    both = lax.dot_general(
                        pair_queries,
                        keys[r, :, n * HD : (n + 1) * HD],
                        (((1,), (1,)), ((), ())),
                        preferred_element_type=F32,
                    )
                    parts.append(both[(n % 2) * G : (n % 2 + 1) * G])
            live = place < length[r]
            row_scores = jnp.where(live, jnp.concatenate(parts, axis=0) * HD ** (-0.5), MASKED_SCORE)
            peak = jnp.max(row_scores, axis=1, keepdims=True)
            weight = jnp.where(live, jnp.exp(row_scores - peak), 0.0)
            total = jnp.sum(weight, axis=1, keepdims=True)
            weight_ref[r] = weight.astype(BF16)
            stats = jnp.where(column == r, peak, stats)
            stats = jnp.where(column == row_count + r, total, stats)
        stats_ref[...] = stats
        copies[count].wait()
        copies[count + 1].wait()

    return on_chip(
        kernel,
        [stays(array) for array in (*fetched, states, cache_values)],
        [HBM] * (count + 2),
        [
            jax.ShapeDtypeStruct((rows_here, HD), F32),
            jax.ShapeDtypeStruct((rows_here, HD), F32),
            jax.ShapeDtypeStruct(states.shape, BF16),
            jax.ShapeDtypeStruct((2 * CAP * BLK, token_count), BF16),
            jax.ShapeDtypeStruct((row_count, H, local_len), BF16),
            jax.ShapeDtypeStruct((H, HD), F32),
            jax.ShapeDtypeStruct((row_count * H, HD), F32),
            jax.ShapeDtypeStruct(cache_values.shape, BF16),
        ],
        [pltpu.SMEM(array.shape, jnp.int32) for array in fetched[:4]]
        + [pltpu.VMEM(array.shape, array.dtype) for array in fetched[4:]]
        + [
            pltpu.SMEM((2 * CAP,), jnp.int32),
            pltpu.SemaphoreType.DMA((count + 2,)),
        ],
        flops=2 * row_count * H * HD * local_len,
        moved=2 * (states.size + cache_keys.size + cache_values.size),
    )


def place_rows(own_states, near_states, table):
    width = own_states.shape[1]
    rows = CAP * BLK

    def kernel(own_ref, near_ref, table_ref, keep_ref, send_ref):
        core = lax.rem(lax.axis_index("section"), 2)

        def place(states):
            placed = jnp.dot(table_ref[...], states[...], preferred_element_type=F32).astype(BF16)
            keep_ref[...] = placed[:rows]
            send_ref[...] = placed[rows:]

        @pl.when(core == 0)
        def _():
            place(own_ref)

        @pl.when(core == 1)
        def _():
            place(near_ref)

    return on_chip(
        kernel,
        (own_states, near_states, table),
        [VMEM] * 3,
        [jax.ShapeDtypeStruct((rows, width), BF16)] * 2,
        moved=own_states.size * 2,
    )


def span_sums(weights, stats, values, after, steps):
    row_count, _, local_len = weights.shape
    width = row_count * HD
    heads_here = H // len(steps)

    def kernel(weight_ref, stats_ref, value_ref, after_ref, span_ref, *refs):
        share_refs, code = refs[:-1], refs[-1]
        rank = lax.axis_index("tensor")
        column = lax.broadcasted_iota(jnp.int32, (H, HD), 1)
        for r in range(row_count):
            for pair in range(KVH // 2):
                pair_weights = weight_ref[r, pl.ds(pair * 2 * G, 2 * G), :]
                for n in (2 * pair, 2 * pair + 1):
                    both = jnp.dot(
                        pair_weights, value_ref[r, :, n * HD : (n + 1) * HD], preferred_element_type=F32
                    )
                    span_ref[pl.ds(n * G, G), pl.ds(r * HD, HD)] = both[(n % 2) * G : (n % 2 + 1) * G]
        stats = stats_ref[...]
        span_ref[:, pl.ds(width, HD)] = stats
        levels = jnp.zeros((H, HD), F32)
        for r in range(row_count):
            peak = jnp.max(jnp.abs(span_ref[:, pl.ds(r * HD, HD)]), axis=1, keepdims=True)
            levels = jnp.where(column == r, peak, levels)
        levels = level_of(levels)
        scale = TOP * jnp.exp(levels * (-LN2 / OCTAVE))
        for r in range(row_count):
            code[:, pl.ds(r * HD, HD)] = as_int16(span_ref[:, pl.ds(r * HD, HD)] * scale[:, r : r + 1])
        peaks = jnp.maximum(stats, -TOP)
        fine = jnp.where(column < row_count, peaks, stats * HD)
        whole = jnp.floor(fine)
        part = (fine - whole) * TOP
        coded = jnp.where(column < 2 * row_count, whole, 0.0)
        shifted = pltpu.roll(jnp.where(column < 2 * row_count, part, 0.0), 2 * row_count, 1)
        moved = pltpu.roll(jnp.where(column < row_count, levels, 0.0), 4 * row_count, 1)
        code[:, pl.ds(width, HD)] = as_int16(coded + shifted + moved)
        for k, step in enumerate(steps[1:]):
            start = pl.multiple_of((rank ^ step) * heads_here, heads_here)
            share_refs[k][...] = code[pl.ds(start, heads_here), :]

    return on_chip(
        kernel,
        [weights, stats, values, after],
        [VMEM] * 3 + [pl.BlockSpec(memory_space=pl.ANY)],
        [jax.ShapeDtypeStruct((H, width + HD), F32)]
        + [jax.ShapeDtypeStruct((heads_here, width + HD), I16)] * (len(steps) - 1),
        [pltpu.VMEM((H, width + HD), I16)],
        flops=2 * row_count * H * HD * local_len,
        moved=12 * values.size,
    )


def project_rows(kept, landed, weight, steps):
    slot_rows, depth = landed.shape
    width = weight.shape[1]
    rows_here = slot_rows // len(steps)
    share_width = width + HD
    step_width = 256

    def kernel(kept_ref, landed_ref, weight_ref, own_ref, *refs):
        share_refs, (held, code) = refs[:-2], refs[-2:]
        far = lax.axis_index("section") >= 2
        rank = lax.axis_index("tensor")
        rows = jnp.where(far, landed_ref[...], kept_ref[...])
        lane = lax.broadcasted_iota(jnp.int32, (slot_rows, HD), 1)
        levels = jnp.zeros((slot_rows, HD), F32)
        for c in range(0, width, step_width):
            product = jnp.dot(rows, weight_ref[:, pl.ds(c, step_width)], preferred_element_type=F32)
            held[:, c : c + step_width] = product
            for m in range(0, step_width, HD):
                tile = product[:, m : m + HD]
                level = level_of(jnp.max(jnp.abs(tile), axis=1, keepdims=True))
                levels = jnp.where(lane == LEVELS + (c + m) // HD, level, levels)
                scaled = tile * (TOP * jnp.exp(level * (-LN2 / OCTAVE)))
                code[:, c + m : c + m + HD] = as_int16(scaled)
        code[:, width:] = as_int16(levels)

        def rows_of(step):
            return pl.ds(pl.multiple_of((rank ^ step) * rows_here, rows_here), rows_here)

        own_ref[...] = held[rows_of(0), :]
        for k, step in enumerate(steps[1:]):
            levels_code = code[rows_of(step), pl.ds(width, HD)]
            share_refs[k][:, pl.ds(0, width)] = code[rows_of(step), pl.ds(0, width)]
            share_refs[k][:, pl.ds(width, HD)] = levels_code

    return on_chip(
        kernel,
        (kept, landed, weight),
        [VMEM] * 3,
        [jax.ShapeDtypeStruct((rows_here, width), F32)]
        + [jax.ShapeDtypeStruct((rows_here, share_width), I16)] * (len(steps) - 1),
        [pltpu.VMEM((slot_rows, width), F32), pltpu.VMEM((slot_rows, width + HD), I16)],
        flops=2 * slot_rows * depth * width,
        moved=2 * weight.size,
    )


def hand_on(piece, ahead):
    count = len(ahead)

    def kernel(piece_ref, *refs):
        refs[count][...] = piece_ref[...]

    return on_chip(
        kernel,
        (piece, *ahead),
        [VMEM] + [pl.BlockSpec(memory_space=pl.ANY)] * count,
        [jax.ShapeDtypeStruct(piece.shape, piece.dtype)],
    )[0]


def add_shares(total, shares):
    rows, width = total.shape
    count = len(shares)

    def kernel(total_ref, *refs):
        share_refs, out_ref = refs[:count], refs[count]
        scales = [
            jnp.exp(as_float(ref[:, pl.ds(ref.shape[1] - HD, HD)]) * (LN2 / OCTAVE)) * (1.0 / TOP)
            for ref in share_refs
        ]
        for n in range(width // HD):
            columns = pl.ds(n * HD, HD)
            part = total_ref[:, columns]
            for ref, scale in zip(share_refs, scales):
                part = part + as_float(ref[:, columns]) * scale[:, LEVELS + n : LEVELS + n + 1]
            out_ref[:, columns] = part

    return on_chip(
        kernel, (total, *shares), [VMEM] * (count + 1), [jax.ShapeDtypeStruct((rows, width), F32)]
    )[0]


def finish_rows(own, shares, cosine, sine):
    rows, width = own.shape
    share_count = len(shares)

    def kernel(own_ref, *refs):
        share_refs = refs[:share_count]
        cosine_ref, sine_ref, out_ref = refs[share_count:]
        scales = [
            jnp.exp(as_float(ref[:, pl.ds(ref.shape[1] - HD, HD)]) * (LN2 / OCTAVE)) * (1.0 / TOP)
            for ref in share_refs
        ]
        for n in range(width // HD):
            columns = pl.ds(n * HD, HD)
            total = own_ref[:, columns]
            for ref, scale in zip(share_refs, scales):
                total = total + as_float(ref[:, columns]) * scale[:, LEVELS + n : LEVELS + n + 1]
            if n < KVH:
                mean = jnp.sum(total * total, axis=1, keepdims=True) * (1.0 / HD)
                total = total * cosine_ref[...] + pltpu.roll(total, HD // 2, 1) * sine_ref[...]
                total = total * lax.rsqrt(mean + NORM_EPSILON)
            out_ref[:, columns] = total.astype(BF16)

    return on_chip(
        kernel,
        (own, *shares, cosine, sine),
        [VMEM] * (share_count + 3),
        [jax.ShapeDtypeStruct((rows, width), BF16)],
    )[0]


def merge_spans(span, shares, queries, new_keys, new_values):
    row_count = new_keys.shape[0]
    share_count = len(shares)
    heads_here = shares[0].shape[0]
    keys_here = heads_here // G
    width = row_count * HD

    def kernel(span_ref, *refs):
        share_refs = refs[:share_count]
        query_ref, key_ref, value_ref, out_ref = refs[share_count:]
        rank = lax.axis_index("tensor")
        heads = pl.ds(pl.multiple_of(rank * heads_here, heads_here), heads_here)
        columns = pl.ds(pl.multiple_of(rank * keys_here * HD, HD), keys_here * HD)
        new_key, new_value = key_ref[:, columns].astype(F32), value_ref[:, columns].astype(F32)

        def spread(tile, r):
            return jnp.concatenate(
                [
                    jnp.broadcast_to(tile[r : r + 1, kk * HD : (kk + 1) * HD], (G, HD))
                    for kk in range(keys_here)
                ],
                axis=0,
            )

        stats, scales = [span_ref[heads, pl.ds(width, HD)]], []
        for ref in share_refs:
            code = as_float(ref[:, pl.ds(width, HD)])
            column = lax.broadcasted_iota(jnp.int32, code.shape, 1)
            fine = code + pltpu.roll(code, HD - 2 * row_count, 1) * (1.0 / TOP)
            stats.append(jnp.where(column < row_count, fine, fine * (1.0 / HD)))
            scales.append(jnp.exp(code * (LN2 / OCTAVE)) * (1.0 / TOP))

        def part(k, r):
            if k == 0:
                return span_ref[heads, pl.ds(r * HD, HD)]
            coded = as_float(share_refs[k - 1][:, pl.ds(r * HD, HD)])
            return coded * scales[k - 1][:, 4 * row_count + r : 4 * row_count + r + 1]

        for r in range(row_count):
            query = query_ref[pl.ds(pl.multiple_of(r * H + rank * heads_here, heads_here), heads_here), :]
            self_score = jnp.sum(query * spread(new_key, r), axis=1, keepdims=True) * HD ** (-0.5)
            row_peak = self_score
            for tile in stats:
                row_peak = jnp.maximum(row_peak, tile[:, r : r + 1])
            self_weight = jnp.exp(self_score - row_peak)
            numerator = self_weight * spread(new_value, r)
            denominator = self_weight
            for k, tile in enumerate(stats):
                factor = jnp.exp(tile[:, r : r + 1] - row_peak)
                numerator += factor * part(k, r)
                denominator += factor * tile[:, row_count + r : row_count + r + 1]
            out_ref[r] = (numerator / denominator).astype(BF16)

    attended = on_chip(
        kernel,
        (span, *shares, queries, new_keys, new_values),
        [VMEM] * (share_count + 4),
        [jax.ShapeDtypeStruct((row_count, heads_here, HD), BF16)],
    )[0]
    return attended.reshape(row_count, heads_here * HD)


def join_rows(pieces, steps):
    count = len(pieces)
    rows, width = pieces[0].shape

    def kernel(*refs):
        piece_refs, out_hbm, sems = refs[:count], refs[count], refs[count + 1]
        rank = lax.axis_index("tensor")
        copies = []
        for step in range(count):
            place = pl.ds(pl.multiple_of(lax.rem(rank + count - steps[step], count) * rows, rows), rows)
            copies.append(pltpu.make_async_copy(piece_refs[step], out_hbm.at[place], sems.at[step]))
        for copy in copies:
            copy.start()
        for copy in copies:
            copy.wait()

    return on_chip(
        kernel,
        pieces,
        [VMEM] * count,
        [jax.ShapeDtypeStruct((count * rows, width), BF16)],
        [pltpu.SemaphoreType.DMA((count,))],
        out_specs=[HBM],
    )[0]


def swap(piece, axis, step):
    return lax.ppermute(piece, axis, [(i, i ^ step) for i in range(lax.axis_size(axis))])


def turn(piece, axis, step):
    count = lax.axis_size(axis)
    return lax.ppermute(piece, axis, [(i, (i + step) % count) for i in range(count)])


def local(
    prompt,
    key_value_weight,
    key_gain,
    prompt_blocks,
    block_owner,
    block_slot,
    queries,
    cache_keys,
    cache_values,
    new_keys,
    new_values,
    decode_lengths,
):
    tensor_count = lax.axis_size("tensor")
    near_states = swap(prompt[0], "section", 1)
    cosine, sine, states, table, weights, stats, row_queries, values = prepare(
        prompt[0], key_gain, block_owner, block_slot, prompt_blocks, queries, cache_keys, cache_values, decode_lengths
    )
    kept, sent = place_rows(states, near_states, table)
    landed = swap(sent, "section", 3)
    steps = (0, 3, 2, 1)
    span, *span_codes = span_sums(weights, stats, values, kept, steps)
    span_shares = [swap(code, "tensor", step) for code, step in zip(span_codes, steps[1:])]
    own, far, near, mid = project_rows(kept, landed, key_value_weight, (0, 3, 1, 2))
    far, near = swap(far, "tensor", 3), swap(near, "tensor", 1)
    mid = swap(hand_on(mid, span_shares), "tensor", 2)
    finished = finish_rows(add_shares(own, [far, near]), [mid], cosine, sine)
    pieces = [finished] + [turn(finished, "tensor", step) for step in steps[1:]]
    block_pool = join_rows(pieces, steps)
    attended = merge_spans(span, span_shares, row_queries, new_keys, new_values)
    return (attended, block_pool.reshape(1, CAP, BLK, -1))


def solution(mesh):
    in_specs = (
        P(("parts", "section"), None, "tensor"),
        P("tensor", None),
        P(),
        P("parts"),
        P("parts"),
        P("parts"),
        P(("parts", "section"), None),
        P(("parts", "section"), "tensor", None),
        P(("parts", "section"), "tensor", None),
        P(("parts", "section"), None),
        P(("parts", "section"), None),
        P(("parts", "section")),
    )
    out_specs = (P(("parts", "section"), "tensor"), P(("parts", "section"), None, None, None))
    tensor_count = mesh.shape["tensor"]
    whole_tiles = tensor_count == 4 and mesh.shape["section"] == 4
    program = local if whole_tiles else local_small_shares
    return jax.shard_map(program, mesh=mesh, in_specs=in_specs, out_specs=out_specs, check_vma=False)
```

```python
import math

import jax
import jax.numpy as jnp
from jax import lax
from jax.experimental import pallas as pl
from jax.experimental.pallas import tpu as pltpu
from jax.sharding import PartitionSpec as P

H = 64
KVH = 8
HD = 128
BLK = 16
SPAN = 128
KVW = 1024
G = 8
NB = 16
CAP = 4


NORM_EPSILON = 1e-06
ROPE_BASE = 1000000.0
MASKED_SCORE = -1e30


def exchange(pieces, axis):
    count = lax.axis_size(axis)
    rank = lax.axis_index(axis)
    landed = [lax.dynamic_index_in_dim(pieces, rank, 0, keepdims=False)]
    for step in range(1, count):
        piece = lax.dynamic_index_in_dim(pieces, rank ^ step, 0, keepdims=False)
        landed.append(lax.ppermute(piece, axis, [(i, i ^ step) for i in range(count)]))
    return landed


def collected(own, axis):
    count = lax.axis_size(axis)
    rank = lax.axis_index(axis)
    landed = [own]
    for step in range(1, count):
        landed.append(lax.ppermute(own, axis, [(i, i ^ step) for i in range(count)]))
    stacked = jnp.zeros((count,) + own.shape, own.dtype)
    for step, piece in enumerate(landed):
        stacked = lax.dynamic_update_index_in_dim(stacked, piece, rank ^ step, 0)
    return stacked


def rows_for_groups(states, block_owner, block_slot, group_count):
    slot_ids = jnp.arange(group_count * CAP, dtype=jnp.int32)
    selector = (block_owner * CAP + block_slot)[None, :] == slot_ids[:, None]
    filled = jnp.any(selector, axis=1)
    source = jnp.argmax(selector, axis=1)
    blocks = states.reshape(NB, BLK, states.shape[1])
    chosen = jnp.where(filled[:, None, None], blocks[source], jnp.zeros((), states.dtype))
    return chosen.reshape(group_count, CAP * BLK, states.shape[1])


def spread(rows, axis):
    count = lax.axis_size(axis)
    landed = jnp.where(lax.axis_index(axis) == 0, rows[0], jnp.zeros_like(rows[0]))
    for k in range(1, count):
        landed = landed + lax.ppermute(rows[k], axis, [(0, k)])
    return landed


def slot_positions(prompt_blocks, block_owner, block_slot, group_index):
    prompt_ends = jnp.cumsum(prompt_blocks)
    prompt_starts = prompt_ends - prompt_blocks
    slot_ids = jnp.arange(CAP, dtype=jnp.int32)
    selector = (block_owner[None, :] == group_index) & (block_slot[None, :] == slot_ids[:, None])
    block = jnp.sum(jnp.where(selector, jnp.arange(NB, dtype=jnp.int32)[None, :], 0), axis=1)
    inside = (block[:, None] >= prompt_starts[None, :]) & (block[:, None] < prompt_ends[None, :])
    first = jnp.sum(jnp.where(inside, prompt_starts[None, :], 0), axis=1)
    return (((block - first) * BLK)[:, None] + jnp.arange(BLK, dtype=jnp.int32)[None, :]).reshape(-1)


def finish_keys(projected, positions, key_gain):
    token_count = projected.shape[0]
    key_heads = projected[:, :KVW].reshape(token_count, KVH, HD)
    inv_root = lax.rsqrt(jnp.mean(key_heads * key_heads, axis=-1, keepdims=True) + NORM_EPSILON)
    key_heads = key_heads * inv_root * key_gain
    half_dim = HD // 2
    frequency = ROPE_BASE ** (jnp.arange(half_dim, dtype=jnp.float32) * (-2.0 / HD))
    angles = positions.astype(jnp.float32)[:, None, None] * frequency[None, None, :]
    cosine = jnp.cos(angles)
    sine_part = jnp.sin(angles)
    lower_half = key_heads[..., :half_dim]
    upper_half = key_heads[..., half_dim:]
    rotated = jnp.concatenate(
        [
            lower_half * cosine - upper_half * sine_part,
            upper_half * cosine + lower_half * sine_part,
        ],
        axis=-1,
    )
    return jnp.concatenate([rotated.reshape(token_count, KVW), projected[:, KVW:]], axis=1).astype(
        jnp.bfloat16
    )


def partial_attention(queries, cache_keys, cache_values, decode_lengths, first_position):
    row_count = queries.shape[0]
    local_len = cache_keys.shape[1]
    span_count = local_len // SPAN
    query_heads = queries.reshape(row_count, KVH, G, HD)
    key_heads = cache_keys.reshape(row_count, local_len, KVH, HD)
    scores = jnp.einsum(
        "rkgd,rpkd->rkgp", query_heads, key_heads, preferred_element_type=jnp.float32
    ) * HD ** (-0.5)
    live_mask = (first_position + jnp.arange(local_len, dtype=jnp.int32))[None, :] < decode_lengths[
        :, None
    ]
    scores = jnp.where(live_mask[:, None, None, :], scores, MASKED_SCORE)
    spans = scores.reshape(row_count, KVH, G, span_count, SPAN)
    span_max = jnp.max(spans, axis=-1)
    live_spans = live_mask.reshape(row_count, 1, 1, span_count, SPAN)
    weights = jnp.where(live_spans, jnp.exp(spans - span_max[..., None]), 0.0)
    span_sum = jnp.sum(weights, axis=-1)
    value_spans = cache_values.reshape(row_count, span_count, SPAN, KVH, HD)
    span_out = jnp.einsum(
        "rkgns,rnskd->rkgnd",
        weights.astype(jnp.bfloat16),
        value_spans,
        preferred_element_type=jnp.float32,
    )
    row_peak = jnp.max(span_max, axis=-1)
    factor = jnp.exp(span_max - row_peak[..., None])
    partial_out = jnp.sum(span_out * factor[..., None], axis=3)
    partial_sum = jnp.sum(span_sum * factor, axis=-1)
    return (
        partial_out.reshape(row_count, H, HD),
        row_peak.reshape(row_count, H),
        partial_sum.reshape(row_count, H),
    )


def combine_partials(former, latter):
    former_out, former_peak, former_sum = former
    latter_out, latter_peak, latter_sum = latter
    highest = jnp.maximum(former_peak, latter_peak)
    former_factor = jnp.exp(former_peak - highest)
    latter_factor = jnp.exp(latter_peak - highest)
    merged_out = former_out * former_factor[..., None] + latter_out * latter_factor[..., None]
    return (merged_out, highest, former_sum * former_factor + latter_sum * latter_factor)


def finish_heads(
    own_out, own_peak, own_sum, queries, new_keys, new_values, tensor_rank, heads_here
):
    row_count = queries.shape[0]
    own_width = heads_here * HD
    own_queries = (
        lax.dynamic_slice_in_dim(queries, tensor_rank * own_width, own_width, 1)
        .reshape(row_count, heads_here, HD)
        .astype(jnp.float32)
    )
    head_ids = tensor_rank * heads_here + jnp.arange(heads_here, dtype=jnp.int32)
    selector = (head_ids[:, None] // G == jnp.arange(KVH, dtype=jnp.int32)[None, :]).astype(
        jnp.float32
    )
    own_keys = jnp.einsum(
        "jk,rkd->rjd",
        selector,
        new_keys.reshape(row_count, KVH, HD).astype(jnp.float32),
        precision=lax.Precision.HIGHEST,
    )
    own_values = jnp.einsum(
        "jk,rkd->rjd",
        selector,
        new_values.reshape(row_count, KVH, HD).astype(jnp.float32),
        precision=lax.Precision.HIGHEST,
    )
    self_score = jnp.sum(own_queries * own_keys, axis=-1) * HD ** (-0.5)
    row_peak = jnp.maximum(own_peak, self_score)
    factor = jnp.exp(own_peak - row_peak)
    self_weight = jnp.exp(self_score - row_peak)
    numerator = own_out * factor[..., None] + self_weight[..., None] * own_values
    denominator = own_sum * factor + self_weight
    return (numerator / denominator[..., None]).reshape(row_count, own_width).astype(jnp.bfloat16)


def local_small_shares(
    prompt,
    key_value_weight,
    key_gain,
    prompt_blocks,
    block_owner,
    block_slot,
    queries,
    cache_keys,
    cache_values,
    new_keys,
    new_values,
    decode_lengths,
):
    tensor_count = lax.axis_size("tensor")
    tensor_rank = lax.axis_index("tensor")
    group_index = lax.axis_index("section")
    group_count = lax.axis_size("section")
    slot_rows = CAP * BLK
    rows_here = slot_rows // tensor_count
    rows = rows_for_groups(prompt[0], block_owner, block_slot, group_count)
    own_rows = spread(rows, "section")
    local_len = cache_keys.shape[1]
    row_count = queries.shape[0]
    heads_here = H // tensor_count
    partial_out, partial_peak, partial_sum = partial_attention(
        queries, cache_keys, cache_values, decode_lengths, tensor_rank * local_len
    )
    stats = jnp.stack([partial_peak, partial_sum], axis=-1).reshape(row_count, tensor_count, heads_here, 2)
    outs = partial_out.reshape(row_count, tensor_count, heads_here, HD)
    packed = jnp.concatenate([outs, jnp.pad(stats, ((0, 0), (0, 0), (0, 0), (0, HD - 2)))], axis=-1)
    shares = exchange(packed.transpose(1, 0, 2, 3), "tensor")
    merged = (shares[0][..., :HD], shares[0][..., HD], shares[0][..., HD + 1])
    for share in shares[1:]:
        merged = combine_partials(merged, (share[..., :HD], share[..., HD], share[..., HD + 1]))
    own_out, own_peak, own_sum = merged
    partial_terms = jnp.dot(own_rows, key_value_weight, preferred_element_type=jnp.float32)
    terms = exchange(partial_terms.reshape(tensor_count, rows_here, -1), "tensor")
    summed = sum(terms[1:], terms[0])
    positions = lax.dynamic_slice_in_dim(
        slot_positions(prompt_blocks, block_owner, block_slot, group_index), tensor_rank * rows_here, rows_here, 0
    )
    prompt_kv = finish_keys(summed, positions, key_gain)
    block_pool = collected(prompt_kv, "tensor").reshape(1, CAP, BLK, -1)
    attended = finish_heads(
        own_out, own_peak, own_sum, queries, new_keys, new_values, tensor_rank, heads_here
    )
    return (attended, block_pool)


VMEM = pl.BlockSpec(memory_space=pltpu.VMEM)
HBM = pl.BlockSpec(memory_space=pltpu.HBM)
F32 = jnp.float32
BF16 = jnp.bfloat16
I16 = jnp.int16
TOP = 32000.0
OCTAVE = 256.0
LN2 = math.log(2.0)
TINY = 1e-30
LEVELS = 64


def on_chip(kernel, operands, in_specs, out_shapes, scratch=(), out_specs=None, flops=0, moved=0):
    return pl.pallas_call(
        kernel,
        out_shape=out_shapes,
        in_specs=in_specs,
        out_specs=out_specs or [VMEM] * len(out_shapes),
        scratch_shapes=list(scratch),
        compiler_params=pltpu.CompilerParams(vmem_limit_bytes=40 * 1024 * 1024),
        cost_estimate=pl.CostEstimate(flops=flops, bytes_accessed=moved, transcendentals=0),
    )(*operands)


def stays(array):
    return pltpu.with_memory_space_constraint(array, pltpu.HBM)


def level_of(peak):
    return jnp.ceil(jnp.log(jnp.maximum(peak, TINY)) * (OCTAVE / LN2))


def as_int16(value):
    return jnp.round(value).astype(jnp.int32).astype(I16)


def as_float(value):
    return value.astype(jnp.int32).astype(F32)


def prepare(
    states, key_gain, block_owner, block_slot, prompt_blocks, queries, cache_keys, cache_values, decode_lengths
):
    token_count = states.shape[0]
    rows_here = CAP * BLK // lax.axis_size("tensor")
    slots_here = rows_here // BLK
    prompt_count = prompt_blocks.shape[0]
    row_count, local_len = cache_keys.shape[0], cache_keys.shape[1]
    fetched = [block_owner, block_slot, prompt_blocks, decode_lengths, key_gain[None, :], queries, cache_keys]
    count = len(fetched)

    def kernel(*refs):
        sources, states_hbm, value_hbm = refs[:count], refs[count], refs[count + 1]
        outs, rest = refs[count + 2 : count + 10], refs[count + 10 :]
        cosine_ref, sine_ref, states_ref, table_ref, weight_ref, stats_ref, query_ref, value_ref = outs
        held, (source, sems) = rest[:count], rest[count:]
        owner, slot, prompts, length, gain, packed, keys = held
        pairs = [*zip(sources, held), (states_hbm, states_ref), (value_hbm, value_ref)]
        copies = [pltpu.make_async_copy(s, d, sems.at[i]) for i, (s, d) in enumerate(pairs)]
        for copy in copies:
            copy.start()
        group = lax.axis_index("section")
        rank = lax.axis_index("tensor")
        core = lax.rem(group, 2)
        for copy in copies[:6]:
            copy.wait()

        for j in range(2 * CAP):
            source[j] = -1
        for b in range(NB):

            @pl.when(owner[b] == core)
            def _():
                source[slot[b]] = b

            @pl.when(owner[b] == 3 - core)
            def _():
                source[CAP + slot[b]] = b

        token = lax.broadcasted_iota(jnp.int32, (BLK, token_count), 1)
        inner = lax.broadcasted_iota(jnp.int32, (BLK, token_count), 0)
        for j in range(2 * CAP):
            chosen = token == source[j] * BLK + inner
            table_ref[pl.ds(j * BLK, BLK), :] = jnp.where(chosen, 1.0, 0.0).astype(BF16)

        lane = lax.broadcasted_iota(jnp.int32, (BLK, HD), 1)
        row = lax.broadcasted_iota(jnp.int32, (BLK, HD), 0)
        half = lax.rem(lane, HD // 2).astype(F32)
        frequency = jnp.exp(half * (-2.0 / HD * math.log(ROPE_BASE)))
        far_gain = pltpu.roll(jnp.broadcast_to(gain[...], (8, HD)), HD // 2, 1)[0:1]
        for s in range(slots_here):
            block = 0
            for b in range(NB):
                block = jnp.where((owner[b] == group) & (slot[b] == rank * slots_here + s), b, block)
            first, begin = 0, 0
            for j in range(prompt_count):
                first = jnp.where(block >= begin, begin, first)
                begin = begin + prompts[j]
            angles = ((block - first) * BLK + row).astype(F32) * frequency
            cosine_ref[pl.ds(s * BLK, BLK), :] = jnp.cos(angles) * gain[...]
            sine = jnp.sin(angles) * far_gain
            sine_ref[pl.ds(s * BLK, BLK), :] = jnp.where(lane < HD // 2, -sine, sine)

        for h in range(H):
            piece = packed[:, pl.ds(h * HD, HD)].astype(F32)
            query_ref[pl.ds(h, row_count, stride=H), :] = piece
        copies[6].wait()
        place = lax.broadcasted_iota(jnp.int32, (H, local_len), 1) + rank * local_len
        column = lax.broadcasted_iota(jnp.int32, (H, HD), 1)
        stats = jnp.zeros((H, HD), F32)
        for r in range(row_count):
            parts = []
            for pair in range(KVH // 2):
                pair_queries = query_ref[pl.ds(r * H + pair * 2 * G, 2 * G), :].astype(BF16)
                for n in (2 * pair, 2 * pair + 1):
                    both = lax.dot_general(
                        pair_queries,
                        keys[r, :, n * HD : (n + 1) * HD],
                        (((1,), (1,)), ((), ())),
                        preferred_element_type=F32,
                    )
                    parts.append(both[(n % 2) * G : (n % 2 + 1) * G])
            live = place < length[r]
            row_scores = jnp.where(live, jnp.concatenate(parts, axis=0) * HD ** (-0.5), MASKED_SCORE)
            peak = jnp.max(row_scores, axis=1, keepdims=True)
            weight = jnp.where(live, jnp.exp(row_scores - peak), 0.0)
            total = jnp.sum(weight, axis=1, keepdims=True)
            weight_ref[r] = weight.astype(BF16)
            stats = jnp.where(column == r, peak, stats)
            stats = jnp.where(column == row_count + r, total, stats)
        stats_ref[...] = stats
        copies[count].wait()
        copies[count + 1].wait()

    return on_chip(
        kernel,
        [stays(array) for array in (*fetched, states, cache_values)],
        [HBM] * (count + 2),
        [
            jax.ShapeDtypeStruct((rows_here, HD), F32),
            jax.ShapeDtypeStruct((rows_here, HD), F32),
            jax.ShapeDtypeStruct(states.shape, BF16),
            jax.ShapeDtypeStruct((2 * CAP * BLK, token_count), BF16),
            jax.ShapeDtypeStruct((row_count, H, local_len), BF16),
            jax.ShapeDtypeStruct((H, HD), F32),
            jax.ShapeDtypeStruct((row_count * H, HD), F32),
            jax.ShapeDtypeStruct(cache_values.shape, BF16),
        ],
        [pltpu.SMEM(array.shape, jnp.int32) for array in fetched[:4]]
        + [pltpu.VMEM(array.shape, array.dtype) for array in fetched[4:]]
        + [
            pltpu.SMEM((2 * CAP,), jnp.int32),
            pltpu.SemaphoreType.DMA((count + 2,)),
        ],
        flops=2 * row_count * H * HD * local_len,
        moved=2 * (states.size + cache_keys.size + cache_values.size),
    )


def place_rows(own_states, near_states, table):
    width = own_states.shape[1]
    rows = CAP * BLK

    def kernel(own_ref, near_ref, table_ref, keep_ref, send_ref):
        core = lax.rem(lax.axis_index("section"), 2)

        def place(states):
            placed = jnp.dot(table_ref[...], states[...], preferred_element_type=F32).astype(BF16)
            keep_ref[...] = placed[:rows]
            send_ref[...] = placed[rows:]

        @pl.when(core == 0)
        def _():
            place(own_ref)

        @pl.when(core == 1)
        def _():
            place(near_ref)

    return on_chip(
        kernel,
        (own_states, near_states, table),
        [VMEM] * 3,
        [jax.ShapeDtypeStruct((rows, width), BF16)] * 2,
        moved=own_states.size * 2,
    )


def span_sums(weights, stats, values, after, steps):
    row_count, _, local_len = weights.shape
    width = row_count * HD
    heads_here = H // len(steps)

    def kernel(weight_ref, stats_ref, value_ref, after_ref, span_ref, *refs):
        share_refs, code = refs[:-1], refs[-1]
        rank = lax.axis_index("tensor")
        column = lax.broadcasted_iota(jnp.int32, (H, HD), 1)
        for r in range(row_count):
            for pair in range(KVH // 2):
                pair_weights = weight_ref[r, pl.ds(pair * 2 * G, 2 * G), :]
                for n in (2 * pair, 2 * pair + 1):
                    both = jnp.dot(
                        pair_weights, value_ref[r, :, n * HD : (n + 1) * HD], preferred_element_type=F32
                    )
                    span_ref[pl.ds(n * G, G), pl.ds(r * HD, HD)] = both[(n % 2) * G : (n % 2 + 1) * G]
        stats = stats_ref[...]
        span_ref[:, pl.ds(width, HD)] = stats
        levels = jnp.zeros((H, HD), F32)
        for r in range(row_count):
            peak = jnp.max(jnp.abs(span_ref[:, pl.ds(r * HD, HD)]), axis=1, keepdims=True)
            levels = jnp.where(column == r, peak, levels)
        levels = level_of(levels)
        scale = TOP * jnp.exp(levels * (-LN2 / OCTAVE))
        for r in range(row_count):
            code[:, pl.ds(r * HD, HD)] = as_int16(span_ref[:, pl.ds(r * HD, HD)] * scale[:, r : r + 1])
        peaks = jnp.maximum(stats, -TOP)
        fine = jnp.where(column < row_count, peaks, stats * HD)
        whole = jnp.floor(fine)
        part = (fine - whole) * TOP
        coded = jnp.where(column < 2 * row_count, whole, 0.0)
        shifted = pltpu.roll(jnp.where(column < 2 * row_count, part, 0.0), 2 * row_count, 1)
        moved = pltpu.roll(jnp.where(column < row_count, levels, 0.0), 4 * row_count, 1)
        code[:, pl.ds(width, HD)] = as_int16(coded + shifted + moved)
        for k, step in enumerate(steps[1:]):
            start = pl.multiple_of((rank ^ step) * heads_here, heads_here)
            share_refs[k][...] = code[pl.ds(start, heads_here), :]

    return on_chip(
        kernel,
        [weights, stats, values, after],
        [VMEM] * 3 + [pl.BlockSpec(memory_space=pl.ANY)],
        [jax.ShapeDtypeStruct((H, width + HD), F32)]
        + [jax.ShapeDtypeStruct((heads_here, width + HD), I16)] * (len(steps) - 1),
        [pltpu.VMEM((H, width + HD), I16)],
        flops=2 * row_count * H * HD * local_len,
        moved=12 * values.size,
    )


def project_rows(kept, landed, weight, steps):
    slot_rows, depth = landed.shape
    width = weight.shape[1]
    rows_here = slot_rows // len(steps)
    share_width = width + HD
    step_width = 256

    def kernel(kept_ref, landed_ref, weight_ref, own_ref, *refs):
        share_refs, (held, code) = refs[:-2], refs[-2:]
        far = lax.axis_index("section") >= 2
        rank = lax.axis_index("tensor")
        rows = jnp.where(far, landed_ref[...], kept_ref[...])
        lane = lax.broadcasted_iota(jnp.int32, (slot_rows, HD), 1)
        levels = jnp.zeros((slot_rows, HD), F32)
        for c in range(0, width, step_width):
            product = jnp.dot(rows, weight_ref[:, pl.ds(c, step_width)], preferred_element_type=F32)
            held[:, c : c + step_width] = product
            for m in range(0, step_width, HD):
                tile = product[:, m : m + HD]
                level = level_of(jnp.max(jnp.abs(tile), axis=1, keepdims=True))
                levels = jnp.where(lane == LEVELS + (c + m) // HD, level, levels)
                scaled = tile * (TOP * jnp.exp(level * (-LN2 / OCTAVE)))
                code[:, c + m : c + m + HD] = as_int16(scaled)
        code[:, width:] = as_int16(levels)

        def rows_of(step):
            return pl.ds(pl.multiple_of((rank ^ step) * rows_here, rows_here), rows_here)

        own_ref[...] = held[rows_of(0), :]
        for k, step in enumerate(steps[1:]):
            levels_code = code[rows_of(step), pl.ds(width, HD)]
            share_refs[k][:, pl.ds(0, width)] = code[rows_of(step), pl.ds(0, width)]
            share_refs[k][:, pl.ds(width, HD)] = levels_code

    return on_chip(
        kernel,
        (kept, landed, weight),
        [VMEM] * 3,
        [jax.ShapeDtypeStruct((rows_here, width), F32)]
        + [jax.ShapeDtypeStruct((rows_here, share_width), I16)] * (len(steps) - 1),
        [pltpu.VMEM((slot_rows, width), F32), pltpu.VMEM((slot_rows, width + HD), I16)],
        flops=2 * slot_rows * depth * width,
        moved=2 * weight.size,
    )


def hand_on(piece, ahead):
    count = len(ahead)

    def kernel(piece_ref, *refs):
        refs[count][...] = piece_ref[...]

    return on_chip(
        kernel,
        (piece, *ahead),
        [VMEM] + [pl.BlockSpec(memory_space=pl.ANY)] * count,
        [jax.ShapeDtypeStruct(piece.shape, piece.dtype)],
    )[0]


def add_shares(total, shares):
    rows, width = total.shape
    count = len(shares)

    def kernel(total_ref, *refs):
        share_refs, out_ref = refs[:count], refs[count]
        scales = [
            jnp.exp(as_float(ref[:, pl.ds(ref.shape[1] - HD, HD)]) * (LN2 / OCTAVE)) * (1.0 / TOP)
            for ref in share_refs
        ]
        for n in range(width // HD):
            columns = pl.ds(n * HD, HD)
            part = total_ref[:, columns]
            for ref, scale in zip(share_refs, scales):
                part = part + as_float(ref[:, columns]) * scale[:, LEVELS + n : LEVELS + n + 1]
            out_ref[:, columns] = part

    return on_chip(
        kernel, (total, *shares), [VMEM] * (count + 1), [jax.ShapeDtypeStruct((rows, width), F32)]
    )[0]


def finish_rows(own, shares, cosine, sine):
    rows, width = own.shape
    share_count = len(shares)

    def kernel(own_ref, *refs):
        share_refs = refs[:share_count]
        cosine_ref, sine_ref, out_ref = refs[share_count:]
        scales = [
            jnp.exp(as_float(ref[:, pl.ds(ref.shape[1] - HD, HD)]) * (LN2 / OCTAVE)) * (1.0 / TOP)
            for ref in share_refs
        ]
        for n in range(width // HD):
            columns = pl.ds(n * HD, HD)
            total = own_ref[:, columns]
            for ref, scale in zip(share_refs, scales):
                total = total + as_float(ref[:, columns]) * scale[:, LEVELS + n : LEVELS + n + 1]
            if n < KVH:
                mean = jnp.sum(total * total, axis=1, keepdims=True) * (1.0 / HD)
                total = total * cosine_ref[...] + pltpu.roll(total, HD // 2, 1) * sine_ref[...]
                total = total * lax.rsqrt(mean + NORM_EPSILON)
            out_ref[:, columns] = total.astype(BF16)

    return on_chip(
        kernel,
        (own, *shares, cosine, sine),
        [VMEM] * (share_count + 3),
        [jax.ShapeDtypeStruct((rows, width), BF16)],
    )[0]


def merge_spans(span, shares, queries, new_keys, new_values):
    row_count = new_keys.shape[0]
    share_count = len(shares)
    heads_here = shares[0].shape[0]
    keys_here = heads_here // G
    width = row_count * HD

    def kernel(span_ref, *refs):
        share_refs = refs[:share_count]
        query_ref, key_ref, value_ref, out_ref = refs[share_count:]
        rank = lax.axis_index("tensor")
        heads = pl.ds(pl.multiple_of(rank * heads_here, heads_here), heads_here)
        columns = pl.ds(pl.multiple_of(rank * keys_here * HD, HD), keys_here * HD)
        new_key, new_value = key_ref[:, columns].astype(F32), value_ref[:, columns].astype(F32)

        def spread(tile, r):
            return jnp.concatenate(
                [
                    jnp.broadcast_to(tile[r : r + 1, kk * HD : (kk + 1) * HD], (G, HD))
                    for kk in range(keys_here)
                ],
                axis=0,
            )

        stats, scales = [span_ref[heads, pl.ds(width, HD)]], []
        for ref in share_refs:
            code = as_float(ref[:, pl.ds(width, HD)])
            column = lax.broadcasted_iota(jnp.int32, code.shape, 1)
            fine = code + pltpu.roll(code, HD - 2 * row_count, 1) * (1.0 / TOP)
            stats.append(jnp.where(column < row_count, fine, fine * (1.0 / HD)))
            scales.append(jnp.exp(code * (LN2 / OCTAVE)) * (1.0 / TOP))

        def part(k, r):
            if k == 0:
                return span_ref[heads, pl.ds(r * HD, HD)]
            coded = as_float(share_refs[k - 1][:, pl.ds(r * HD, HD)])
            return coded * scales[k - 1][:, 4 * row_count + r : 4 * row_count + r + 1]

        for r in range(row_count):
            query = query_ref[pl.ds(pl.multiple_of(r * H + rank * heads_here, heads_here), heads_here), :]
            self_score = jnp.sum(query * spread(new_key, r), axis=1, keepdims=True) * HD ** (-0.5)
            row_peak = self_score
            for tile in stats:
                row_peak = jnp.maximum(row_peak, tile[:, r : r + 1])
            self_weight = jnp.exp(self_score - row_peak)
            numerator = self_weight * spread(new_value, r)
            denominator = self_weight
            for k, tile in enumerate(stats):
                factor = jnp.exp(tile[:, r : r + 1] - row_peak)
                numerator += factor * part(k, r)
                denominator += factor * tile[:, row_count + r : row_count + r + 1]
            out_ref[r] = (numerator / denominator).astype(BF16)

    attended = on_chip(
        kernel,
        (span, *shares, queries, new_keys, new_values),
        [VMEM] * (share_count + 4),
        [jax.ShapeDtypeStruct((row_count, heads_here, HD), BF16)],
    )[0]
    return attended.reshape(row_count, heads_here * HD)


def join_rows(pieces, steps):
    count = len(pieces)
    rows, width = pieces[0].shape

    def kernel(*refs):
        piece_refs, out_hbm, sems = refs[:count], refs[count], refs[count + 1]
        rank = lax.axis_index("tensor")
        copies = []
        for step in range(count):
            place = pl.ds(pl.multiple_of((rank ^ steps[step]) * rows, rows), rows)
            copies.append(pltpu.make_async_copy(piece_refs[step], out_hbm.at[place], sems.at[step]))
        for copy in copies:
            copy.start()
        for copy in copies:
            copy.wait()

    return on_chip(
        kernel,
        pieces,
        [VMEM] * count,
        [jax.ShapeDtypeStruct((count * rows, width), BF16)],
        [pltpu.SemaphoreType.DMA((count,))],
        out_specs=[HBM],
    )[0]


def swap(piece, axis, step):
    return lax.ppermute(piece, axis, [(i, i ^ step) for i in range(lax.axis_size(axis))])


def turn(piece, axis, step):
    count = lax.axis_size(axis)
    return lax.ppermute(piece, axis, [(i, (i + step) % count) for i in range(count)])


def local(
    prompt,
    key_value_weight,
    key_gain,
    prompt_blocks,
    block_owner,
    block_slot,
    queries,
    cache_keys,
    cache_values,
    new_keys,
    new_values,
    decode_lengths,
):
    tensor_count = lax.axis_size("tensor")
    near_states = swap(prompt[0], "section", 1)
    cosine, sine, states, table, weights, stats, row_queries, values = prepare(
        prompt[0], key_gain, block_owner, block_slot, prompt_blocks, queries, cache_keys, cache_values, decode_lengths
    )
    kept, sent = place_rows(states, near_states, table)
    landed = swap(sent, "section", 3)
    steps = (0, 3, 2, 1)
    span, *span_codes = span_sums(weights, stats, values, kept, steps)
    span_shares = [swap(code, "tensor", step) for code, step in zip(span_codes, steps[1:])]
    own, far, near, mid = project_rows(kept, landed, key_value_weight, (0, 3, 1, 2))
    far, near = swap(far, "tensor", 3), swap(near, "tensor", 1)
    mid = swap(hand_on(mid, span_shares), "tensor", 2)
    finished = finish_rows(add_shares(own, [far, near]), [mid], cosine, sine)
    steps = (0, 2, 1, 3)
    pieces = [finished] + [swap(finished, "tensor", step) for step in steps[1:]]
    block_pool = join_rows(pieces, steps)
    attended = merge_spans(span, span_shares, row_queries, new_keys, new_values)
    return (attended, block_pool.reshape(1, CAP, BLK, -1))


def solution(mesh):
    in_specs = (
        P(("parts", "section"), None, "tensor"),
        P("tensor", None),
        P(),
        P("parts"),
        P("parts"),
        P("parts"),
        P(("parts", "section"), None),
        P(("parts", "section"), "tensor", None),
        P(("parts", "section"), "tensor", None),
        P(("parts", "section"), None),
        P(("parts", "section"), None),
        P(("parts", "section")),
    )
    out_specs = (P(("parts", "section"), "tensor"), P(("parts", "section"), None, None, None))
    tensor_count = mesh.shape["tensor"]
    whole_tiles = tensor_count == 4 and mesh.shape["section"] == 4
    program = local if whole_tiles else local_small_shares
    return jax.shard_map(program, mesh=mesh, in_specs=in_specs, out_specs=out_specs, check_vma=False)
```
